32 devices in a mesh: groups: 2 (over x), vir: 16 (over z, y, core).
Axes of the slice: x: 2, y: 2, z: 4, core: 2. Of those that a mesh axis runs over, the one named last changes fastest.
Arguments:
- amplitudes: bfloat16 [256, 64, 384], P(('groups', 'vir')), parts along dimension 0, may hold values from -12 to 12
- ij_counts: int32 [16], P('groups'), parts along dimension 0, may hold values from 1 to 32, 128 in all
- integrals: bfloat16 [1024, 64, 384], P(('groups', 'vir')), parts along dimension 0, may hold values from -1 to 1
- ab_irrep: int32 [1024], P(('groups', 'vir')), parts along dimension 0, may hold values from 0 to 7, as said below
Outputs:
- residual: bfloat16 [1024, 64, 2048], P(('groups', 'vir')), parts along dimension 0
- norms: float32 [16], P('groups'), parts along dimension 0
The draws below stay inside these ranges and needn't reach their ends.
There are 2 independent parts, one for each index of `groups`. The reference program is written for one: setup_inputs(seed, part) draws one part's arguments, and reference() takes and returns one part's arrays. A program takes and returns all parts, laid end to end along the dimension named above; each array names one. Nothing has to cross between parts.
Inputs may be any that keep to these rules, and one draw needn't show every extreme that they name: `ij_counts`: every symmetry holds at least one occupied-pair tile and at most 32; some symmetry holds exactly 32. The counts sum to 128. `ab_irrep`: every symmetry holds at least one ab tile.
All inputs are finite; a program needn't handle non-finite values.
Results may differ from the reference program's by a relative error of at most 0.001.
Values may be sent and summed in bfloat16 or wider, within the bound.
No kernel may reach another device: no remote copies, remote signals or barrier semaphores. Data moves between devices by JAX's collectives and lax.ppermute only.
A program may use at most 128 MiB of HBM per device.

```python
import math
import jax
import jax.numpy as jnp
import numpy as np
from jax import lax

TILE = 64
SYMS = 8
CDW = 384
IJT = 128
IJCAP = 32
ABT = 512


def column_scales(key, spread):
    return jnp.exp(jax.random.uniform(key, (CDW,), jnp.float32, -spread, spread))


def normal_entries(key, shape):
    return jnp.clip(jax.random.normal(key, shape, jnp.float32), -4.0, 4.0)


def draw_amplitudes(key, part):
    scales = column_scales(key, 1.15)
    key = jax.random.fold_in(key, 11)
    entry_key = jax.random.fold_in(key, 0)
    entries = normal_entries(entry_key, (IJT, TILE, CDW))
    values = jnp.clip(entries * scales[None, None, :], -12.0, 12.0)
    return values.astype(jnp.bfloat16)


def draw_integrals(key, part):
    scales = column_scales(key, 1.15)
    key = jax.random.fold_in(key, 13)
    entries = normal_entries(key, (ABT, TILE, CDW))
    factor = jnp.float32(0.3) / jnp.sqrt(jnp.float32(CDW))
    values = jnp.clip(entries * scales[None, None, :] * factor, -1.0, 1.0)
    return values.astype(jnp.bfloat16)


def draw_ab_irrep(key, part):
    key = jax.random.fold_in(key, 7)
    weighted = jnp.asarray(np.repeat(np.arange(SYMS), np.arange(1, SYMS + 1)), dtype=jnp.int32)
    first_key, second_key = jax.random.split(key)
    picks = jax.random.randint(first_key, (ABT - SYMS,), 0, weighted.shape[0])
    rest = weighted[picks]
    listing = jnp.concatenate([jnp.arange(SYMS, dtype=jnp.int32), rest]).astype(jnp.int32)
    return jax.random.permutation(second_key, listing).astype(jnp.int32)


def split_up(count, total, reach, lean):
    loads = [(1 << 20) // math.isqrt(rank ** lean) + 1 for rank in range(2, count + 1)]
    surplus, counts = total - reach - (count - 1), [1] * (count - 1)
    while surplus > 0:
        candidates = [i for i in range(count - 1) if counts[i] < reach]
        pool, left = sum([loads[i] for i in candidates]), surplus
        for i in candidates:
            more = min(reach - counts[i], max(1, left * loads[i] // pool), surplus)
            counts[i] = counts[i] + more
            surplus = surplus - more
    return np.array([reach] + counts)


def ragged_sizes(rng, count, total, bound, skew):
    if count == 2:
        one = jax.random.randint(rng, (), max(1, total - bound), min(bound, total - 1) + 1)
        return jnp.stack([one, total - one])
    sizes = jnp.asarray(split_up(count, total, bound, skew), jnp.int32)
    pairs = (count - 1) // 2
    source_of, taker = sizes[1:1 + 2 * pairs:2], sizes[2:2 + 2 * pairs:2]
    room = jnp.minimum(source_of - 1, bound - taker)
    passed = jax.random.randint(jax.random.fold_in(rng, 1), (pairs,), 0, 1 << 20) % (room + 1)
    sizes = sizes.at[1:1 + 2 * pairs:2].set(source_of - passed).at[2:2 + 2 * pairs:2].set(taker + passed)
    return sizes[jax.random.permutation(jax.random.fold_in(rng, 2), count)]


def setup_inputs(seed: int = 0, part: int = 0) -> dict:
    key_of = jax.random.split(jax.random.key(seed), 5)
    own_keys = jax.random.split(jax.random.fold_in(key_of[4], part), 5)
    amplitudes = draw_amplitudes(jax.random.fold_in(jax.random.fold_in(key_of[4], part), 71), part)
    ij_counts = ragged_sizes(own_keys[1], SYMS, IJT, IJCAP, 2).astype(jnp.int32)
    integrals = draw_integrals(jax.random.fold_in(jax.random.fold_in(key_of[4], part), 71), part)
    ab_irrep = draw_ab_irrep(jax.random.fold_in(jax.random.fold_in(key_of[4], part), 71), part)
    return {"amplitudes": amplitudes, "ij_counts": ij_counts, "integrals": integrals, "ab_irrep": ab_irrep}


def reference(amplitudes, ij_counts, integrals, ab_irrep):
    offsets = (jnp.cumsum(ij_counts) - ij_counts).astype(jnp.int32)
    position = jnp.arange(IJCAP, dtype=jnp.int32)
    source = offsets[:, None] + position[None, :]
    valid = position[None, :] < ij_counts[:, None]
    source = jnp.clip(source, 0, IJT - 1).astype(jnp.int32)
    picked = amplitudes[source.reshape(-1)]
    picked = jnp.where(valid.reshape(-1)[:, None, None], picked, jnp.zeros_like(picked))
    stacks = picked.reshape(SYMS, IJCAP * TILE, CDW)

    def one_group(group):
        tile_block, irrep_group = group
        chosen = stacks[irrep_group]
        products = jnp.einsum('tcd,tqd->tcq', tile_block.astype(jnp.float32), chosen.astype(jnp.float32))
        return (products.astype(jnp.bfloat16), lax.optimization_barrier(jnp.sum(products * products, axis=(1, 2))))
    residual, squares = lax.map(one_group, (integrals.reshape(ABT // 8, 8, TILE, CDW), ab_irrep.reshape(ABT // 8, 8)))
    match = ab_irrep[:, None] == jnp.arange(SYMS, dtype=jnp.int32)[None, :]
    irrep_sums = lax.optimization_barrier(jnp.sum(jnp.where(match, squares.reshape(-1)[:, None], jnp.float32(0.0)), axis=0))
    ab_counts = lax.optimization_barrier(jnp.sum(match.astype(jnp.float32), axis=0))
    entries = ab_counts * ij_counts.astype(jnp.float32) * float(TILE * TILE)
    norms = jnp.sqrt(irrep_sums / entries + 1e-06)
    return (residual.reshape(ABT, TILE, IJCAP * TILE), norms)
```

```python
import functools

import jax
import jax.numpy as jnp
from jax import lax
from jax.experimental import pallas as pl
from jax.experimental.pallas import tpu as pltpu
from jax.sharding import PartitionSpec as P

BATCH = 4
VMEM_BYTES = 56 * 1024 * 1024


def ladder_kernel(
    capacity, shard_tiles, n_sources,
    counts_ref, irrep_ref, dest_ref, v_hbm, *refs,
):
    sources = refs[:n_sources]
    res_hbm, stats_ref = refs[n_sources:n_sources + 2]
    a_buf, v_buf, o_buf, acc_ref, size_ref, first_ref, next_ref, offset_ref, order_ref = (
        refs[n_sources + 2:n_sources + 11]
    )
    a_sem, v_sem, o_sem = refs[n_sources + 11:]
    own_tiles, rows, width = v_hbm.shape
    irreps = counts_ref.shape[0]
    all_tiles = sum(source.shape[0] for source in sources)

    piece = 0
    for source in sources:
        for start in range(0, source.shape[0], shard_tiles):
            pltpu.make_async_copy(
                source.at[pl.ds(start, shard_tiles)],
                a_buf.at[pl.ds(dest_ref[piece], shard_tiles)],
                a_sem,
            ).start()
            piece += 1

    for s in range(irreps):
        size_ref[s] = 0

    def count(l, carry):
        s = irrep_ref[l]
        size_ref[s] = size_ref[s] + 1
        return carry

    lax.fori_loop(0, own_tiles, count, 0)
    first, offset = jnp.int32(0), jnp.int32(0)
    for s in range(irreps):
        first_ref[s] = first
        next_ref[s] = first
        offset_ref[s] = offset
        first = first + size_ref[s]
        offset = offset + counts_ref[s]

    def place(l, carry):
        s = irrep_ref[l]
        slot = next_ref[s]
        next_ref[s] = slot + 1
        order_ref[slot] = l
        pltpu.make_async_copy(v_hbm.at[l], v_buf.at[slot], v_sem).start()
        return carry

    lax.fori_loop(0, own_tiles, place, 0)
    pltpu.make_async_copy(v_hbm, v_buf.at[pl.ds(0, own_tiles)], v_sem).wait()
    whole = a_buf.at[pl.ds(0, all_tiles)]
    pltpu.make_async_copy(whole, whole, a_sem).wait()

    side = BATCH * rows
    row_at = lax.broadcasted_iota(jnp.int32, (side, side), 0)
    col_at = lax.broadcasted_iota(jnp.int32, (side, side), 1)

    def symmetry(s, carry):
        size, slot0 = size_ref[s], first_ref[s]
        tiles, offset = counts_ref[s], offset_ref[s]
        blocks = (tiles + BATCH - 1) // BATCH

        def member_batch(i, total):
            slot = slot0 + i * BATCH
            rows_left = (size - i * BATCH) * rows

            def column_block(j, total):
                left = v_buf[pl.ds(slot, BATCH)].reshape(side, width)
                right = a_buf[pl.ds(offset + j * BATCH, BATCH)].reshape(side, width)
                product = lax.dot_general(
                    left, right, (((1,), (1,)), ((), ())),
                    preferred_element_type=jnp.float32,
                )
                keep = (row_at < rows_left) & (col_at < (tiles - j * BATCH) * rows)
                product = jnp.where(keep, product, 0.0)
                o_buf[pl.ds(slot, BATCH), :, pl.ds(pl.multiple_of(j * side, side), side)] = (
                    product.astype(jnp.bfloat16).reshape(BATCH, rows, side)
                )
                squares = (product * product).reshape(side // 8, 8, side)
                return total + jnp.sum(squares, axis=0)

            def blank_block(j, inner):
                o_buf[pl.ds(slot, BATCH), :, pl.ds(pl.multiple_of(j * side, side), side)] = (
                    jnp.zeros((BATCH, rows, side), jnp.bfloat16)
                )
                return inner

            total = lax.fori_loop(0, blocks, column_block, total)
            lax.fori_loop(blocks, capacity // BATCH, blank_block, 0)
            for t in range(BATCH):
                @pl.when(i * BATCH + t < size)
                def _():
                    pltpu.make_async_copy(
                        o_buf.at[slot + t], res_hbm.at[order_ref[slot + t]], o_sem
                    ).start()
            return total

        acc_ref[s] = lax.fori_loop(
            0, (size + BATCH - 1) // BATCH, member_batch, jnp.zeros((8, side), jnp.float32)
        )
        return carry

    lax.fori_loop(0, irreps, symmetry, 0)
    sums = jnp.sum(acc_ref[...], axis=1)
    sums = sum(sums[:, k:k + 128] for k in range(0, side, 128))
    stats_ref[0] = sums
    at_row = lax.broadcasted_iota(jnp.int32, sums.shape, 0)
    at_lane = lax.broadcasted_iota(jnp.int32, sums.shape, 1)
    sizes = jnp.zeros(sums.shape, jnp.int32)
    for s in range(irreps):
        sizes = jnp.where((at_row == s) & (at_lane == 0), size_ref[s], sizes)
    stats_ref[1] = sizes.astype(jnp.float32)
    pltpu.make_async_copy(o_buf.at[pl.ds(0, own_tiles)], res_hbm, o_sem).wait()


def ladder(counts, irrep, dest, integrals, sources, shard_tiles, capacity):
    own_tiles, rows, width = integrals.shape
    irreps = counts.shape[0]
    all_tiles = sum(source.shape[0] for source in sources)
    smem = pl.BlockSpec(memory_space=pltpu.SMEM)
    anywhere = pl.BlockSpec(memory_space=pl.ANY)
    return pl.pallas_call(
        functools.partial(ladder_kernel, capacity, shard_tiles, len(sources)),
        out_shape=(
            jax.ShapeDtypeStruct((own_tiles, rows, capacity * rows), jnp.bfloat16),
            jax.ShapeDtypeStruct((2, irreps, 128), jnp.float32),
        ),
        in_specs=[smem, smem, smem] + [anywhere] * (1 + len(sources)),
        out_specs=(anywhere, pl.BlockSpec(memory_space=pltpu.VMEM)),
        scratch_shapes=[
            pltpu.VMEM((all_tiles + BATCH, rows, width), jnp.bfloat16),
            pltpu.VMEM((own_tiles + BATCH, rows, width), jnp.bfloat16),
            pltpu.VMEM((own_tiles + BATCH, rows, capacity * rows), jnp.bfloat16),
            pltpu.VMEM((irreps, 8, BATCH * rows), jnp.float32),
            pltpu.SMEM((irreps,), jnp.int32),
            pltpu.SMEM((irreps,), jnp.int32),
            pltpu.SMEM((irreps,), jnp.int32),
            pltpu.SMEM((irreps,), jnp.int32),
            pltpu.SMEM((own_tiles,), jnp.int32),
            pltpu.SemaphoreType.DMA,
            pltpu.SemaphoreType.DMA,
            pltpu.SemaphoreType.DMA,
        ],
        compiler_params=pltpu.CompilerParams(vmem_limit_bytes=VMEM_BYTES),
        name="ladder",
    )(counts, irrep, dest, integrals, *sources)


def per_device(amplitudes, ij_counts, integrals, ab_irrep):
    shard_tiles, rows, _ = amplitudes.shape
    devices = lax.axis_size("vir")
    me = lax.axis_index("vir")
    capacity = shard_tiles * devices // 4
    same_core = [list(range(core, devices, 2)) for core in range(2)]
    swap_core = [(d, d ^ 1) for d in range(devices)]

    mine = lax.all_gather(amplitudes, "vir", axis=0, tiled=True, axis_index_groups=same_core)
    other = lax.ppermute(mine, "vir", swap_core)
    core = me % 2
    half = jnp.arange(devices // 2, dtype=jnp.int32) * 2
    dest = jnp.concatenate([half + core, half + 1 - core]) * shard_tiles

    residual, stats = ladder(ij_counts, ab_irrep, dest, integrals, [mine, other], shard_tiles, capacity)

    step = 1
    while step < devices:
        stats = stats + lax.ppermute(stats, "vir", [(d, d ^ step) for d in range(devices)])
        step *= 2
    irrep_sums, ab_counts = jnp.sum(stats, axis=2)
    entries = ab_counts * ij_counts.astype(jnp.float32) * float(rows * rows)
    return residual, jnp.sqrt(irrep_sums / entries + 1e-06)


def solution(mesh):
    in_specs = (
        P(("groups", "vir"), None, None),
        P("groups"),
        P(("groups", "vir"), None, None),
        P(("groups", "vir")),
    )
    out_specs = (P(("groups", "vir"), None, None), P("groups"))
    return jax.shard_map(
        per_device, mesh=mesh, in_specs=in_specs, out_specs=out_specs, check_vma=False
    )
```

```python
import functools

import jax
import jax.numpy as jnp
from jax import lax
from jax.experimental import pallas as pl
from jax.experimental.pallas import tpu as pltpu
from jax.sharding import PartitionSpec as P

BATCH = 4
VMEM_BYTES = 56 * 1024 * 1024


def ladder_kernel(
    capacity, shard_tiles, n_sources,
    counts_ref, irrep_ref, dest_ref, v_hbm, *refs,
):
    sources = refs[:n_sources]
    res_hbm, stats_ref = refs[n_sources:n_sources + 2]
    a_buf, v_buf, o_buf, acc_ref, size_ref, first_ref, next_ref, offset_ref, order_ref = (
        refs[n_sources + 2:n_sources + 11]
    )
    a_sem, v_sem, o_sem = refs[n_sources + 11:]
    own_tiles, rows, width = v_hbm.shape
    irreps = counts_ref.shape[0]
    all_tiles = sum(source.shape[0] for source in sources)

    piece = 0
    for source in sources:
        for start in range(0, source.shape[0], shard_tiles):
            pltpu.make_async_copy(
                source.at[pl.ds(start, shard_tiles)],
                a_buf.at[pl.ds(dest_ref[piece], shard_tiles)],
                a_sem,
            ).start()
            piece += 1

    for s in range(irreps):
        size_ref[s] = 0

    def count(l, carry):
        s = irrep_ref[l]
        size_ref[s] = size_ref[s] + 1
        return carry

    lax.fori_loop(0, own_tiles, count, 0)
    first, offset = jnp.int32(0), jnp.int32(0)
    for s in range(irreps):
        first_ref[s] = first
        next_ref[s] = first
        offset_ref[s] = offset
        first = first + size_ref[s]
        offset = offset + counts_ref[s]

    def place(l, carry):
        s = irrep_ref[l]
        slot = next_ref[s]
        next_ref[s] = slot + 1
        order_ref[slot] = l
        pltpu.make_async_copy(v_hbm.at[l], v_buf.at[slot], v_sem).start()
        return carry

    lax.fori_loop(0, own_tiles, place, 0)
    pltpu.make_async_copy(v_hbm, v_buf.at[pl.ds(0, own_tiles)], v_sem).wait()
    whole = a_buf.at[pl.ds(0, all_tiles)]
    pltpu.make_async_copy(whole, whole, a_sem).wait()

    side = BATCH * rows
    row_at = lax.broadcasted_iota(jnp.int32, (side, side), 0)
    col_at = lax.broadcasted_iota(jnp.int32, (side, side), 1)

    def symmetry(s, carry):
        size, slot0 = size_ref[s], first_ref[s]
        tiles, offset = counts_ref[s], offset_ref[s]
        blocks = (tiles + BATCH - 1) // BATCH

        def member_batch(i, total):
            slot = slot0 + i * BATCH
            rows_left = (size - i * BATCH) * rows

            def column_block(j, total):
                left = v_buf[pl.ds(slot, BATCH)].reshape(side, width)
                right = a_buf[pl.ds(offset + j * BATCH, BATCH)].reshape(side, width)
                product = lax.dot_general(
                    left, right, (((1,), (1,)), ((), ())),
                    preferred_element_type=jnp.float32,
                )
                keep = (row_at < rows_left) & (col_at < (tiles - j * BATCH) * rows)
                product = jnp.where(keep, product, 0.0)
                o_buf[pl.ds(slot, BATCH), :, pl.ds(pl.multiple_of(j * side, side), side)] = (
                    product.astype(jnp.bfloat16).reshape(BATCH, rows, side)
                )
                squares = (product * product).reshape(side // 8, 8, side)
                return total + jnp.sum(squares, axis=0)

            def blank_block(j, inner):
                o_buf[pl.ds(slot, BATCH), :, pl.ds(pl.multiple_of(j * side, side), side)] = (
                    jnp.zeros((BATCH, rows, side), jnp.bfloat16)
                )
                return inner

            total = lax.fori_loop(0, blocks, column_block, total)
            lax.fori_loop(blocks, capacity // BATCH, blank_block, 0)
            for t in range(BATCH):
                @pl.when(i * BATCH + t < size)
                def _():
                    pltpu.make_async_copy(
                        o_buf.at[slot + t], res_hbm.at[order_ref[slot + t]], o_sem
                    ).start()
            return total

        acc_ref[s] = lax.fori_loop(
            0, (size + BATCH - 1) // BATCH, member_batch, jnp.zeros((8, side), jnp.float32)
        )
        return carry

    lax.fori_loop(0, irreps, symmetry, 0)
    sums = jnp.sum(acc_ref[...], axis=1)
    sums = sum(sums[:, k:k + 128] for k in range(0, side, 128))
    stats_ref[0] = sums
    at_row = lax.broadcasted_iota(jnp.int32, sums.shape, 0)
    at_lane = lax.broadcasted_iota(jnp.int32, sums.shape, 1)
    sizes = jnp.zeros(sums.shape, jnp.int32)
    for s in range(irreps):
        sizes = jnp.where((at_row == s) & (at_lane == 0), size_ref[s], sizes)
    stats_ref[1] = sizes.astype(jnp.float32)
    pltpu.make_async_copy(o_buf.at[pl.ds(0, own_tiles)], res_hbm, o_sem).wait()


def ladder(counts, irrep, dest, integrals, sources, shard_tiles, capacity):
    own_tiles, rows, width = integrals.shape
    irreps = counts.shape[0]
    all_tiles = sum(source.shape[0] for source in sources)
    smem = pl.BlockSpec(memory_space=pltpu.SMEM)
    anywhere = pl.BlockSpec(memory_space=pl.ANY)
    return pl.pallas_call(
        functools.partial(ladder_kernel, capacity, shard_tiles, len(sources)),
        out_shape=(
            jax.ShapeDtypeStruct((own_tiles, rows, capacity * rows), jnp.bfloat16),
            jax.ShapeDtypeStruct((2, irreps, 128), jnp.float32),
        ),
        in_specs=[smem, smem, smem] + [anywhere] * (1 + len(sources)),
        out_specs=(anywhere, pl.BlockSpec(memory_space=pltpu.VMEM)),
        scratch_shapes=[
            pltpu.VMEM((all_tiles + BATCH, rows, width), jnp.bfloat16),
            pltpu.VMEM((own_tiles + BATCH, rows, width), jnp.bfloat16),
            pltpu.VMEM((own_tiles + BATCH, rows, capacity * rows), jnp.bfloat16),
            pltpu.VMEM((irreps, 8, BATCH * rows), jnp.float32),
            pltpu.SMEM((irreps,), jnp.int32),
            pltpu.SMEM((irreps,), jnp.int32),
            pltpu.SMEM((irreps,), jnp.int32),
            pltpu.SMEM((irreps,), jnp.int32),
            pltpu.SMEM((own_tiles,), jnp.int32),
            pltpu.SemaphoreType.DMA,
            pltpu.SemaphoreType.DMA,
            pltpu.SemaphoreType.DMA,
        ],
        compiler_params=pltpu.CompilerParams(vmem_limit_bytes=VMEM_BYTES),
        name="ladder",
    )(counts, irrep, dest, integrals, *sources)


def per_device(amplitudes, ij_counts, integrals, ab_irrep):
    shard_tiles, rows, _ = amplitudes.shape
    devices = lax.axis_size("vir")
    depth = devices // 4
    me = lax.axis_index("vir")
    z, y, core = me // 4, me // 2 % 2, me % 2
    capacity = shard_tiles * devices // 4

    def shift_z(x, by):
        return lax.ppermute(x, "vir", [(d, (d + 4 * by) % devices) for d in range(devices)])

    def swap(x, bit):
        return lax.ppermute(x, "vir", [(d, d ^ bit) for d in range(devices)])

    sources, dest = [], []
    here = amplitudes
    for k in range(depth):
        there = swap(here, 2)
        sources += [here, there, swap(here, 1), swap(there, 1)]
        at = (z + depth - k) % depth
        for other_y, other_core in ((0, 0), (1, 0), (0, 1), (1, 1)):
            dest.append((at * 2 + (y ^ other_y)) * 2 + (core ^ other_core))
        if k < depth - 1:
            here = shift_z(here, 1)
    dest = jnp.stack(dest) * shard_tiles

    residual, stats = ladder(ij_counts, ab_irrep, dest, integrals, sources, shard_tiles, capacity)

    stats = sum([shift_z(stats, by) for by in range(1, depth)], stats)
    stats = sum([swap(stats, bits) for bits in (1, 2, 3)], stats)
    irrep_sums, ab_counts = jnp.sum(stats, axis=2)
    entries = ab_counts * ij_counts.astype(jnp.float32) * float(rows * rows)
    return residual, jnp.sqrt(irrep_sums / entries + 1e-06)


def solution(mesh):
    in_specs = (
        P(("groups", "vir"), None, None),
        P("groups"),
        P(("groups", "vir"), None, None),
        P(("groups", "vir")),
    )
    out_specs = (P(("groups", "vir"), None, None), P("groups"))
    return jax.shard_map(
        per_device, mesh=mesh, in_specs=in_specs, out_specs=out_specs, check_vma=False
    )
```

```python
import functools

import jax
import jax.numpy as jnp
from jax import lax
from jax.experimental import pallas as pl
from jax.experimental.pallas import tpu as pltpu
from jax.sharding import PartitionSpec as P

BATCH = 4
VMEM_BYTES = 56 * 1024 * 1024


def ladder_kernel(
    capacity, shard_tiles, n_sources,
    counts_ref, irrep_ref, dest_ref, v_hbm, *refs,
):
    sources = refs[:n_sources]
    res_hbm, stats_ref = refs[n_sources:n_sources + 2]
    a_buf, v_buf, o_buf, acc_ref, size_ref, first_ref, next_ref, offset_ref, order_ref = (
        refs[n_sources + 2:n_sources + 11]
    )
    a_sem, v_sem, o_sem = refs[n_sources + 11:]
    own_tiles, rows, width = v_hbm.shape
    irreps = counts_ref.shape[0]
    all_tiles = sum(source.shape[0] for source in sources)

    piece = 0
    for source in sources:
        for start in range(0, source.shape[0], shard_tiles):
            pltpu.make_async_copy(
                source.at[pl.ds(start, shard_tiles)],
                a_buf.at[pl.ds(dest_ref[piece], shard_tiles)],
                a_sem,
            ).start()
            piece += 1

    for s in range(irreps):
        size_ref[s] = 0

    def count(l, carry):
        s = irrep_ref[l]
        size_ref[s] = size_ref[s] + 1
        return carry

    lax.fori_loop(0, own_tiles, count, 0)
    first, offset = jnp.int32(0), jnp.int32(0)
    for s in range(irreps):
        first_ref[s] = first
        next_ref[s] = first
        offset_ref[s] = offset
        first = first + size_ref[s]
        offset = offset + counts_ref[s]

    def place(l, carry):
        s = irrep_ref[l]
        slot = next_ref[s]
        next_ref[s] = slot + 1
        order_ref[slot] = l
        pltpu.make_async_copy(v_hbm.at[l], v_buf.at[slot], v_sem).start()
        return carry

    lax.fori_loop(0, own_tiles, place, 0)
    pltpu.make_async_copy(v_hbm, v_buf.at[pl.ds(0, own_tiles)], v_sem).wait()
    whole = a_buf.at[pl.ds(0, all_tiles)]
    pltpu.make_async_copy(whole, whole, a_sem).wait()

    side = BATCH * rows
    row_at = lax.broadcasted_iota(jnp.int32, (side, side), 0)
    col_at = lax.broadcasted_iota(jnp.int32, (side, side), 1)

    def symmetry(s, carry):
        size, slot0 = size_ref[s], first_ref[s]
        tiles, offset = counts_ref[s], offset_ref[s]
        blocks = (tiles + BATCH - 1) // BATCH

        def member_batch(i, total):
            slot = slot0 + i * BATCH
            rows_left = (size - i * BATCH) * rows

            def column_block(j, total):
                left = v_buf[pl.ds(slot, BATCH)].reshape(side, width)
                right = a_buf[pl.ds(offset + j * BATCH, BATCH)].reshape(side, width)
                product = lax.dot_general(
                    left, right, (((1,), (1,)), ((), ())),
                    preferred_element_type=jnp.float32,
                )
                keep = (row_at < rows_left) & (col_at < (tiles - j * BATCH) * rows)
                product = jnp.where(keep, product, 0.0)
                o_buf[pl.ds(slot, BATCH), :, pl.ds(pl.multiple_of(j * side, side), side)] = (
                    product.astype(jnp.bfloat16).reshape(BATCH, rows, side)
                )
                squares = (product * product).reshape(side // 8, 8, side)
                return total + jnp.sum(squares, axis=0)

            def blank_block(j, inner):
                o_buf[pl.ds(slot, BATCH), :, pl.ds(pl.multiple_of(j * side, side), side)] = (
                    jnp.zeros((BATCH, rows, side), jnp.bfloat16)
                )
                return inner

            total = lax.fori_loop(0, blocks, column_block, total)
            lax.fori_loop(blocks, capacity // BATCH, blank_block, 0)
            for t in range(BATCH):
                @pl.when(i * BATCH + t < size)
                def _():
                    pltpu.make_async_copy(
                        o_buf.at[slot + t], res_hbm.at[order_ref[slot + t]], o_sem
                    ).start()
            return total

        acc_ref[s] = lax.fori_loop(
            0, (size + BATCH - 1) // BATCH, member_batch, jnp.zeros((8, side), jnp.float32)
        )
        return carry

    lax.fori_loop(0, irreps, symmetry, 0)
    sums = jnp.sum(acc_ref[...], axis=1)
    sums = sum(sums[:, k:k + 128] for k in range(0, side, 128))
    stats_ref[0] = sums
    at_row = lax.broadcasted_iota(jnp.int32, sums.shape, 0)
    at_lane = lax.broadcasted_iota(jnp.int32, sums.shape, 1)
    sizes = jnp.zeros(sums.shape, jnp.int32)
    for s in range(irreps):
        sizes = jnp.where((at_row == s) & (at_lane == 0), size_ref[s], sizes)
    stats_ref[1] = sizes.astype(jnp.float32)
    pltpu.make_async_copy(o_buf.at[pl.ds(0, own_tiles)], res_hbm, o_sem).wait()


def ladder(counts, irrep, dest, integrals, sources, shard_tiles, capacity):
    own_tiles, rows, width = integrals.shape
    irreps = counts.shape[0]
    all_tiles = sum(source.shape[0] for source in sources)
    smem = pl.BlockSpec(memory_space=pltpu.SMEM)
    anywhere = pl.BlockSpec(memory_space=pl.ANY)
    return pl.pallas_call(
        functools.partial(ladder_kernel, capacity, shard_tiles, len(sources)),
        out_shape=(
            jax.ShapeDtypeStruct((own_tiles, rows, capacity * rows), jnp.bfloat16),
            jax.ShapeDtypeStruct((2, irreps, 128), jnp.float32),
        ),
        in_specs=[smem, smem, smem] + [anywhere] * (1 + len(sources)),
        out_specs=(anywhere, pl.BlockSpec(memory_space=pltpu.VMEM)),
        scratch_shapes=[
            pltpu.VMEM((all_tiles + BATCH, rows, width), jnp.bfloat16),
            pltpu.VMEM((own_tiles + BATCH, rows, width), jnp.bfloat16),
            pltpu.VMEM((own_tiles + BATCH, rows, capacity * rows), jnp.bfloat16),
            pltpu.VMEM((irreps, 8, BATCH * rows), jnp.float32),
            pltpu.SMEM((irreps,), jnp.int32),
            pltpu.SMEM((irreps,), jnp.int32),
            pltpu.SMEM((irreps,), jnp.int32),
            pltpu.SMEM((irreps,), jnp.int32),
            pltpu.SMEM((own_tiles,), jnp.int32),
            pltpu.SemaphoreType.DMA,
            pltpu.SemaphoreType.DMA,
            pltpu.SemaphoreType.DMA,
        ],
        compiler_params=pltpu.CompilerParams(vmem_limit_bytes=VMEM_BYTES),
        name="ladder",
    )(counts, irrep, dest, integrals, *sources)


def per_device(amplitudes, ij_counts, integrals, ab_irrep):
    shard_tiles, rows, _ = amplitudes.shape
    devices = lax.axis_size("vir")
    depth = devices // 4
    me = lax.axis_index("vir")
    z, y, core = me // 4, me // 2 % 2, me % 2
    capacity = shard_tiles * devices // 4

    def shift_z(x, by):
        return lax.ppermute(x, "vir", [(d, (d + 4 * by) % devices) for d in range(devices)])

    def swap(x, bit):
        return lax.ppermute(x, "vir", [(d, d ^ bit) for d in range(devices)])

    def after(x, *earlier):
        return lax.optimization_barrier((x, *earlier))[0]

    half = shard_tiles // 2
    a = {(0, h): amplitudes[h * half:(h + 1) * half] for h in range(2)}
    b = {}
    z_done, y_done = [], []
    last = 2 * depth - 2
    for i in range(last + 1):
        k, h = i // 2, i % 2
        y_in = a[k, h]
        if i >= 2:
            y_in = after(y_in, y_done[i - 2])
        b[k, h] = swap(y_in, 2)
        y_done.append(b[k, h])
        if i < last:
            a[k + 1, h] = shift_z(a[k, h], 1)
            z_done.append(a[k + 1, h])
        else:
            b[k, 1] = shift_z(after(b[k - 1, 1], z_done[i - 2]), 1)
    sources, dest = [], []
    for k in range(depth):
        at = (z + depth - k) % depth
        for h in range(2):
            sources += [a[k, h], b[k, h], swap(a[k, h], 1), swap(b[k, h], 1)]
            for other_y, other_core in ((0, 0), (1, 0), (0, 1), (1, 1)):
                dest.append((((at * 2 + (y ^ other_y)) * 2 + (core ^ other_core)) * 2 + h))
    dest = jnp.stack(dest) * half

    residual, stats = ladder(ij_counts, ab_irrep, dest, integrals, sources, half, capacity)

    stats = sum([shift_z(stats, by) for by in range(1, depth)], stats)
    stats = sum([swap(stats, bits) for bits in (1, 2, 3)], stats)
    irrep_sums, ab_counts = jnp.sum(stats, axis=2)
    entries = ab_counts * ij_counts.astype(jnp.float32) * float(rows * rows)
    return residual, jnp.sqrt(irrep_sums / entries + 1e-06)


def solution(mesh):
    in_specs = (
        P(("groups", "vir"), None, None),
        P("groups"),
        P(("groups", "vir"), None, None),
        P(("groups", "vir")),
    )
    out_specs = (P(("groups", "vir"), None, None), P("groups"))
    return jax.shard_map(
        per_device, mesh=mesh, in_specs=in_specs, out_specs=out_specs, check_vma=False
    )
```

```python
import functools

import jax
import jax.numpy as jnp
from jax import lax
from jax.experimental import pallas as pl
from jax.experimental.pallas import tpu as pltpu
from jax.sharding import PartitionSpec as P

BATCH = 4
EDGE = BATCH - 1


def prepare_kernel(
    counts_ref, irrep_ref, v_ref, sorted_ref, order_ref, size_ref, first_ref, offset_ref,
    stats_ref, next_ref, sem,
):
    own_tiles = v_ref.shape[0]
    irreps = counts_ref.shape[0]
    for s in range(irreps):
        size_ref[s] = 0

    def count(l, carry):
        s = irrep_ref[l]
        size_ref[s] = size_ref[s] + 1
        return carry

    lax.fori_loop(0, own_tiles, count, 0)
    first, offset = jnp.int32(0), jnp.int32(0)
    for s in range(irreps):
        first_ref[s] = first
        next_ref[s] = first
        offset_ref[s] = offset
        first = first + size_ref[s]
        offset = offset + counts_ref[s]

    def place(l, carry):
        s = irrep_ref[l]
        slot = next_ref[s]
        next_ref[s] = slot + 1
        order_ref[slot] = l
        pltpu.make_async_copy(v_ref.at[l], sorted_ref.at[slot], sem).start()
        return carry

    lax.fori_loop(0, own_tiles, place, 0)
    shape = stats_ref.shape[1:]
    at_row = lax.broadcasted_iota(jnp.int32, shape, 0)
    at_lane = lax.broadcasted_iota(jnp.int32, shape, 1)
    sizes = jnp.zeros(shape, jnp.int32)
    for s in range(irreps):
        sizes = jnp.where((at_row == s) & (at_lane == 0), size_ref[s], sizes)
    stats_ref[0] = jnp.zeros(shape, jnp.float32)
    stats_ref[1] = sizes.astype(jnp.float32)
    pltpu.make_async_copy(v_ref, sorted_ref.at[pl.ds(0, own_tiles)], sem).wait()


def prepare(counts, irrep, integrals):
    own_tiles, rows, width = integrals.shape
    irreps = counts.shape[0]
    smem = pl.BlockSpec(memory_space=pltpu.SMEM)
    anywhere = pl.BlockSpec(memory_space=pl.ANY)
    return pl.pallas_call(
        prepare_kernel,
        out_shape=(
            jax.ShapeDtypeStruct((own_tiles + BATCH, rows, width), integrals.dtype),
            jax.ShapeDtypeStruct((own_tiles,), jnp.int32),
            jax.ShapeDtypeStruct((irreps,), jnp.int32),
            jax.ShapeDtypeStruct((irreps,), jnp.int32),
            jax.ShapeDtypeStruct((irreps,), jnp.int32),
            jax.ShapeDtypeStruct((2, irreps, 128), jnp.float32),
        ),
        in_specs=[smem, smem, anywhere],
        out_specs=(anywhere, smem, smem, smem, smem, pl.BlockSpec(memory_space=pltpu.VMEM)),
        scratch_shapes=[pltpu.SMEM((irreps,), jnp.int32), pltpu.SemaphoreType.DMA],
        name="prepare",
    )(counts, irrep, integrals)


def ladder_kernel(
    step, depth, shard_tiles, layout, n_above, n_below,
    me_ref, counts_ref, order_ref, size_ref, first_ref, offset_ref,
    stats_in_ref, v_hbm, res_in_ref, *refs,
):
    del res_in_ref
    fresh, refs = refs[:len(layout)], refs[len(layout):]
    above, refs = refs[:n_above], refs[n_above:]
    below, refs = refs[:n_below], refs[n_below:]
    res_hbm, stats_ref, a_buf, v_buf, o_buf, acc_ref, a_sem, v_sem, o_sem = refs
    own_tiles = order_ref.shape[0]
    irreps = counts_ref.shape[0]
    rows, width = a_buf.shape[1:]
    side = BATCH * rows
    reach = 4 * shard_tiles

    me = me_ref[0]
    z, y, core = me // 4, me // 2 % 2, me % 2
    position = lax.rem(z + depth - step, depth)
    low, high = position * reach, (position + 1) * reach

    pltpu.make_async_copy(v_hbm, v_buf, v_sem).start()
    for source, (other_y, other_core, tile) in zip(fresh, layout):
        own_y = (1 - y) if other_y else y
        own_core = (1 - core) if other_core else core
        pltpu.make_async_copy(
            source,
            a_buf.at[pl.ds(BATCH + (own_y * 2 + own_core) * shard_tiles + tile, source.shape[0])],
            a_sem,
        ).start()
    for index, source in enumerate(above):
        @pl.when(y + 2 * core == index)
        def _():
            pltpu.make_async_copy(
                source.at[pl.ds(0, EDGE)], a_buf.at[pl.ds(BATCH + reach, EDGE)], a_sem
            ).start()
    for index, source in enumerate(below):
        @pl.when(3 - y - 2 * core == index)
        def _():
            pltpu.make_async_copy(
                source.at[pl.ds(shard_tiles - EDGE, EDGE)], a_buf.at[pl.ds(1, EDGE)], a_sem
            ).start()
    arrived = reach + EDGE * (bool(above) + bool(below))
    whole = a_buf.at[pl.ds(0, arrived)]
    pltpu.make_async_copy(v_hbm, v_buf, v_sem).wait()
    pltpu.make_async_copy(whole, whole, a_sem).wait()

    row_at = lax.broadcasted_iota(jnp.int32, (side, side), 0)
    col_at = lax.broadcasted_iota(jnp.int32, (side, side), 1)

    def symmetry(s, started):
        size, slot0 = size_ref[s], first_ref[s]
        tiles, offset = counts_ref[s], offset_ref[s]
        blocks = (tiles + BATCH - 1) // BATCH
        if below:
            block0 = jnp.maximum(low - offset, 0) // BATCH
        else:
            block0 = (jnp.maximum(low - offset, 0) + BATCH - 1) // BATCH
        if above:
            block1 = (jnp.maximum(high - offset, 0) + BATCH - 1) // BATCH
        else:
            block1 = jnp.where(
                offset + tiles <= high, blocks, jnp.maximum(high - offset, 0) // BATCH
            )
        block1 = jnp.where(offset + tiles <= low, block0, jnp.minimum(block1, blocks))
        block1 = jnp.maximum(block1, block0)
        batches = (size + BATCH - 1) // BATCH

        def member_batch(i, total):
            slot = slot0 + i * BATCH
            members = jnp.minimum(size - i * BATCH, BATCH)

            def column_block(j, total):
                columns = pl.ds(pl.multiple_of(j * side, side), side)
                left = v_buf[pl.ds(slot, BATCH)].reshape(side, width)
                right = a_buf[pl.ds(BATCH + offset + j * BATCH - low, BATCH)].reshape(side, width)
                product = lax.dot_general(
                    left, right, (((1,), (1,)), ((), ())),
                    preferred_element_type=jnp.float32,
                )
                keep = (row_at < members * rows) & (col_at < (tiles - j * BATCH) * rows)
                product = jnp.where(keep, product, 0.0)
                o_buf[pl.ds(slot, BATCH), :, columns] = (
                    product.astype(jnp.bfloat16).reshape(BATCH, rows, side)
                )
                for t in range(BATCH):
                    @pl.when(t < members)
                    def _():
                        pltpu.make_async_copy(
                            o_buf.at[slot + t, :, columns],
                            res_hbm.at[order_ref[slot + t], :, columns],
                            o_sem,
                        ).start()
                squares = (product * product).reshape(side // 8, 8, side)
                return total + jnp.sum(squares, axis=0)

            return lax.fori_loop(block0, block1, column_block, total)

        acc_ref[s] = lax.fori_loop(0, batches, member_batch, jnp.zeros((8, side), jnp.float32))
        return started + size * (block1 - block0)

    started = lax.fori_loop(0, irreps, symmetry, 0)
    sums = jnp.sum(acc_ref[...], axis=1)
    sums = sum(sums[:, k:k + 128] for k in range(0, side, 128))
    stats_ref[0] = stats_in_ref[0] + sums
    stats_ref[1] = stats_in_ref[1]

    def finish(n, carry):
        pltpu.make_async_copy(
            o_buf.at[0, :, pl.ds(0, side)], res_hbm.at[0, :, pl.ds(0, side)], o_sem
        ).wait()
        return carry

    lax.fori_loop(0, started, finish, 0)


def ladder(step, depth, shard_tiles, me, counts, plan, residual, stats, fresh, layout, above, below):
    ordered, order, size, first, offset = plan
    slots, rows, width = ordered.shape
    irreps = counts.shape[0]
    smem = pl.BlockSpec(memory_space=pltpu.SMEM)
    vmem = pl.BlockSpec(memory_space=pltpu.VMEM)
    anywhere = pl.BlockSpec(memory_space=pl.ANY)
    scratch = [
        pltpu.VMEM((4 * shard_tiles + 2 * BATCH, rows, width), jnp.bfloat16),
        pltpu.VMEM((slots, rows, width), jnp.bfloat16),
        pltpu.VMEM((slots, rows, residual.shape[2]), jnp.bfloat16),
        pltpu.VMEM((irreps, 8, BATCH * rows), jnp.float32),
    ]
    vmem_bytes = 2 * (scratch[0].shape[0] + slots) * rows * width + 2 * slots * residual[0].size
    flops = 2 * residual.size * width // (2 * depth)
    return pl.pallas_call(
        functools.partial(
            ladder_kernel, step, depth, shard_tiles, layout, len(above), len(below)
        ),
        out_shape=(
            jax.ShapeDtypeStruct(residual.shape, residual.dtype),
            jax.ShapeDtypeStruct(stats.shape, stats.dtype),
        ),
        in_specs=[smem] * 6 + [vmem] + [anywhere] * (2 + len(fresh) + len(above) + len(below)),
        out_specs=(anywhere, vmem),
        scratch_shapes=scratch + [pltpu.SemaphoreType.DMA] * 3,
        input_output_aliases={8: 0},
        compiler_params=pltpu.CompilerParams(vmem_limit_bytes=vmem_bytes + 6 * 1024 * 1024),
        cost_estimate=pl.CostEstimate(
            flops=flops, bytes_accessed=residual.size * 2 // depth, transcendentals=0
        ),
        name=f"ladder_{step}",
    )(
        me, counts, order, size, first, offset, stats, ordered, residual,
        *fresh, *above, *below,
    )


def per_device(amplitudes, ij_counts, integrals, ab_irrep):
    shard_tiles, rows, _ = amplitudes.shape
    own_tiles = integrals.shape[0]
    devices = lax.axis_size("vir")
    depth = devices // 4
    me = lax.axis_index("vir").astype(jnp.int32).reshape(1)
    capacity = shard_tiles * devices // 4

    def shift_z(x):
        return lax.ppermute(x, "vir", [(d, (d + 4) % devices) for d in range(devices)])

    def swap(x, bits):
        return lax.ppermute(x, "vir", [(d, d ^ bits) for d in range(devices)])

    *plan, stats = prepare(ij_counts, ab_irrep, integrals)
    residual = jnp.zeros((own_tiles, rows, capacity * rows), jnp.bfloat16)
    half = shard_tiles // 2
    full_layout = ((0, 0, 0), (1, 0, 0), (0, 1, 0), (1, 1, 0))
    split_layout = ((0, 0, 0), (1, 0, 0), (1, 0, half), (0, 1, 0), (1, 1, 0), (1, 1, half))

    def run(step, residual, stats, groups):
        fresh = groups[step]
        return ladder(
            step, depth, shard_tiles, me, ij_counts, plan, residual, stats, fresh,
            full_layout if len(fresh) == 4 else split_layout,
            groups[step - 1] if step else (),
            groups[0] if step == depth - 1 else (),
        )

    groups = []
    here, previous = amplitudes, None
    for k in range(depth):
        if k:
            here, residual, stats, *previous = lax.optimization_barrier(
                (here, residual, stats, *previous)
            )
        if k < depth - 1:
            following = shift_z(here)
            there = (swap(here, 2),)
        else:
            there = (swap(here[:half], 2), shift_z(previous[1][half:]))
        across = swap(here, 1)
        if k:
            groups.append((*previous, swap(previous[1], 1)))
            residual, stats = run(k - 1, residual, stats, groups)
        previous = (here, *there, across)
        here = following
    residual, stats, *previous = lax.optimization_barrier((residual, stats, *previous))
    groups.append((*previous, *(swap(piece, 1) for piece in previous[1:-1])))
    residual, stats = run(depth - 1, residual, stats, groups)

    stats = sum(
        [lax.ppermute(stats, "vir", [(d, (d + 4 * by) % devices) for d in range(devices)])
         for by in range(1, depth)],
        stats,
    )
    stats = sum([swap(stats, bits) for bits in (1, 2, 3)], stats)
    irrep_sums, ab_counts = jnp.sum(stats, axis=2)
    entries = ab_counts * ij_counts.astype(jnp.float32) * float(rows * rows)
    return residual, jnp.sqrt(irrep_sums / entries + 1e-06)


def solution(mesh):
    in_specs = (
        P(("groups", "vir"), None, None),
        P("groups"),
        P(("groups", "vir"), None, None),
        P(("groups", "vir")),
    )
    out_specs = (P(("groups", "vir"), None, None), P("groups"))
    return jax.shard_map(
        per_device, mesh=mesh, in_specs=in_specs, out_specs=out_specs, check_vma=False
    )
```

```python
import functools

import jax
import jax.numpy as jnp
from jax import lax
from jax.experimental import pallas as pl
from jax.experimental.pallas import tpu as pltpu
from jax.sharding import PartitionSpec as P

BATCH = 4
UNROLL = 4
EDGE = BATCH - 1


def prepare_kernel(
    counts_ref, irrep_ref, v_ref, res_ref, sorted_ref, order_ref, size_ref, first_ref, offset_ref,
    stats_ref, blank_ref, next_ref, sem, blank_sem,
):
    own_tiles = v_ref.shape[0]
    irreps = counts_ref.shape[0]
    blank_ref[...] = jnp.zeros(blank_ref.shape, blank_ref.dtype)
    group = blank_ref.shape[0]
    for l in range(0, own_tiles, group):
        pltpu.make_async_copy(blank_ref, res_ref.at[pl.ds(l, group)], blank_sem).start()
    for s in range(irreps):
        size_ref[s] = 0

    def count(l, carry):
        s = irrep_ref[l]
        size_ref[s] = size_ref[s] + 1
        return carry

    lax.fori_loop(0, own_tiles, count, 0)
    first, offset = jnp.int32(0), jnp.int32(0)
    for s in range(irreps):
        first_ref[s] = first
        next_ref[s] = first
        offset_ref[s] = offset
        first = first + size_ref[s]
        offset = offset + counts_ref[s]

    def place(l, carry):
        s = irrep_ref[l]
        slot = next_ref[s]
        next_ref[s] = slot + 1
        order_ref[slot] = l
        pltpu.make_async_copy(v_ref.at[l], sorted_ref.at[slot], sem).start()
        return carry

    lax.fori_loop(0, own_tiles, place, 0)
    spare = sorted_ref.shape[0] - own_tiles
    sorted_ref[pl.ds(own_tiles, spare)] = jnp.zeros((spare, *sorted_ref.shape[1:]), sorted_ref.dtype)
    shape = stats_ref.shape[1:]
    at_row = lax.broadcasted_iota(jnp.int32, shape, 0)
    at_lane = lax.broadcasted_iota(jnp.int32, shape, 1)
    sizes = jnp.zeros(shape, jnp.int32)
    for s in range(irreps):
        sizes = jnp.where((at_row == s) & (at_lane == 0), size_ref[s], sizes)
    stats_ref[0] = jnp.zeros(shape, jnp.float32)
    stats_ref[1] = sizes.astype(jnp.float32)
    pltpu.make_async_copy(v_ref, sorted_ref.at[pl.ds(0, own_tiles)], sem).wait()
    pltpu.make_async_copy(res_ref, res_ref, blank_sem).wait()


def prepare(counts, irrep, integrals, capacity):
    own_tiles, rows, width = integrals.shape
    irreps = counts.shape[0]
    smem = pl.BlockSpec(memory_space=pltpu.SMEM)
    vmem = pl.BlockSpec(memory_space=pltpu.VMEM)
    anywhere = pl.BlockSpec(memory_space=pl.ANY)
    return pl.pallas_call(
        prepare_kernel,
        out_shape=(
            jax.ShapeDtypeStruct((own_tiles, rows, capacity * rows), jnp.bfloat16),
            jax.ShapeDtypeStruct((own_tiles + BATCH, rows, width), integrals.dtype),
            jax.ShapeDtypeStruct((own_tiles,), jnp.int32),
            jax.ShapeDtypeStruct((irreps,), jnp.int32),
            jax.ShapeDtypeStruct((irreps,), jnp.int32),
            jax.ShapeDtypeStruct((irreps,), jnp.int32),
            jax.ShapeDtypeStruct((2, irreps, 128), jnp.float32),
        ),
        in_specs=[smem, smem, anywhere],
        out_specs=(anywhere, vmem, smem, smem, smem, smem, vmem),
        scratch_shapes=[
            pltpu.VMEM((2, rows, capacity * rows), jnp.bfloat16),
            pltpu.SMEM((irreps,), jnp.int32),
            pltpu.SemaphoreType.DMA,
            pltpu.SemaphoreType.DMA,
        ],
        compiler_params=pltpu.CompilerParams(vmem_limit_bytes=8 * 1024 * 1024),
        cost_estimate=pl.CostEstimate(
            flops=0, bytes_accessed=2 * own_tiles * rows * capacity * rows, transcendentals=0
        ),
        name="prepare",
    )(counts, irrep, integrals)


def ladder_kernel(
    step, depth, shard_tiles, layout, n_above, n_below,
    me_ref, counts_ref, order_ref, size_ref, first_ref, offset_ref,
    stats_in_ref, v_ref, res_in_ref, *refs,
):
    del res_in_ref
    fresh, refs = refs[:len(layout)], refs[len(layout):]
    above, refs = refs[:n_above], refs[n_above:]
    below, refs = refs[:n_below], refs[n_below:]
    (
        res_hbm, stats_ref, a_buf, o_buf, acc_ref,
        slot_ref, tile_ref, block_ref, member_ref, limit_ref, group_ref, a_sem, o_sem,
    ) = refs
    own_tiles = order_ref.shape[0]
    irreps = counts_ref.shape[0]
    rows, width = a_buf.shape[1:]
    side = BATCH * rows
    reach = 4 * shard_tiles

    me = me_ref[0]
    z, y, core = me // 4, me // 2 % 2, me % 2
    position = lax.rem(z + depth - step, depth)
    low, high = position * reach, (position + 1) * reach

    for source, (other_y, other_core, tile) in zip(fresh, layout):
        own_y = (1 - y) if other_y else y
        own_core = (1 - core) if other_core else core
        pltpu.make_async_copy(
            source,
            a_buf.at[pl.ds(BATCH + (own_y * 2 + own_core) * shard_tiles + tile, source.shape[0])],
            a_sem,
        ).start()
    for index, source in enumerate(above):
        @pl.when(y + 2 * core == index)
        def _():
            pltpu.make_async_copy(
                source.at[pl.ds(0, EDGE)], a_buf.at[pl.ds(BATCH + reach, EDGE)], a_sem
            ).start()
    for index, source in enumerate(below):
        @pl.when(3 - y - 2 * core == index)
        def _():
            pltpu.make_async_copy(
                source.at[pl.ds(shard_tiles - EDGE, EDGE)], a_buf.at[pl.ds(1, EDGE)], a_sem
            ).start()

    def symmetry(s, items):
        size, slot0 = size_ref[s], first_ref[s]
        tiles, offset = counts_ref[s], offset_ref[s]
        blocks = (tiles + BATCH - 1) // BATCH
        if below:
            block0 = jnp.maximum(low - offset, 0) // BATCH
        else:
            block0 = (jnp.maximum(low - offset, 0) + BATCH - 1) // BATCH
        if above:
            block1 = (jnp.maximum(high - offset, 0) + BATCH - 1) // BATCH
        else:
            block1 = jnp.where(
                offset + tiles <= high, blocks, jnp.maximum(high - offset, 0) // BATCH
            )
        block1 = jnp.where(offset + tiles <= low, block0, jnp.minimum(block1, blocks))

        def member_batch(i, items):
            def column_block(j, items):
                slot_ref[items] = slot0 + i * BATCH
                tile_ref[items] = BATCH + offset + j * BATCH - low
                block_ref[items] = j
                member_ref[items] = jnp.minimum(size - i * BATCH, BATCH)
                limit_ref[items] = (tiles - j * BATCH) * rows
                group_ref[items] = s
                return items + 1

            return lax.fori_loop(block0, block1, column_block, items)

        return lax.fori_loop(0, (size + BATCH - 1) // BATCH, member_batch, items)

    items = lax.fori_loop(0, irreps, symmetry, 0)
    for spare in range(UNROLL - 1):
        slot_ref[items + spare] = own_tiles
        tile_ref[items + spare] = BATCH
        block_ref[items + spare] = 0
        member_ref[items + spare] = 0
        limit_ref[items + spare] = 0
        group_ref[items + spare] = 0
    acc_ref[...] = jnp.zeros(acc_ref.shape, acc_ref.dtype)
    for start, stop in ((0, 1 if below else BATCH), (reach + BATCH + (EDGE if above else 0), a_buf.shape[0])):
        a_buf[pl.ds(start, stop - start)] = jnp.zeros((stop - start, rows, width), a_buf.dtype)
    arrived = reach + EDGE * (bool(above) + bool(below))
    whole = a_buf.at[pl.ds(0, arrived)]
    pltpu.make_async_copy(whole, whole, a_sem).wait()

    col_at = lax.broadcasted_iota(jnp.int32, (1, side), 1)

    def product(n):
        slot, members = slot_ref[n], member_ref[n]
        left = v_ref[pl.ds(slot, BATCH)].reshape(side, width)
        right = a_buf[pl.ds(tile_ref[n], BATCH)].reshape(side, width)
        values = lax.dot_general(
            left, right, (((1,), (1,)), ((), ())), preferred_element_type=jnp.float32
        )
        values = jnp.where(col_at < limit_ref[n], values, 0.0).reshape(BATCH, rows, side)
        columns = pl.ds(pl.multiple_of(block_ref[n] * side, side), side)
        o_buf[pl.ds(slot, BATCH), :, columns] = values.astype(jnp.bfloat16)
        squares = jnp.sum((values * values).reshape(BATCH, rows // 8, 8, side), axis=1)
        total = jnp.zeros((8, side), jnp.float32)
        for t in range(BATCH):
            total = total + jnp.where(t < members, squares[t], 0.0)
        acc_ref[group_ref[n]] += total

    def send(n, started):
        slot, members = slot_ref[n], member_ref[n]
        columns = pl.ds(pl.multiple_of(block_ref[n] * side, side), side)

        def one(t, carry):
            pltpu.make_async_copy(
                o_buf.at[slot + t, :, columns],
                res_hbm.at[order_ref[slot + t], :, columns],
                o_sem,
            ).start()
            return carry

        lax.fori_loop(0, members, one, 0)
        return started + members

    def several(u, started):
        for n in range(UNROLL):
            product(u * UNROLL + n)
        for n in range(UNROLL):
            started = send(u * UNROLL + n, started)
        return started

    started = lax.fori_loop(0, (items + UNROLL - 1) // UNROLL, several, 0)
    sums = jnp.sum(acc_ref[...], axis=1)
    sums = sum(sums[:, k:k + 128] for k in range(0, side, 128))
    stats_ref[0] = stats_in_ref[0] + sums
    stats_ref[1] = stats_in_ref[1]

    def finish(n, carry):
        pltpu.make_async_copy(
            o_buf.at[0, :, pl.ds(0, side)], res_hbm.at[0, :, pl.ds(0, side)], o_sem
        ).wait()
        return carry

    lax.fori_loop(0, started, finish, 0)


def ladder(step, depth, shard_tiles, me, counts, plan, residual, stats, fresh, layout, above, below):
    ordered, order, size, first, offset = plan
    slots, rows, width = ordered.shape
    irreps = counts.shape[0]
    smem = pl.BlockSpec(memory_space=pltpu.SMEM)
    vmem = pl.BlockSpec(memory_space=pltpu.VMEM)
    anywhere = pl.BlockSpec(memory_space=pl.ANY)
    own_tiles = order.shape[0]
    most = (own_tiles // BATCH + irreps) * (4 * shard_tiles // BATCH + 2 * irreps) + UNROLL
    a_tiles = 4 * shard_tiles + 2 * BATCH
    scratch = [
        pltpu.VMEM((a_tiles, rows, width), jnp.bfloat16),
        pltpu.VMEM((slots, rows, residual.shape[2]), jnp.bfloat16),
        pltpu.VMEM((irreps, 8, BATCH * rows), jnp.float32),
    ] + [pltpu.SMEM((most,), jnp.int32)] * 6
    vmem_bytes = 2 * (a_tiles + slots) * rows * width + 2 * slots * residual[0].size
    flops = 2 * residual.size * width // (2 * depth)
    return pl.pallas_call(
        functools.partial(
            ladder_kernel, step, depth, shard_tiles, layout, len(above), len(below)
        ),
        out_shape=(
            jax.ShapeDtypeStruct(residual.shape, residual.dtype),
            jax.ShapeDtypeStruct(stats.shape, stats.dtype),
        ),
        in_specs=[smem] * 6 + [vmem] * 2 + [anywhere] * (1 + len(fresh) + len(above) + len(below)),
        out_specs=(anywhere, vmem),
        scratch_shapes=scratch + [pltpu.SemaphoreType.DMA] * 2,
        input_output_aliases={8: 0},
        compiler_params=pltpu.CompilerParams(vmem_limit_bytes=vmem_bytes + 6 * 1024 * 1024),
        cost_estimate=pl.CostEstimate(
            flops=flops, bytes_accessed=residual.size * 2 // depth, transcendentals=0
        ),
        name=f"ladder_{step}",
    )(
        me, counts, order, size, first, offset, stats, ordered, residual,
        *fresh, *above, *below,
    )


def per_device(amplitudes, ij_counts, integrals, ab_irrep):
    shard_tiles, rows, _ = amplitudes.shape
    devices = lax.axis_size("vir")
    depth = devices // 4
    me = lax.axis_index("vir").astype(jnp.int32).reshape(1)
    capacity = shard_tiles * devices // 4

    def shift_z(x):
        return lax.ppermute(x, "vir", [(d, (d + 4) % devices) for d in range(devices)])

    def swap(x, bits):
        return lax.ppermute(x, "vir", [(d, d ^ bits) for d in range(devices)])

    residual, *plan, stats = prepare(ij_counts, ab_irrep, integrals, capacity)
    half = shard_tiles // 2
    full_layout = ((0, 0, 0), (1, 0, 0), (0, 1, 0), (1, 1, 0))
    split_layout = ((0, 0, 0), (1, 0, 0), (1, 0, half), (0, 1, 0), (1, 1, 0), (1, 1, half))

    def run(step, residual, stats, groups):
        fresh = groups[step]
        return ladder(
            step, depth, shard_tiles, me, ij_counts, plan, residual, stats, fresh,
            full_layout if len(fresh) == 4 else split_layout,
            groups[step - 1] if step else (),
            groups[0] if step == depth - 1 else (),
        )

    groups = []
    here, previous = amplitudes, None
    for k in range(depth):
        if k:
            here, residual, stats, *previous = lax.optimization_barrier(
                (here, residual, stats, *previous)
            )
        if k < depth - 1:
            following = shift_z(here)
            there = (swap(here, 2),)
        else:
            there = (swap(here[:half], 2), shift_z(previous[1][half:]))
        across = swap(here, 1)
        if k:
            groups.append((*previous, swap(previous[1], 1)))
            residual, stats = run(k - 1, residual, stats, groups)
        previous = (here, *there, across)
        here = following
    residual, stats, *previous = lax.optimization_barrier((residual, stats, *previous))
    groups.append((*previous, *(swap(piece, 1) for piece in previous[1:-1])))
    residual, stats = run(depth - 1, residual, stats, groups)

    stats = sum(
        [lax.ppermute(stats, "vir", [(d, (d + 4 * by) % devices) for d in range(devices)])
         for by in range(1, depth)],
        stats,
    )
    stats = sum([swap(stats, bits) for bits in (1, 2, 3)], stats)
    irrep_sums, ab_counts = jnp.sum(stats, axis=2)
    entries = ab_counts * ij_counts.astype(jnp.float32) * float(rows * rows)
    return residual, jnp.sqrt(irrep_sums / entries + 1e-06)


def solution(mesh):
    in_specs = (
        P(("groups", "vir"), None, None),
        P("groups"),
        P(("groups", "vir"), None, None),
        P(("groups", "vir")),
    )
    out_specs = (P(("groups", "vir"), None, None), P("groups"))
    return jax.shard_map(
        per_device, mesh=mesh, in_specs=in_specs, out_specs=out_specs, check_vma=False
    )
```

```python
import functools

import jax
import jax.numpy as jnp
from jax import lax
from jax.experimental import pallas as pl
from jax.experimental.pallas import tpu as pltpu
from jax.sharding import PartitionSpec as P

BATCH = 4
UNROLL = 4


def ring_of(depth):
    return [0, *range(1, depth, 2), *range(depth - 2 + depth % 2, 0, -2)]


def ring_place(z, depth):
    return jnp.where(z % 2 == 1, (z + 1) // 2, (depth - z // 2) % depth)


def ring_position(place, depth):
    return jnp.where(place <= depth // 2, jnp.maximum(2 * place - 1, 0), 2 * (depth - place))


def prepare_kernel(
    depth, shard_tiles,
    me_ref, counts_ref, irrep_ref, v_ref,
    res_ref, sorted_ref, gathered_ref, stats_ref, order_ref, begin_ref, item_ref,
    blank_ref, size_ref, first_ref, next_ref, cursor_ref, call_ref, sem, blank_sem,
):
    own_tiles = v_ref.shape[0]
    irreps = counts_ref.shape[0]
    rows = v_ref.shape[1]
    most = item_ref.shape[0] // 6
    blank_ref[...] = jnp.zeros(blank_ref.shape, blank_ref.dtype)
    group = blank_ref.shape[0]
    for l in range(0, own_tiles, group):
        pltpu.make_async_copy(blank_ref, res_ref.at[pl.ds(l, group)], blank_sem).start()

    for s in range(irreps):
        size_ref[s] = 0

    def count(l, carry):
        s = irrep_ref[l]
        size_ref[s] = size_ref[s] + 1
        return carry

    lax.fori_loop(0, own_tiles, count, 0)
    first = jnp.int32(0)
    for s in range(irreps):
        first_ref[s] = first
        next_ref[s] = first
        first = first + size_ref[s]

    def place(l, carry):
        s = irrep_ref[l]
        slot = next_ref[s]
        next_ref[s] = slot + 1
        order_ref[slot] = l
        pltpu.make_async_copy(v_ref.at[l], sorted_ref.at[slot], sem).start()
        return carry

    lax.fori_loop(0, own_tiles, place, 0)
    for buffer in (sorted_ref, gathered_ref):
        spare = jnp.zeros((BATCH, *buffer.shape[1:]), buffer.dtype)
        buffer[pl.ds(buffer.shape[0] - BATCH, BATCH)] = spare

    me = me_ref[0]
    z, y = me // 4, me // 2 % 2
    for part in range(2 * depth):
        lag = lax.rem(ring_place(z, depth) - ring_place(jnp.int32(part // 2), depth) + depth, depth)
        call_ref[part] = jnp.where(y == part % 2, jnp.maximum(lag - 1, 0), lag)
    for call in range(depth):
        cursor_ref[call] = 0

    def walk(visit):
        def symmetry(s, offset):
            tiles = counts_ref[s]
            batches = (size_ref[s] + BATCH - 1) // BATCH

            def block(j, carry):
                low = offset + j * BATCH
                high = offset + jnp.minimum(tiles, j * BATCH + BATCH) - 1
                call = jnp.maximum(
                    call_ref[low // (2 * shard_tiles)], call_ref[high // (2 * shard_tiles)]
                )
                visit(s, j, low, tiles, batches, call)
                return carry

            lax.fori_loop(0, (tiles + BATCH - 1) // BATCH, block, 0)
            return offset + tiles

        lax.fori_loop(0, irreps, symmetry, jnp.int32(0))

    def tally(s, j, low, tiles, batches, call):
        cursor_ref[call] = cursor_ref[call] + batches

    def write(n, slot, tile, block, members, limit, group):
        for field, value in enumerate((slot, tile, block, members, limit, group)):
            item_ref[field * most + n] = value

    def enter(s, j, low, tiles, batches, call):
        def one(i, n):
            write(
                n, first_ref[s] + i * BATCH, low, j,
                jnp.minimum(size_ref[s] - i * BATCH, BATCH), (tiles - j * BATCH) * rows, s,
            )
            return n + 1

        cursor_ref[call] = lax.fori_loop(0, batches, one, cursor_ref[call])

    walk(tally)
    begin = jnp.int32(0)
    for call in range(depth):
        begin_ref[call] = begin
        items = cursor_ref[call]
        cursor_ref[call] = begin
        begin = begin + (items + UNROLL - 1) // UNROLL * UNROLL
    begin_ref[depth] = begin
    walk(enter)
    for call in range(depth):
        def fill(n, carry):
            write(n, own_tiles, 0, 0, 0, 0, 0)
            return carry

        lax.fori_loop(cursor_ref[call], begin_ref[call + 1], fill, 0)

    shape = stats_ref.shape[1:]
    at_row = lax.broadcasted_iota(jnp.int32, shape, 0)
    at_lane = lax.broadcasted_iota(jnp.int32, shape, 1)
    sizes = jnp.zeros(shape, jnp.int32)
    for s in range(irreps):
        sizes = jnp.where((at_row == s) & (at_lane == 0), size_ref[s], sizes)
    stats_ref[0] = jnp.zeros(shape, jnp.float32)
    stats_ref[1] = sizes.astype(jnp.float32)
    pltpu.make_async_copy(v_ref, sorted_ref.at[pl.ds(0, own_tiles)], sem).wait()
    pltpu.make_async_copy(res_ref, res_ref, blank_sem).wait()


def prepare(me, counts, irrep, integrals, depth, shard_tiles):
    own_tiles, rows, width = integrals.shape
    irreps = counts.shape[0]
    capacity = shard_tiles * depth
    all_tiles = 4 * shard_tiles * depth
    most = (all_tiles // BATCH + irreps) * (own_tiles // BATCH) + depth * UNROLL
    smem = pl.BlockSpec(memory_space=pltpu.SMEM)
    vmem = pl.BlockSpec(memory_space=pltpu.VMEM)
    anywhere = pl.BlockSpec(memory_space=pl.ANY)
    return pl.pallas_call(
        functools.partial(prepare_kernel, depth, shard_tiles),
        out_shape=(
            jax.ShapeDtypeStruct((own_tiles, rows, capacity * rows), jnp.bfloat16),
            jax.ShapeDtypeStruct((own_tiles + BATCH, rows, width), integrals.dtype),
            jax.ShapeDtypeStruct((all_tiles + BATCH, rows, width), jnp.bfloat16),
            jax.ShapeDtypeStruct((2, irreps, 128), jnp.float32),
            jax.ShapeDtypeStruct((own_tiles,), jnp.int32),
            jax.ShapeDtypeStruct((depth + 1,), jnp.int32),
            jax.ShapeDtypeStruct((6 * most,), jnp.int32),
        ),
        in_specs=[smem, smem, smem, anywhere],
        out_specs=(anywhere, vmem, vmem, vmem, smem, smem, smem),
        scratch_shapes=[
            pltpu.VMEM((2, rows, capacity * rows), jnp.bfloat16),
            pltpu.SMEM((irreps,), jnp.int32),
            pltpu.SMEM((irreps,), jnp.int32),
            pltpu.SMEM((irreps,), jnp.int32),
            pltpu.SMEM((depth,), jnp.int32),
            pltpu.SMEM((2 * depth,), jnp.int32),
            pltpu.SemaphoreType.DMA,
            pltpu.SemaphoreType.DMA,
        ],
        compiler_params=pltpu.CompilerParams(vmem_limit_bytes=32 * 1024 * 1024),
        cost_estimate=pl.CostEstimate(
            flops=0, bytes_accessed=2 * own_tiles * rows * capacity * rows, transcendentals=0
        ),
        name="prepare",
    )(me, counts, irrep, integrals)


def ladder_kernel(
    call, depth, shard_tiles, layout,
    me_ref, order_ref, begin_ref, item_ref, stats_in_ref, v_ref, res_in_ref, gathered_in_ref, *refs,
):
    del res_in_ref, gathered_in_ref
    fresh, refs = refs[:len(layout)], refs[len(layout):]
    res_hbm, gathered_ref, stats_ref, o_buf, acc_ref, a_sem, o_sem = refs
    rows, width = v_ref.shape[1:]
    side = BATCH * rows
    most = item_ref.shape[0] // 6

    me = me_ref[0]
    z, y, core = me // 4, me // 2 % 2, me % 2
    arrivals = []
    for source, (lag, other_y, other_core, tile) in zip(fresh, layout):
        at = ring_position(lax.rem(ring_place(z, depth) - lag + depth, depth), depth)
        own_y = (1 - y) if other_y else y
        own_core = (1 - core) if other_core else core
        arrivals.append(pltpu.make_async_copy(
            source,
            gathered_ref.at[
                pl.ds(((at * 2 + own_y) * 2 + own_core) * shard_tiles + tile, source.shape[0])
            ],
            a_sem.at[len(arrivals)],
        ))
    for arrival in arrivals:
        arrival.start()
    acc_ref[...] = jnp.zeros(acc_ref.shape, acc_ref.dtype)
    for arrival in arrivals:
        arrival.wait()

    col_at = lax.broadcasted_iota(jnp.int32, (1, side), 1)

    def item(n):
        return [item_ref[field * most + n] for field in range(6)]

    def product(n):
        slot, tile, block, members, limit, group = item(n)
        left = v_ref[pl.ds(slot, BATCH)].reshape(side, width)
        right = gathered_ref[pl.ds(tile, BATCH)].reshape(side, width)
        values = lax.dot_general(
            left, right, (((1,), (1,)), ((), ())), preferred_element_type=jnp.float32
        )
        values = jnp.where(col_at < limit, values, 0.0).reshape(BATCH, rows, side)
        columns = pl.ds(pl.multiple_of(block * side, side), side)
        o_buf[pl.ds(slot, BATCH), :, columns] = values.astype(jnp.bfloat16)
        squares = jnp.sum((values * values).reshape(BATCH, rows // 8, 8, side), axis=1)
        total = jnp.zeros((8, side), jnp.float32)
        for t in range(BATCH):
            total = total + jnp.where(t < members, squares[t], 0.0)
        acc_ref[group] += total

    def send(n, started):
        slot, _, block, members, _, _ = item(n)
        columns = pl.ds(pl.multiple_of(block * side, side), side)

        def one(t, carry):
            pltpu.make_async_copy(
                o_buf.at[slot + t, :, columns],
                res_hbm.at[order_ref[slot + t], :, columns],
                o_sem,
            ).start()
            return carry

        lax.fori_loop(0, members, one, 0)
        return started + members

    def several(u, started):
        for n in range(UNROLL):
            product(u * UNROLL + n)
        for n in range(UNROLL):
            started = send(u * UNROLL + n, started)
        return started

    started = lax.fori_loop(
        begin_ref[call] // UNROLL, begin_ref[call + 1] // UNROLL, several, jnp.int32(0)
    )
    sums = jnp.sum(acc_ref[...], axis=1)
    sums = sum(sums[:, k:k + 128] for k in range(0, side, 128))
    stats_ref[0] = stats_in_ref[0] + sums
    stats_ref[1] = stats_in_ref[1]

    def finish(n, carry):
        pltpu.make_async_copy(
            o_buf.at[0, :, pl.ds(0, side)], res_hbm.at[0, :, pl.ds(0, side)], o_sem
        ).wait()
        return carry

    lax.fori_loop(0, started, finish, 0)


def ladder(call, depth, shard_tiles, me, plan, state, fresh, layout):
    ordered, order, begin, items = plan
    residual, gathered, stats = state
    slots, rows, width = ordered.shape
    smem = pl.BlockSpec(memory_space=pltpu.SMEM)
    vmem = pl.BlockSpec(memory_space=pltpu.VMEM)
    anywhere = pl.BlockSpec(memory_space=pl.ANY)
    out_bytes = 2 * slots * residual[0].size
    tiles = sum(source.shape[0] for source in fresh)
    return pl.pallas_call(
        functools.partial(ladder_kernel, call, depth, shard_tiles, layout),
        out_shape=tuple(jax.ShapeDtypeStruct(x.shape, x.dtype) for x in state),
        in_specs=[smem] * 4 + [vmem] * 2 + [anywhere, vmem] + [anywhere] * len(fresh),
        out_specs=(anywhere, vmem, vmem),
        scratch_shapes=[
            pltpu.VMEM((slots, rows, residual.shape[2]), jnp.bfloat16),
            pltpu.VMEM((stats.shape[1], 8, BATCH * rows), jnp.float32),
            pltpu.SemaphoreType.DMA((len(fresh),)),
            pltpu.SemaphoreType.DMA,
        ],
        input_output_aliases={6: 0, 7: 1},
        compiler_params=pltpu.CompilerParams(
            vmem_limit_bytes=out_bytes + 2 * ordered.size + 4 * gathered.size + 6 * 1024 * 1024
        ),
        cost_estimate=pl.CostEstimate(
            flops=residual.size * width * tiles // (4 * shard_tiles * depth),
            bytes_accessed=2 * residual.size * tiles // (4 * shard_tiles * depth),
            transcendentals=0,
        ),
        name=f"ladder_{call}",
    )(me, order, begin, items, stats, ordered, residual, gathered, *fresh)


def per_device(amplitudes, ij_counts, integrals, ab_irrep):
    shard_tiles, rows, _ = amplitudes.shape
    devices = lax.axis_size("vir")
    depth = devices // 4
    me = lax.axis_index("vir").astype(jnp.int32).reshape(1)
    ring = ring_of(depth)
    hop = []
    for d in range(devices):
        following = ring[(ring.index(d // 4) + 1) % depth]
        hop.append((d, following * 4 + d % 4))

    def shift_z(x):
        return lax.ppermute(x, "vir", hop)

    def swap(x, bits):
        return lax.ppermute(x, "vir", [(d, d ^ bits) for d in range(devices)])

    residual, ordered, gathered, stats, order, begin, items = prepare(
        me, ij_counts, ab_irrep, integrals, depth, shard_tiles
    )
    plan = (ordered, order, begin, items)
    state = (residual, gathered, stats)
    half = shard_tiles // 2

    a, b, c = amplitudes, None, None
    early, early_layout = (), ()
    for k in range(depth):
        if k:
            a, b, c, *state = lax.optimization_barrier((a, b, c, *state))
        if k < depth - 1:
            following = shift_z(a)
            there = swap(a, 2)
        else:
            there = (swap(a[:half], 2), shift_z(b[half:]))
        across = swap(a, 1)
        if k == 0:
            early, early_layout = (a, across), ((0, 0, 0, 0), (0, 0, 1, 0))
        else:
            state = ladder(
                k - 1, depth, shard_tiles, me, plan, state,
                (*early, b, swap(b, 1), a, across),
                (*early_layout, (k - 1, 1, 0, 0), (k - 1, 1, 1, 0), (k, 0, 0, 0), (k, 0, 1, 0)),
            )
            early, early_layout = (), ()
        a, b, c = following, there, across
    *b, residual, gathered, stats = lax.optimization_barrier((*b, *state))
    state = ladder(
        depth - 1, depth, shard_tiles, me, plan, (residual, gathered, stats),
        (*b, *(swap(piece, 1) for piece in b)),
        tuple((depth - 1, 1, core, tile) for core in range(2) for tile in (0, half)),
    )
    residual, _, stats = state

    stats = sum([swap(stats, bits) for bits in (1, 2, 3)], stats)
    bits = 4
    while bits < devices:
        stats = stats + swap(stats, bits)
        bits *= 2
    irrep_sums, ab_counts = jnp.sum(stats, axis=2)
    entries = ab_counts * ij_counts.astype(jnp.float32) * float(rows * rows)
    return residual, jnp.sqrt(irrep_sums / entries + 1e-06)


def solution(mesh):
    in_specs = (
        P(("groups", "vir"), None, None),
        P("groups"),
        P(("groups", "vir"), None, None),
        P(("groups", "vir")),
    )
    out_specs = (P(("groups", "vir"), None, None), P("groups"))
    return jax.shard_map(
        per_device, mesh=mesh, in_specs=in_specs, out_specs=out_specs, check_vma=False
    )
```

```python
import functools

import jax
import jax.numpy as jnp
from jax import lax
from jax.experimental import pallas as pl
from jax.experimental.pallas import tpu as pltpu
from jax.sharding import PartitionSpec as P

BATCH = 4
UNROLL = 4


def ring_of(depth):
    return [0, *range(1, depth, 2), *range(depth - 2 + depth % 2, 0, -2)]


def ring_place(z, depth):
    return jnp.where(z % 2 == 1, (z + 1) // 2, (depth - z // 2) % depth)


def ring_position(place, depth):
    return jnp.where(place <= depth // 2, jnp.maximum(2 * place - 1, 0), 2 * (depth - place))


def prepare_kernel(
    depth, shard_tiles,
    me_ref, counts_hbm, irrep_hbm, v_ref,
    res_ref, sorted_ref, gathered_ref, stats_ref, order_ref, begin_ref, item_ref,
    counts_ref, irrep_ref, blank_ref, size_ref, first_ref, next_ref, cursor_ref, call_ref,
    sem, blank_sem, counts_sem, irrep_sem,
):
    own_tiles = v_ref.shape[0]
    irreps = counts_ref.shape[0]
    rows = v_ref.shape[1]
    most = item_ref.shape[0] // 6
    counts_copy = pltpu.make_async_copy(counts_hbm, counts_ref, counts_sem)
    irrep_copy = pltpu.make_async_copy(irrep_hbm, irrep_ref, irrep_sem)
    counts_copy.start()
    irrep_copy.start()
    blank_ref[...] = jnp.zeros(blank_ref.shape, blank_ref.dtype)
    group = blank_ref.shape[0]
    for l in range(0, own_tiles, group):
        pltpu.make_async_copy(blank_ref, res_ref.at[pl.ds(l, group)], blank_sem).start()

    for s in range(irreps):
        size_ref[s] = 0
    counts_copy.wait()
    irrep_copy.wait()

    def count(l, carry):
        s = irrep_ref[l]
        size_ref[s] = size_ref[s] + 1
        return carry

    lax.fori_loop(0, own_tiles, count, 0)
    first = jnp.int32(0)
    for s in range(irreps):
        first_ref[s] = first
        next_ref[s] = first
        first = first + size_ref[s]

    def place(l, carry):
        s = irrep_ref[l]
        slot = next_ref[s]
        next_ref[s] = slot + 1
        order_ref[slot] = l
        pltpu.make_async_copy(v_ref.at[l], sorted_ref.at[slot], sem).start()
        return carry

    lax.fori_loop(0, own_tiles, place, 0)
    for buffer in (sorted_ref, gathered_ref):
        spare = jnp.zeros((BATCH, *buffer.shape[1:]), buffer.dtype)
        buffer[pl.ds(buffer.shape[0] - BATCH, BATCH)] = spare

    me = me_ref[0]
    z, y, core = me // 4, me // 2 % 2, me % 2
    for shard in range(4 * depth):
        lag = lax.rem(ring_place(z, depth) - ring_place(jnp.int32(shard // 4), depth) + depth, depth)
        own_y = jnp.where(core == shard % 2, jnp.maximum(lag - 1, 0), jnp.minimum(lag, depth - 2))
        other_y = jnp.where(
            (core == shard % 2) | (lag == depth - 1), lag, jnp.minimum(lag + 1, depth - 2)
        )
        call_ref[shard] = jnp.where(y == shard // 2 % 2, own_y, other_y)
    for call in range(depth):
        cursor_ref[call] = 0

    def walk(visit):
        def symmetry(s, offset):
            tiles = counts_ref[s]
            batches = (size_ref[s] + BATCH - 1) // BATCH

            def block(j, carry):
                low = offset + j * BATCH
                high = offset + jnp.minimum(tiles, j * BATCH + BATCH) - 1
                call = jnp.maximum(
                    call_ref[low // shard_tiles], call_ref[high // shard_tiles]
                )
                visit(s, j, low, tiles, batches, call)
                return carry

            lax.fori_loop(0, (tiles + BATCH - 1) // BATCH, block, 0)
            return offset + tiles

        lax.fori_loop(0, irreps, symmetry, jnp.int32(0))

    def tally(s, j, low, tiles, batches, call):
        cursor_ref[call] = cursor_ref[call] + batches

    def write(n, slot, tile, block, members, limit, group):
        for field, value in enumerate((slot, tile, block, members, limit, group)):
            item_ref[field * most + n] = value

    def enter(s, j, low, tiles, batches, call):
        def one(i, n):
            write(
                n, first_ref[s] + i * BATCH, low, j,
                jnp.minimum(size_ref[s] - i * BATCH, BATCH), (tiles - j * BATCH) * rows, s,
            )
            return n + 1

        cursor_ref[call] = lax.fori_loop(0, batches, one, cursor_ref[call])

    walk(tally)
    begin = jnp.int32(0)
    for call in range(depth):
        begin_ref[call] = begin
        items = cursor_ref[call]
        cursor_ref[call] = begin
        begin = begin + (items + UNROLL - 1) // UNROLL * UNROLL
    begin_ref[depth] = begin
    walk(enter)
    for call in range(depth):
        def fill(n, carry):
            write(n, own_tiles, 0, 0, 0, 0, 0)
            return carry

        lax.fori_loop(cursor_ref[call], begin_ref[call + 1], fill, 0)

    shape = stats_ref.shape[2:]
    at_row = lax.broadcasted_iota(jnp.int32, shape, 0)
    at_lane = lax.broadcasted_iota(jnp.int32, shape, 1)
    sizes = jnp.zeros(shape, jnp.int32)
    for s in range(irreps):
        sizes = jnp.where((at_row == s) & (at_lane == 0), size_ref[s], sizes)
    stats_ref[0, 0] = jnp.zeros(shape, jnp.float32)
    stats_ref[0, 1] = sizes.astype(jnp.float32)
    pltpu.make_async_copy(v_ref, sorted_ref.at[pl.ds(0, own_tiles)], sem).wait()
    pltpu.make_async_copy(res_ref, res_ref, blank_sem).wait()


def prepare(me, counts, irrep, integrals, depth, shard_tiles):
    own_tiles, rows, width = integrals.shape
    irreps = counts.shape[0]
    capacity = shard_tiles * depth
    all_tiles = 4 * shard_tiles * depth
    most = (all_tiles // BATCH + irreps) * (own_tiles // BATCH) + depth * UNROLL
    smem = pl.BlockSpec(memory_space=pltpu.SMEM)
    vmem = pl.BlockSpec(memory_space=pltpu.VMEM)
    anywhere = pl.BlockSpec(memory_space=pl.ANY)
    hbm = pl.BlockSpec(memory_space=pltpu.HBM)
    return pl.pallas_call(
        functools.partial(prepare_kernel, depth, shard_tiles),
        out_shape=(
            jax.ShapeDtypeStruct((own_tiles, rows, capacity * rows), jnp.bfloat16),
            jax.ShapeDtypeStruct((own_tiles + BATCH, rows, width), integrals.dtype),
            jax.ShapeDtypeStruct((all_tiles + BATCH, rows, width), jnp.bfloat16),
            jax.ShapeDtypeStruct((1, 2, irreps, 128), jnp.float32),
            jax.ShapeDtypeStruct((own_tiles,), jnp.int32),
            jax.ShapeDtypeStruct((depth + 1,), jnp.int32),
            jax.ShapeDtypeStruct((6 * most,), jnp.int32),
        ),
        in_specs=[smem, hbm, hbm, hbm],
        out_specs=(anywhere, vmem, vmem, vmem, smem, smem, smem),
        scratch_shapes=[
            pltpu.SMEM((irreps,), jnp.int32),
            pltpu.SMEM((own_tiles,), jnp.int32),
            pltpu.VMEM((2, rows, capacity * rows), jnp.bfloat16),
            pltpu.SMEM((irreps,), jnp.int32),
            pltpu.SMEM((irreps,), jnp.int32),
            pltpu.SMEM((irreps,), jnp.int32),
            pltpu.SMEM((depth,), jnp.int32),
            pltpu.SMEM((4 * depth,), jnp.int32),
            pltpu.SemaphoreType.DMA,
            pltpu.SemaphoreType.DMA,
            pltpu.SemaphoreType.DMA,
            pltpu.SemaphoreType.DMA,
        ],
        compiler_params=pltpu.CompilerParams(vmem_limit_bytes=32 * 1024 * 1024),
        cost_estimate=pl.CostEstimate(
            flops=0, bytes_accessed=2 * own_tiles * rows * capacity * rows, transcendentals=0
        ),
        name="prepare",
    )(me, counts, irrep, integrals)


def ladder_kernel(
    call, depth, shard_tiles, layout,
    me_ref, order_ref, begin_ref, item_ref, stats_in_ref, v_ref, res_in_ref, gathered_in_ref, *refs,
):
    del res_in_ref, gathered_in_ref
    fresh, refs = refs[:len(layout)], refs[len(layout):]
    res_hbm, gathered_ref, stats_ref, o_buf, acc_ref, a_sem, o_sem = refs
    rows, width = v_ref.shape[1:]
    side = BATCH * rows
    most = item_ref.shape[0] // 6

    me = me_ref[0]
    z, y, core = me // 4, me // 2 % 2, me % 2
    arrivals = []
    for source, (lag, other_y, other_core) in zip(fresh, layout):
        at = ring_position(lax.rem(ring_place(z, depth) - lag + depth, depth), depth)
        own_y = (1 - y) if other_y else y
        own_core = (1 - core) if other_core else core
        arrivals.append(pltpu.make_async_copy(
            source,
            gathered_ref.at[
                pl.ds(((at * 2 + own_y) * 2 + own_core) * shard_tiles, shard_tiles)
            ],
            a_sem.at[len(arrivals)],
        ))
    for arrival in arrivals:
        arrival.start()
    acc_ref[...] = jnp.zeros(acc_ref.shape, acc_ref.dtype)
    for arrival in arrivals:
        arrival.wait()

    col_at = lax.broadcasted_iota(jnp.int32, (1, side), 1)

    def item(n):
        return [item_ref[field * most + n] for field in range(6)]

    def product(n):
        slot, tile, block, members, limit, group = item(n)
        left = v_ref[pl.ds(slot, BATCH)].reshape(side, width)
        right = gathered_ref[pl.ds(tile, BATCH)].reshape(side, width)
        values = lax.dot_general(
            left, right, (((1,), (1,)), ((), ())), preferred_element_type=jnp.float32
        )
        values = jnp.where(col_at < limit, values, 0.0).reshape(BATCH, rows, side)
        columns = pl.ds(pl.multiple_of(block * side, side), side)
        o_buf[pl.ds(slot, BATCH), :, columns] = values.astype(jnp.bfloat16)
        squares = jnp.sum((values * values).reshape(BATCH, rows // 8, 8, side), axis=1)
        total = jnp.zeros((8, side), jnp.float32)
        for t in range(BATCH):
            total = total + jnp.where(t < members, squares[t], 0.0)
        acc_ref[group] += total

    def send(n, started):
        slot, _, block, members, _, _ = item(n)
        columns = pl.ds(pl.multiple_of(block * side, side), side)

        def one(t, carry):
            pltpu.make_async_copy(
                o_buf.at[slot + t, :, columns],
                res_hbm.at[order_ref[slot + t], :, columns],
                o_sem,
            ).start()
            return carry

        lax.fori_loop(0, members, one, 0)
        return started + members

    def several(u, started):
        for n in range(UNROLL):
            product(u * UNROLL + n)
        for n in range(UNROLL):
            started = send(u * UNROLL + n, started)
        return started

    started = lax.fori_loop(
        begin_ref[call] // UNROLL, begin_ref[call + 1] // UNROLL, several, jnp.int32(0)
    )
    sums = jnp.sum(acc_ref[...], axis=1)
    sums = sum(sums[:, k:k + 128] for k in range(0, side, 128))
    for copy in range(stats_ref.shape[0]):
        stats_ref[copy, 0] = stats_in_ref[0, 0] + sums
        stats_ref[copy, 1] = stats_in_ref[0, 1]

    def finish(n, carry):
        pltpu.make_async_copy(
            o_buf.at[0, :, pl.ds(0, side)], res_hbm.at[0, :, pl.ds(0, side)], o_sem
        ).wait()
        return carry

    lax.fori_loop(0, started, finish, 0)


def ladder(call, depth, shard_tiles, me, plan, state, fresh, layout, copies=1):
    ordered, order, begin, items = plan
    residual, gathered, stats = state
    slots, rows, width = ordered.shape
    irreps = stats.shape[2]
    smem = pl.BlockSpec(memory_space=pltpu.SMEM)
    vmem = pl.BlockSpec(memory_space=pltpu.VMEM)
    anywhere = pl.BlockSpec(memory_space=pl.ANY)
    hbm = pl.BlockSpec(memory_space=pltpu.HBM)
    out_bytes = 2 * slots * residual[0].size
    tiles = sum(source.shape[0] for source in fresh)
    return pl.pallas_call(
        functools.partial(ladder_kernel, call, depth, shard_tiles, layout),
        out_shape=(
            jax.ShapeDtypeStruct(residual.shape, residual.dtype),
            jax.ShapeDtypeStruct(gathered.shape, gathered.dtype),
            jax.ShapeDtypeStruct((copies, 2, irreps, 128), jnp.float32),
        ),
        in_specs=[smem] * 4 + [vmem] * 2 + [anywhere, vmem] + [
            hbm if where == (0, 0, 0) else anywhere for where in layout
        ],
        out_specs=(anywhere, vmem, vmem),
        scratch_shapes=[
            pltpu.VMEM((slots, rows, residual.shape[2]), jnp.bfloat16),
            pltpu.VMEM((irreps, 8, BATCH * rows), jnp.float32),
            pltpu.SemaphoreType.DMA((len(fresh),)),
            pltpu.SemaphoreType.DMA,
        ],
        input_output_aliases={6: 0, 7: 1},
        compiler_params=pltpu.CompilerParams(
            vmem_limit_bytes=out_bytes + 2 * ordered.size + 4 * gathered.size + 6 * 1024 * 1024
        ),
        cost_estimate=pl.CostEstimate(
            flops=residual.size * width * tiles // (4 * shard_tiles * depth),
            bytes_accessed=2 * residual.size * tiles // (4 * shard_tiles * depth),
            transcendentals=0,
        ),
        name=f"ladder_{call}",
    )(me, order, begin, items, stats, ordered, residual, gathered, *fresh)


def per_device(amplitudes, ij_counts, integrals, ab_irrep):
    shard_tiles, rows, _ = amplitudes.shape
    devices = lax.axis_size("vir")
    depth = devices // 4
    me = lax.axis_index("vir").astype(jnp.int32).reshape(1)
    ring = ring_of(depth)
    hop = []
    for d in range(devices):
        following = ring[(ring.index(d // 4) + 1) % depth]
        hop.append((d, following * 4 + d % 4))

    def shift_z(x):
        return lax.ppermute(x, "vir", hop)

    def swap(x, bits):
        return lax.ppermute(x, "vir", [(d, d ^ bits) for d in range(devices)])

    residual, ordered, gathered, stats, order, begin, items = prepare(
        me, ij_counts, ab_irrep, integrals, depth, shard_tiles
    )
    plan = (ordered, order, begin, items)
    state = (residual, gathered, stats)

    a, b, c, d = [amplitudes], [], [], []
    for k in range(depth):
        if k:
            d[-1:], c[-1], b[-1], a[k], state = lax.optimization_barrier(
                (d[-1:], c[-1], b[-1], a[k], state)
            )
        if k < depth - 1:
            a.append(shift_z(a[k]))
        b.append(swap(a[k], 2))
        c.append(swap(a[k], 1))
        if k:
            d.append(swap(b[k - 1], 1))
            fresh = {(k, 0, 0): a[k], (k - 1, 1, 0): b[k - 1], (k - 1, 0, 1): c[k - 1]}
            if k == 1:
                fresh[0, 0, 0] = a[0]
            else:
                fresh[k - 2, 1, 1] = d[k - 2]
            if k == depth - 1:
                fresh[k, 0, 1], fresh[k - 1, 1, 1] = c[k], d[k - 1]
            state = ladder(
                k - 1, depth, shard_tiles, me, plan, state, tuple(fresh.values()), tuple(fresh)
            )
    last, *state = lax.optimization_barrier((b[-1], *state))
    residual, _, stats = ladder(
        depth - 1, depth, shard_tiles, me, plan, state,
        (last, swap(last, 1)), ((depth - 1, 1, 0), (depth - 1, 1, 1)), devices,
    )

    stats = lax.all_to_all(stats, "vir", 0, 0, tiled=True)
    irrep_sums, ab_counts = jnp.sum(stats, axis=(0, 3))
    entries = ab_counts * ij_counts.astype(jnp.float32) * float(rows * rows)
    return residual, jnp.sqrt(irrep_sums / entries + 1e-06)


def solution(mesh):
    in_specs = (
        P(("groups", "vir"), None, None),
        P("groups"),
        P(("groups", "vir"), None, None),
        P(("groups", "vir")),
    )
    out_specs = (P(("groups", "vir"), None, None), P("groups"))
    return jax.shard_map(
        per_device, mesh=mesh, in_specs=in_specs, out_specs=out_specs, check_vma=False
    )
```

```python
import functools

import jax
import jax.numpy as jnp
from jax import lax
from jax.experimental import pallas as pl
from jax.experimental.pallas import tpu as pltpu
from jax.sharding import PartitionSpec as P

BATCH = 4
UNROLL = 4


def ring_of(depth):
    return [0, *range(1, depth, 2), *range(depth - 2 + depth % 2, 0, -2)]


def ring_place(z, depth):
    return jnp.where(z % 2 == 1, (z + 1) // 2, (depth - z // 2) % depth)


def ring_position(place, depth):
    return jnp.where(place <= depth // 2, jnp.maximum(2 * place - 1, 0), 2 * (depth - place))


def prepare_kernel(
    counts_ref, irrep_ref, v_ref,
    res_ref, sorted_ref, gathered_ref, stats_ref, order_ref, size_ref, first_ref,
    blank_ref, next_ref, sem, blank_sem,
):
    own_tiles = v_ref.shape[0]
    irreps = counts_ref.shape[0]
    blank_ref[...] = jnp.zeros(blank_ref.shape, blank_ref.dtype)
    group = blank_ref.shape[0]
    for l in range(0, own_tiles, group):
        pltpu.make_async_copy(blank_ref, res_ref.at[pl.ds(l, group)], blank_sem).start()

    for s in range(irreps):
        size_ref[s] = 0

    def count(l, carry):
        s = irrep_ref[l]
        size_ref[s] = size_ref[s] + 1
        return carry

    lax.fori_loop(0, own_tiles, count, 0)
    first = jnp.int32(0)
    for s in range(irreps):
        first_ref[s] = first
        next_ref[s] = first
        first = first + size_ref[s]

    def place(l, carry):
        s = irrep_ref[l]
        slot = next_ref[s]
        next_ref[s] = slot + 1
        order_ref[slot] = l
        pltpu.make_async_copy(v_ref.at[l], sorted_ref.at[slot], sem).start()
        return carry

    lax.fori_loop(0, own_tiles, place, 0)
    for buffer in (sorted_ref, gathered_ref):
        spare = jnp.zeros((BATCH, *buffer.shape[1:]), buffer.dtype)
        buffer[pl.ds(buffer.shape[0] - BATCH, BATCH)] = spare
    shape = stats_ref.shape[1:]
    at_row = lax.broadcasted_iota(jnp.int32, shape, 0)
    at_lane = lax.broadcasted_iota(jnp.int32, shape, 1)
    sizes = jnp.zeros(shape, jnp.int32)
    for s in range(irreps):
        sizes = jnp.where((at_row == s) & (at_lane == 0), size_ref[s], sizes)
    stats_ref[0] = jnp.zeros(shape, jnp.float32)
    stats_ref[1] = sizes.astype(jnp.float32)
    pltpu.make_async_copy(v_ref, sorted_ref.at[pl.ds(0, own_tiles)], sem).wait()
    pltpu.make_async_copy(res_ref, res_ref, blank_sem).wait()


def prepare(counts, irrep, integrals, depth, shard_tiles):
    own_tiles, rows, width = integrals.shape
    irreps = counts.shape[0]
    columns = shard_tiles * depth * rows
    smem = pl.BlockSpec(memory_space=pltpu.SMEM)
    vmem = pl.BlockSpec(memory_space=pltpu.VMEM)
    anywhere = pl.BlockSpec(memory_space=pl.ANY)
    return pl.pallas_call(
        prepare_kernel,
        out_shape=(
            jax.ShapeDtypeStruct((own_tiles, rows, columns), jnp.bfloat16),
            jax.ShapeDtypeStruct((own_tiles + BATCH, rows, width), integrals.dtype),
            jax.ShapeDtypeStruct((4 * shard_tiles * depth + BATCH, rows, width), jnp.bfloat16),
            jax.ShapeDtypeStruct((2, irreps, 128), jnp.float32),
            jax.ShapeDtypeStruct((own_tiles,), jnp.int32),
            jax.ShapeDtypeStruct((irreps,), jnp.int32),
            jax.ShapeDtypeStruct((irreps,), jnp.int32),
        ),
        in_specs=[smem, smem, anywhere],
        out_specs=(anywhere, vmem, vmem, vmem, smem, smem, smem),
        scratch_shapes=[
            pltpu.VMEM((2, rows, columns), jnp.bfloat16),
            pltpu.SMEM((irreps,), jnp.int32),
            pltpu.SemaphoreType.DMA,
            pltpu.SemaphoreType.DMA,
        ],
        compiler_params=pltpu.CompilerParams(vmem_limit_bytes=32 * 1024 * 1024),
        cost_estimate=pl.CostEstimate(
            flops=0, bytes_accessed=2 * own_tiles * rows * columns, transcendentals=0
        ),
        name="prepare",
    )(counts, irrep, integrals)


def plan_kernel(
    depth, shard_tiles, rows, own_tiles,
    me_ref, counts_ref, size_ref, first_ref, begin_ref, item_ref, cursor_ref, call_ref,
):
    irreps = counts_ref.shape[0]
    calls = begin_ref.shape[0] - 1
    most = item_ref.shape[0] // 6

    me = me_ref[0]
    z, y, core = me // 4, me // 2 % 2, me % 2
    for shard in range(4 * depth):
        lag = lax.rem(ring_place(z, depth) - ring_place(jnp.int32(shard // 4), depth) + depth, depth)
        same_core = core == shard % 2
        own_y = jnp.where(same_core, jnp.maximum(lag - 1, 0), jnp.minimum(lag, depth - 2))
        other_y = jnp.where(
            same_core | (lag == depth - 1), lag, jnp.minimum(lag + 1, depth - 2)
        )
        call_ref[shard] = jnp.where(y == shard // 2 % 2, own_y, other_y)
    for call in range(calls):
        cursor_ref[call] = 0

    def walk(visit):
        def symmetry(s, offset):
            tiles = counts_ref[s]
            batches = (size_ref[s] + BATCH - 1) // BATCH

            def block(j, carry):
                low = offset + j * BATCH
                high = offset + jnp.minimum(tiles, j * BATCH + BATCH) - 1
                call = jnp.maximum(call_ref[low // shard_tiles], call_ref[high // shard_tiles])
                visit(s, j, low, tiles, batches, call)
                return carry

            lax.fori_loop(0, (tiles + BATCH - 1) // BATCH, block, 0)
            return offset + tiles

        lax.fori_loop(0, irreps, symmetry, jnp.int32(0))

    def tally(s, j, low, tiles, batches, call):
        cursor_ref[call] = cursor_ref[call] + batches

    def write(n, slot, tile, block, members, limit, group):
        for field, value in enumerate((slot, tile, block, members, limit, group)):
            item_ref[field * most + n] = value

    def enter(s, j, low, tiles, batches, call):
        def one(i, n):
            write(
                n, first_ref[s] + i * BATCH, low, j,
                jnp.minimum(size_ref[s] - i * BATCH, BATCH), (tiles - j * BATCH) * rows, s,
            )
            return n + 1

        cursor_ref[call] = lax.fori_loop(0, batches, one, cursor_ref[call])

    walk(tally)
    begin = jnp.int32(0)
    for call in range(calls):
        begin_ref[call] = begin
        items = cursor_ref[call]
        cursor_ref[call] = begin
        begin = begin + (items + UNROLL - 1) // UNROLL * UNROLL
    begin_ref[calls] = begin
    walk(enter)
    for call in range(calls):
        def fill(n, carry):
            write(n, own_tiles, 0, 0, 0, 0, 0)
            return carry

        lax.fori_loop(cursor_ref[call], begin_ref[call + 1], fill, 0)


def plan(me, counts, size, first, depth, shard_tiles, rows, own_tiles):
    irreps = counts.shape[0]
    calls = depth
    blocks = 4 * shard_tiles * depth // BATCH + irreps
    most = blocks * (own_tiles // BATCH) + calls * UNROLL
    smem = pl.BlockSpec(memory_space=pltpu.SMEM)
    return pl.pallas_call(
        functools.partial(plan_kernel, depth, shard_tiles, rows, own_tiles),
        out_shape=(
            jax.ShapeDtypeStruct((calls + 1,), jnp.int32),
            jax.ShapeDtypeStruct((6 * most,), jnp.int32),
        ),
        in_specs=[smem] * 4,
        out_specs=(smem, smem),
        scratch_shapes=[
            pltpu.SMEM((calls,), jnp.int32), pltpu.SMEM((4 * depth,), jnp.int32)
        ],
        name="plan",
    )(me, counts, size, first)


def ladder_kernel(
    call, depth, shard_tiles, layout,
    me_ref, order_ref, begin_ref, item_ref, stats_in_ref, v_ref, res_in_ref, gathered_in_ref, *refs,
):
    del res_in_ref, gathered_in_ref
    fresh, refs = refs[:len(layout)], refs[len(layout):]
    res_hbm, gathered_ref, stats_ref, o_buf, acc_ref, a_sem, o_sem = refs
    rows, width = v_ref.shape[1:]
    side = BATCH * rows
    most = item_ref.shape[0] // 6

    me = me_ref[0]
    z, y, core = me // 4, me // 2 % 2, me % 2
    arrivals = []
    for source, (lag, other_y, other_core) in zip(fresh, layout):
        at = ring_position(lax.rem(ring_place(z, depth) - lag + depth, depth), depth)
        own_y = (1 - y) if other_y else y
        own_core = (1 - core) if other_core else core
        arrivals.append(pltpu.make_async_copy(
            source,
            gathered_ref.at[
                pl.ds(((at * 2 + own_y) * 2 + own_core) * shard_tiles, shard_tiles)
            ],
            a_sem.at[len(arrivals)],
        ))
    for arrival in arrivals:
        arrival.start()
    acc_ref[...] = jnp.zeros(acc_ref.shape, acc_ref.dtype)
    for arrival in arrivals:
        arrival.wait()

    col_at = lax.broadcasted_iota(jnp.int32, (1, side), 1)

    def item(n):
        return [item_ref[field * most + n] for field in range(6)]

    def product(n):
        slot, tile, block, members, limit, group = item(n)
        left = v_ref[pl.ds(slot, BATCH)].reshape(side, width)
        right = gathered_ref[pl.ds(tile, BATCH)].reshape(side, width)
        values = lax.dot_general(
            left, right, (((1,), (1,)), ((), ())), preferred_element_type=jnp.float32
        )
        values = jnp.where(col_at < limit, values, 0.0).reshape(BATCH, rows, side)
        columns = pl.ds(pl.multiple_of(block * side, side), side)
        o_buf[pl.ds(slot, BATCH), :, columns] = values.astype(jnp.bfloat16)
        squares = jnp.sum((values * values).reshape(BATCH, rows // 8, 8, side), axis=1)
        total = jnp.zeros((8, side), jnp.float32)
        for t in range(BATCH):
            total = total + jnp.where(t < members, squares[t], 0.0)
        acc_ref[group] += total

    def send(n, started):
        slot, _, block, members, _, _ = item(n)
        columns = pl.ds(pl.multiple_of(block * side, side), side)

        def one(t, carry):
            pltpu.make_async_copy(
                o_buf.at[slot + t, :, columns],
                res_hbm.at[order_ref[slot + t], :, columns],
                o_sem,
            ).start()
            return carry

        lax.fori_loop(0, members, one, 0)
        return started + members

    def several(u, started):
        for n in range(UNROLL):
            product(u * UNROLL + n)
        for n in range(UNROLL):
            started = send(u * UNROLL + n, started)
        return started

    started = lax.fori_loop(
        begin_ref[call] // UNROLL, begin_ref[call + 1] // UNROLL, several, jnp.int32(0)
    )
    sums = jnp.sum(acc_ref[...], axis=1)
    sums = sum(sums[:, k:k + 128] for k in range(0, side, 128))
    stats_ref[0] = stats_in_ref[0] + sums
    stats_ref[1] = stats_in_ref[1]

    def finish(n, carry):
        pltpu.make_async_copy(
            o_buf.at[0, :, pl.ds(0, side)], res_hbm.at[0, :, pl.ds(0, side)], o_sem
        ).wait()
        return carry

    lax.fori_loop(0, started, finish, 0)


def ladder(call, depth, shard_tiles, me, listing, state, arrived):
    ordered, order, begin, items = listing
    residual, gathered, stats = state
    layout, fresh = tuple(arrived), tuple(arrived.values())
    slots, rows, width = ordered.shape
    irreps = stats.shape[1]
    smem = pl.BlockSpec(memory_space=pltpu.SMEM)
    vmem = pl.BlockSpec(memory_space=pltpu.VMEM)
    anywhere = pl.BlockSpec(memory_space=pl.ANY)
    hbm = pl.BlockSpec(memory_space=pltpu.HBM)
    out_bytes = 2 * slots * residual[0].size
    tiles = sum(source.shape[0] for source in fresh)
    return pl.pallas_call(
        functools.partial(ladder_kernel, call, depth, shard_tiles, layout),
        out_shape=(
            jax.ShapeDtypeStruct(residual.shape, residual.dtype),
            jax.ShapeDtypeStruct(gathered.shape, gathered.dtype),
            jax.ShapeDtypeStruct(stats.shape, stats.dtype),
        ),
        in_specs=[smem] * 4 + [vmem] * 2 + [anywhere, vmem] + [
            hbm if where == (0, 0, 0) else anywhere for where in layout
        ],
        out_specs=(anywhere, vmem, vmem),
        scratch_shapes=[
            pltpu.VMEM((slots, rows, residual.shape[2]), jnp.bfloat16),
            pltpu.VMEM((irreps, 8, BATCH * rows), jnp.float32),
            pltpu.SemaphoreType.DMA((len(fresh),)),
            pltpu.SemaphoreType.DMA,
        ],
        input_output_aliases={6: 0, 7: 1},
        compiler_params=pltpu.CompilerParams(
            vmem_limit_bytes=out_bytes + 2 * ordered.size + 4 * gathered.size + 6 * 1024 * 1024
        ),
        cost_estimate=pl.CostEstimate(
            flops=residual.size * width * tiles // (4 * shard_tiles * depth),
            bytes_accessed=2 * residual.size * tiles // (4 * shard_tiles * depth),
            transcendentals=0,
        ),
        name=f"ladder_{call}",
    )(me, order, begin, items, stats, ordered, residual, gathered, *fresh)


def per_device(amplitudes, ij_counts, integrals, ab_irrep):
    shard_tiles, rows, _ = amplitudes.shape
    devices = lax.axis_size("vir")
    depth = devices // 4
    me = lax.axis_index("vir").astype(jnp.int32).reshape(1)
    ring = ring_of(depth)
    hop = []
    for d in range(devices):
        following = ring[(ring.index(d // 4) + 1) % depth]
        hop.append((d, following * 4 + d % 4))

    def shift_z(x):
        return lax.ppermute(x, "vir", hop)

    def swap(x, bits):
        return lax.ppermute(x, "vir", [(d, d ^ bits) for d in range(devices)])

    residual, ordered, gathered, stats, order, size, first = prepare(
        ij_counts, ab_irrep, integrals, depth, shard_tiles
    )
    state = (residual, gathered, stats)

    a, b, c, d = [amplitudes], [], [], []
    for k in range(depth):
        if k:
            c[-1], a[k], b[-1], d[-1:], state = lax.optimization_barrier(
                (c[-1], a[k], b[-1], d[-1:], state)
            )
        b.append(swap(a[k], 2))
        if k < depth - 1:
            a.append(shift_z(a[k]))
        c.append(swap(a[k], 1))
        if k == 0:
            continue
        d.append(swap(b[k - 1], 1))
        arrived = {(k, 0, 0): a[k], (k - 1, 1, 0): b[k - 1], (k - 1, 0, 1): c[k - 1]}
        if k == 1:
            arrived[0, 0, 0] = a[0]
            me, state = lax.optimization_barrier((me, state))
            begin, items = plan(
                me, ij_counts, size, first, depth, shard_tiles, rows, integrals.shape[0]
            )
            listing = (ordered, order, begin, items)
        else:
            arrived[k - 2, 1, 1] = d[k - 2]
        if k == depth - 1:
            arrived[k, 0, 1], arrived[k - 1, 1, 1] = c[k], d[k - 1]
        state = ladder(k - 1, depth, shard_tiles, me, listing, state, arrived)
    last, state = lax.optimization_barrier((b[-1], state))
    residual, _, stats = ladder(
        depth - 1, depth, shard_tiles, me, listing, state,
        {(depth - 1, 1, 0): last, (depth - 1, 1, 1): swap(last, 1)},
    )

    stats = sum([swap(stats, bits) for bits in (1, 2, 3)], stats)
    stats = sum([swap(stats, 4 * bits) for bits in range(1, depth)], stats)
    irrep_sums, ab_counts = jnp.sum(stats, axis=2)
    entries = ab_counts * ij_counts.astype(jnp.float32) * float(rows * rows)
    return residual, jnp.sqrt(irrep_sums / entries + 1e-06)


def solution(mesh):
    in_specs = (
        P(("groups", "vir"), None, None),
        P("groups"),
        P(("groups", "vir"), None, None),
        P(("groups", "vir")),
    )
    out_specs = (P(("groups", "vir"), None, None), P("groups"))
    return jax.shard_map(
        per_device, mesh=mesh, in_specs=in_specs, out_specs=out_specs, check_vma=False
    )
```

```python
import functools

import jax
import jax.numpy as jnp
from jax import lax
from jax.experimental import pallas as pl
from jax.experimental.pallas import tpu as pltpu
from jax.sharding import PartitionSpec as P

BATCH = 4
UNROLL = 4


def ring_of(depth):
    return [0, *range(1, depth, 2), *range(depth - 2 + depth % 2, 0, -2)]


def ring_place(z, depth):
    return jnp.where(z % 2 == 1, (z + 1) // 2, (depth - z // 2) % depth)


def ring_position(place, depth):
    return jnp.where(place <= depth // 2, jnp.maximum(2 * place - 1, 0), 2 * (depth - place))


def prepare_kernel(
    depth, shard_tiles,
    me_ref, counts_ref, irrep_ref,
    res_ref, gathered_ref, stats_ref, order_ref, offset_ref, stop_ref, end_ref, item_ref,
    blank_ref, next_ref, call_ref, blank_sem,
):
    own_tiles = irrep_ref.shape[0]
    irreps = counts_ref.shape[0]
    most = item_ref.shape[0] // depth
    blank_ref[...] = jnp.zeros(blank_ref.shape, blank_ref.dtype)
    group = blank_ref.shape[0]
    for l in range(0, own_tiles, group):
        pltpu.make_async_copy(blank_ref, res_ref.at[pl.ds(l, group)], blank_sem).start()

    for s in range(irreps):
        stop_ref[s] = 0
    for t in range(BATCH):
        order_ref[own_tiles + t] = 0

    def count(l, carry):
        s = irrep_ref[l]
        stop_ref[s] = stop_ref[s] + 1
        return carry

    lax.fori_loop(0, own_tiles, count, 0)
    first, offset = jnp.int32(0), jnp.int32(0)
    for s in range(irreps):
        next_ref[s] = first
        first = first + stop_ref[s]
        stop_ref[s] = first
        offset_ref[s] = offset
        offset = offset + counts_ref[s]

    def place(l, carry):
        s = irrep_ref[l]
        slot = next_ref[s]
        next_ref[s] = slot + 1
        order_ref[slot] = l
        return carry

    lax.fori_loop(0, own_tiles, place, 0)

    me = me_ref[0]
    z, y, core = me // 4, me // 2 % 2, me % 2
    for shard in range(4 * depth):
        lag = lax.rem(ring_place(z, depth) - ring_place(jnp.int32(shard // 4), depth) + depth, depth)
        same_core = core == shard % 2
        own_y = jnp.where(same_core, jnp.maximum(lag - 1, 0), jnp.minimum(lag, depth - 2))
        other_y = jnp.where(
            same_core | (lag == depth - 1), lag, jnp.minimum(lag + 1, depth - 2)
        )
        call_ref[shard] = jnp.where(y == shard // 2 % 2, own_y, other_y)

    for call in range(depth):
        end_ref[call] = call * most

    def symmetry(s, first):
        tiles, offset, stop = counts_ref[s], offset_ref[s], stop_ref[s]

        def block(j, carry):
            low = offset + j * BATCH
            high = offset + jnp.minimum(tiles, j * BATCH + BATCH) - 1
            call = jnp.maximum(call_ref[low // shard_tiles], call_ref[high // shard_tiles])
            word = (j * 256 + s) * 256 + first

            def batch(i, n):
                item_ref[n] = word + i * BATCH
                return n + 1

            end_ref[call] = lax.fori_loop(
                0, (stop - first + BATCH - 1) // BATCH, batch, end_ref[call]
            )
            return carry

        lax.fori_loop(0, (tiles + BATCH - 1) // BATCH, block, 0)
        return stop

    lax.fori_loop(0, irreps, symmetry, jnp.int32(0))
    for call in range(depth):
        end = end_ref[call]
        for spare in range(UNROLL - 1):
            item_ref[end + spare] = own_tiles

    spare = jnp.zeros((BATCH, *gathered_ref.shape[1:]), gathered_ref.dtype)
    gathered_ref[pl.ds(gathered_ref.shape[0] - BATCH, BATCH)] = spare
    shape = stats_ref.shape[1:]
    at_row = lax.broadcasted_iota(jnp.int32, shape, 0)
    at_lane = lax.broadcasted_iota(jnp.int32, shape, 1)
    sizes = jnp.zeros(shape, jnp.int32)
    first = jnp.int32(0)
    for s in range(irreps):
        sizes = jnp.where((at_row == s) & (at_lane == 0), stop_ref[s] - first, sizes)
        first = stop_ref[s]
    stats_ref[0] = jnp.zeros(shape, jnp.float32)
    stats_ref[1] = sizes.astype(jnp.float32)
    pltpu.make_async_copy(res_ref, res_ref, blank_sem).wait()


def prepare(me, counts, irrep, depth, shard_tiles, rows, width):
    own_tiles = irrep.shape[0]
    irreps = counts.shape[0]
    columns = shard_tiles * depth * rows
    all_tiles = 4 * shard_tiles * depth
    most = (all_tiles // BATCH + irreps) * (own_tiles // BATCH) + UNROLL
    smem = pl.BlockSpec(memory_space=pltpu.SMEM)
    vmem = pl.BlockSpec(memory_space=pltpu.VMEM)
    anywhere = pl.BlockSpec(memory_space=pl.ANY)
    return pl.pallas_call(
        functools.partial(prepare_kernel, depth, shard_tiles),
        out_shape=(
            jax.ShapeDtypeStruct((own_tiles, rows, columns), jnp.bfloat16),
            jax.ShapeDtypeStruct((all_tiles + BATCH, rows, width), jnp.bfloat16),
            jax.ShapeDtypeStruct((2, irreps, 128), jnp.float32),
            jax.ShapeDtypeStruct((own_tiles + BATCH,), jnp.int32),
            jax.ShapeDtypeStruct((irreps,), jnp.int32),
            jax.ShapeDtypeStruct((irreps,), jnp.int32),
            jax.ShapeDtypeStruct((depth,), jnp.int32),
            jax.ShapeDtypeStruct((depth * most,), jnp.int32),
        ),
        in_specs=[smem] * 3,
        out_specs=(anywhere, vmem, vmem, smem, smem, smem, smem, smem),
        scratch_shapes=[
            pltpu.VMEM((2, rows, columns), jnp.bfloat16),
            pltpu.SMEM((irreps,), jnp.int32),
            pltpu.SMEM((4 * depth,), jnp.int32),
            pltpu.SemaphoreType.DMA,
        ],
        compiler_params=pltpu.CompilerParams(
            vmem_limit_bytes=4 * all_tiles * rows * width + 4 * 1024 * 1024
        ),
        cost_estimate=pl.CostEstimate(
            flops=0, bytes_accessed=2 * own_tiles * rows * columns, transcendentals=0
        ),
        name="prepare",
    )(me, counts, irrep)


def ladder_kernel(
    call, depth, shard_tiles, layout,
    me_ref, counts_ref, order_ref, offset_ref, stop_ref, end_ref, item_ref,
    stats_in_ref, v_ref, res_in_ref, gathered_in_ref, *refs,
):
    del res_in_ref, gathered_in_ref
    fresh, refs = refs[:len(layout)], refs[len(layout):]
    res_hbm, gathered_ref, stats_ref, o_buf, acc_ref, a_sem, o_sem = refs
    rows, width = v_ref.shape[1:]
    side = BATCH * rows
    most = item_ref.shape[0] // depth

    me = me_ref[0]
    z, y, core = me // 4, me // 2 % 2, me % 2
    arrivals = []
    for source, (lag, other_y, other_core) in zip(fresh, layout):
        at = ring_position(lax.rem(ring_place(z, depth) - lag + depth, depth), depth)
        own_y = (1 - y) if other_y else y
        own_core = (1 - core) if other_core else core
        arrivals.append(pltpu.make_async_copy(
            source,
            gathered_ref.at[
                pl.ds(((at * 2 + own_y) * 2 + own_core) * shard_tiles, shard_tiles)
            ],
            a_sem.at[len(arrivals)],
        ))
    for arrival in arrivals:
        arrival.start()
    acc_ref[...] = jnp.zeros(acc_ref.shape, acc_ref.dtype)
    for arrival in arrivals:
        arrival.wait()

    col_at = lax.broadcasted_iota(jnp.int32, (1, side), 1)

    def item(n):
        word = item_ref[n]
        slot, group, block = word & 255, (word >> 8) & 255, word >> 16
        return slot, group, block, jnp.minimum(stop_ref[group] - slot, BATCH)

    def product(n):
        slot, group, block, members = item(n)
        left = jnp.concatenate([v_ref[order_ref[slot + t]] for t in range(BATCH)])
        right = gathered_ref[pl.ds(offset_ref[group] + block * BATCH, BATCH)].reshape(side, width)
        values = lax.dot_general(
            left, right, (((1,), (1,)), ((), ())), preferred_element_type=jnp.float32
        )
        limit = (counts_ref[group] - block * BATCH) * rows
        values = jnp.where(col_at < limit, values, 0.0).reshape(BATCH, rows, side)
        columns = pl.ds(pl.multiple_of(block * side, side), side)
        o_buf[pl.ds(slot, BATCH), :, columns] = values.astype(jnp.bfloat16)
        squares = jnp.sum((values * values).reshape(BATCH, rows // 8, 8, side), axis=1)
        total = jnp.zeros((8, side), jnp.float32)
        for t in range(BATCH):
            total = total + jnp.where(t < members, squares[t], 0.0)
        acc_ref[group] += total

    def send(n, started):
        slot, _, block, members = item(n)
        members = jnp.maximum(members, 0)
        columns = pl.ds(pl.multiple_of(block * side, side), side)

        def one(t, carry):
            pltpu.make_async_copy(
                o_buf.at[slot + t, :, columns],
                res_hbm.at[order_ref[slot + t], :, columns],
                o_sem,
            ).start()
            return carry

        lax.fori_loop(0, members, one, 0)
        return started + members

    def several(u, started):
        for n in range(UNROLL):
            product(call * most + u * UNROLL + n)
        for n in range(UNROLL):
            started = send(call * most + u * UNROLL + n, started)
        return started

    items = end_ref[call] - call * most
    started = lax.fori_loop(0, (items + UNROLL - 1) // UNROLL, several, jnp.int32(0))
    sums = jnp.sum(acc_ref[...], axis=1)
    sums = sum(sums[:, k:k + 128] for k in range(0, side, 128))
    stats_ref[0] = stats_in_ref[0] + sums
    stats_ref[1] = stats_in_ref[1]

    def finish(n, carry):
        pltpu.make_async_copy(
            o_buf.at[0, :, pl.ds(0, side)], res_hbm.at[0, :, pl.ds(0, side)], o_sem
        ).wait()
        return carry

    lax.fori_loop(0, started, finish, 0)


def ladder(call, depth, shard_tiles, integrals, listing, state, arrived):
    residual, gathered, stats = state
    layout, fresh = tuple(arrived), tuple(arrived.values())
    own_tiles, rows, width = integrals.shape
    slots = own_tiles + BATCH
    irreps = stats.shape[1]
    smem = pl.BlockSpec(memory_space=pltpu.SMEM)
    vmem = pl.BlockSpec(memory_space=pltpu.VMEM)
    anywhere = pl.BlockSpec(memory_space=pl.ANY)
    out_bytes = 2 * slots * residual[0].size
    tiles = sum(source.shape[0] for source in fresh)
    return pl.pallas_call(
        functools.partial(ladder_kernel, call, depth, shard_tiles, layout),
        out_shape=(
            jax.ShapeDtypeStruct(residual.shape, residual.dtype),
            jax.ShapeDtypeStruct(gathered.shape, gathered.dtype),
            jax.ShapeDtypeStruct(stats.shape, stats.dtype),
        ),
        in_specs=[smem] * 7 + [vmem] * 2 + [anywhere, vmem] + [anywhere] * len(fresh),
        out_specs=(anywhere, vmem, vmem),
        scratch_shapes=[
            pltpu.VMEM((slots, rows, residual.shape[2]), jnp.bfloat16),
            pltpu.VMEM((irreps, 8, BATCH * rows), jnp.float32),
            pltpu.SemaphoreType.DMA((len(fresh),)),
            pltpu.SemaphoreType.DMA,
        ],
        input_output_aliases={9: 0, 10: 1},
        compiler_params=pltpu.CompilerParams(
            vmem_limit_bytes=out_bytes + 2 * integrals.size + 4 * gathered.size + 6 * 1024 * 1024
        ),
        cost_estimate=pl.CostEstimate(
            flops=residual.size * width * tiles // (4 * shard_tiles * depth),
            bytes_accessed=2 * residual.size * tiles // (4 * shard_tiles * depth),
            transcendentals=0,
        ),
        name=f"ladder_{call}",
    )(*listing, stats, integrals, residual, gathered, *fresh)


def per_device(amplitudes, ij_counts, integrals, ab_irrep):
    shard_tiles, rows, width = amplitudes.shape
    devices = lax.axis_size("vir")
    depth = devices // 4
    me = lax.axis_index("vir").astype(jnp.int32).reshape(1)
    ring = ring_of(depth)
    hop = []
    for d in range(devices):
        following = ring[(ring.index(d // 4) + 1) % depth]
        hop.append((d, following * 4 + d % 4))

    def shift_z(x):
        return lax.ppermute(x, "vir", hop)

    def swap(x, bits):
        return lax.ppermute(x, "vir", [(d, d ^ bits) for d in range(devices)])

    residual, gathered, stats, *listing = prepare(
        me, ij_counts, ab_irrep, depth, shard_tiles, rows, width
    )
    listing = (me, ij_counts, *listing)
    state = (residual, gathered, stats)

    a, b, c, d = [amplitudes], [], [], []
    for k in range(depth):
        if k:
            c[-1], a[k], b[-1], d[-1:], state = lax.optimization_barrier(
                (c[-1], a[k], b[-1], d[-1:], state)
            )
        b.append(swap(a[k], 2))
        if k < depth - 1:
            a.append(shift_z(a[k]))
        c.append(swap(a[k], 1))
        if k == 0:
            continue
        d.append(swap(b[k - 1], 1))
        arrived = {(k, 0, 0): a[k], (k - 1, 1, 0): b[k - 1], (k - 1, 0, 1): c[k - 1]}
        if k == 1:
            arrived[0, 0, 0] = a[0]
        else:
            arrived[k - 2, 1, 1] = d[k - 2]
        if k == depth - 1:
            arrived[k, 0, 1], arrived[k - 1, 1, 1] = c[k], d[k - 1]
        state = ladder(k - 1, depth, shard_tiles, integrals, listing, state, arrived)
    last, state = lax.optimization_barrier((b[-1], state))
    residual, _, stats = ladder(
        depth - 1, depth, shard_tiles, integrals, listing, state,
        {(depth - 1, 1, 0): last, (depth - 1, 1, 1): swap(last, 1)},
    )

    stats = sum([swap(stats, bits) for bits in (1, 2, 3)], stats)
    stats = sum([swap(stats, 4 * bits) for bits in range(1, depth)], stats)
    irrep_sums, ab_counts = jnp.sum(stats, axis=2)
    entries = ab_counts * ij_counts.astype(jnp.float32) * float(rows * rows)
    return residual, jnp.sqrt(irrep_sums / entries + 1e-06)


def solution(mesh):
    in_specs = (
        P(("groups", "vir"), None, None),
        P("groups"),
        P(("groups", "vir"), None, None),
        P(("groups", "vir")),
    )
    out_specs = (P(("groups", "vir"), None, None), P("groups"))
    return jax.shard_map(
        per_device, mesh=mesh, in_specs=in_specs, out_specs=out_specs, check_vma=False
    )
```

```python
import functools

import jax
import jax.numpy as jnp
from jax import lax
from jax.experimental import pallas as pl
from jax.experimental.pallas import tpu as pltpu
from jax.sharding import PartitionSpec as P

BATCH = 4
UNROLL = 4


def ring_of(depth):
    return [0, *range(1, depth, 2), *range(depth - 2 + depth % 2, 0, -2)]


def ring_place(z, depth):
    return jnp.where(z % 2 == 1, (z + 1) // 2, (depth - z // 2) % depth)


def ring_position(place, depth):
    return jnp.where(place <= depth // 2, jnp.maximum(2 * place - 1, 0), 2 * (depth - place))


def prepare_kernel(
    depth, shard_tiles,
    me_ref, counts_ref, irrep_ref,
    res_ref, gathered_ref, stats_ref, order_ref, offset_ref, stop_ref, end_ref, item_ref,
    blank_ref, next_ref, call_ref, blank_sem,
):
    own_tiles = irrep_ref.shape[0]
    irreps = counts_ref.shape[0]
    most = item_ref.shape[0] // depth
    blank_ref[...] = jnp.zeros(blank_ref.shape, blank_ref.dtype)
    group = blank_ref.shape[0]
    for l in range(0, own_tiles, group):
        pltpu.make_async_copy(blank_ref, res_ref.at[pl.ds(l, group)], blank_sem).start()

    for s in range(irreps):
        stop_ref[s] = 0
    for t in range(BATCH):
        order_ref[own_tiles + t] = 0

    def count(l, carry):
        s = irrep_ref[l]
        stop_ref[s] = stop_ref[s] + 1
        return carry

    lax.fori_loop(0, own_tiles, count, 0)
    first, offset = jnp.int32(0), jnp.int32(0)
    for s in range(irreps):
        next_ref[s] = first
        first = first + stop_ref[s]
        stop_ref[s] = first
        offset_ref[s] = offset
        offset = offset + counts_ref[s]

    def place(l, carry):
        s = irrep_ref[l]
        slot = next_ref[s]
        next_ref[s] = slot + 1
        order_ref[slot] = l
        return carry

    lax.fori_loop(0, own_tiles, place, 0)

    me = me_ref[0]
    z, y, core = me // 4, me // 2 % 2, me % 2
    for shard in range(4 * depth):
        lag = lax.rem(ring_place(z, depth) - ring_place(jnp.int32(shard // 4), depth) + depth, depth)
        same_core = core == shard % 2
        own_y = jnp.where(same_core, jnp.maximum(lag - 1, 0), jnp.minimum(lag, depth - 2))
        other_y = jnp.where(
            same_core | (lag == depth - 1), lag, jnp.minimum(lag + 1, depth - 2)
        )
        call_ref[shard] = jnp.where(y == shard // 2 % 2, own_y, other_y)

    for call in range(depth):
        end_ref[call] = call * most

    def symmetry(s, first):
        tiles, offset, stop = counts_ref[s], offset_ref[s], stop_ref[s]

        def block(j, carry):
            low = offset + j * BATCH
            high = offset + jnp.minimum(tiles, j * BATCH + BATCH) - 1
            call = jnp.maximum(call_ref[low // shard_tiles], call_ref[high // shard_tiles])
            word = (j * 256 + s) * 256 + first

            def batch(i, n):
                item_ref[n] = word + i * BATCH
                return n + 1

            end_ref[call] = lax.fori_loop(
                0, (stop - first + BATCH - 1) // BATCH, batch, end_ref[call]
            )
            return carry

        lax.fori_loop(0, (tiles + BATCH - 1) // BATCH, block, 0)
        return stop

    lax.fori_loop(0, irreps, symmetry, jnp.int32(0))
    for call in range(depth):
        end = end_ref[call]
        for spare in range(UNROLL - 1):
            item_ref[end + spare] = own_tiles

    spare = jnp.zeros((BATCH, *gathered_ref.shape[1:]), gathered_ref.dtype)
    gathered_ref[pl.ds(gathered_ref.shape[0] - BATCH, BATCH)] = spare
    shape = stats_ref.shape[1:]
    at_row = lax.broadcasted_iota(jnp.int32, shape, 0)
    at_lane = lax.broadcasted_iota(jnp.int32, shape, 1)
    sizes = jnp.zeros(shape, jnp.int32)
    first = jnp.int32(0)
    for s in range(irreps):
        sizes = jnp.where((at_row == s) & (at_lane == 0), stop_ref[s] - first, sizes)
        first = stop_ref[s]
    stats_ref[0] = jnp.zeros(shape, jnp.float32)
    stats_ref[1] = sizes.astype(jnp.float32)
    pltpu.make_async_copy(res_ref, res_ref, blank_sem).wait()


def prepare(me, counts, irrep, depth, shard_tiles, rows, width):
    own_tiles = irrep.shape[0]
    irreps = counts.shape[0]
    columns = shard_tiles * depth * rows
    all_tiles = 4 * shard_tiles * depth
    most = (all_tiles // BATCH + irreps) * (own_tiles // BATCH) + UNROLL
    smem = pl.BlockSpec(memory_space=pltpu.SMEM)
    vmem = pl.BlockSpec(memory_space=pltpu.VMEM)
    anywhere = pl.BlockSpec(memory_space=pl.ANY)
    return pl.pallas_call(
        functools.partial(prepare_kernel, depth, shard_tiles),
        out_shape=(
            jax.ShapeDtypeStruct((own_tiles, rows, columns), jnp.bfloat16),
            jax.ShapeDtypeStruct((all_tiles + BATCH, rows, width), jnp.bfloat16),
            jax.ShapeDtypeStruct((2, irreps, 128), jnp.float32),
            jax.ShapeDtypeStruct((own_tiles + BATCH,), jnp.int32),
            jax.ShapeDtypeStruct((irreps,), jnp.int32),
            jax.ShapeDtypeStruct((irreps,), jnp.int32),
            jax.ShapeDtypeStruct((depth,), jnp.int32),
            jax.ShapeDtypeStruct((depth * most,), jnp.int32),
        ),
        in_specs=[smem] * 3,
        out_specs=(anywhere, vmem, vmem, smem, smem, smem, smem, smem),
        scratch_shapes=[
            pltpu.VMEM((2, rows, columns), jnp.bfloat16),
            pltpu.SMEM((irreps,), jnp.int32),
            pltpu.SMEM((4 * depth,), jnp.int32),
            pltpu.SemaphoreType.DMA,
        ],
        compiler_params=pltpu.CompilerParams(
            vmem_limit_bytes=4 * all_tiles * rows * width + 4 * 1024 * 1024
        ),
        cost_estimate=pl.CostEstimate(
            flops=0, bytes_accessed=2 * own_tiles * rows * columns, transcendentals=0
        ),
        name="prepare",
    )(me, counts, irrep)


def ladder_kernel(
    call, depth, shard_tiles, layout,
    me_ref, counts_ref, order_ref, offset_ref, stop_ref, end_ref, item_ref,
    stats_in_ref, v_ref, res_in_ref, gathered_in_ref, *refs,
):
    del res_in_ref, gathered_in_ref
    fresh, refs = refs[:len(layout)], refs[len(layout):]
    res_hbm, gathered_ref, stats_ref, o_buf, acc_ref, a_sem, o_sem = refs
    rows, width = v_ref.shape[1:]
    side = BATCH * rows
    most = item_ref.shape[0] // depth

    me = me_ref[0]
    z, y, core = me // 4, me // 2 % 2, me % 2
    arrivals = []
    for source, (lag, other_y, other_core) in zip(fresh, layout):
        at = ring_position(lax.rem(ring_place(z, depth) - lag + depth, depth), depth)
        own_y = (1 - y) if other_y else y
        own_core = (1 - core) if other_core else core
        arrivals.append(pltpu.make_async_copy(
            source,
            gathered_ref.at[
                pl.ds(((at * 2 + own_y) * 2 + own_core) * shard_tiles, shard_tiles)
            ],
            a_sem.at[len(arrivals)],
        ))
    for arrival in arrivals:
        arrival.start()
    acc_ref[...] = jnp.zeros(acc_ref.shape, acc_ref.dtype)
    for arrival in arrivals:
        arrival.wait()

    col_at = lax.broadcasted_iota(jnp.int32, (1, side), 1)

    def item(n):
        word = item_ref[n]
        slot, group, block = word & 255, (word >> 8) & 255, word >> 16
        return slot, group, block, jnp.minimum(stop_ref[group] - slot, BATCH)

    def multiply(n):
        slot, group, block, _ = item(n)
        left = jnp.concatenate([v_ref[order_ref[slot + t]] for t in range(BATCH)])
        right = gathered_ref[pl.ds(offset_ref[group] + block * BATCH, BATCH)].reshape(side, width)
        return lax.dot_general(
            left, right, (((1,), (1,)), ((), ())), preferred_element_type=jnp.float32
        )

    def keep(n, values):
        slot, group, block, members = item(n)
        limit = (counts_ref[group] - block * BATCH) * rows
        values = jnp.where(col_at < limit, values, 0.0).reshape(BATCH, rows, side)
        columns = pl.ds(pl.multiple_of(block * side, side), side)
        o_buf[pl.ds(slot, BATCH), :, columns] = values.astype(jnp.bfloat16)
        squares = jnp.sum((values * values).reshape(BATCH, rows // 8, 8, side), axis=1)
        total = jnp.zeros((8, side), jnp.float32)
        for t in range(BATCH):
            total = total + jnp.where(t < members, squares[t], 0.0)
        acc_ref[group] += total

    def send(n, started):
        slot, _, block, members = item(n)
        members = jnp.maximum(members, 0)
        columns = pl.ds(pl.multiple_of(block * side, side), side)

        def one(t, carry):
            pltpu.make_async_copy(
                o_buf.at[slot + t, :, columns],
                res_hbm.at[order_ref[slot + t], :, columns],
                o_sem,
            ).start()
            return carry

        lax.fori_loop(0, members, one, 0)
        return started + members

    def several(u, started):
        first = call * most + u * UNROLL
        values = multiply(first)
        for n in range(1, UNROLL):
            following = multiply(first + n)
            keep(first + n - 1, values)
            values = following
        keep(first + UNROLL - 1, values)
        for n in range(UNROLL):
            started = send(first + n, started)
        return started

    items = end_ref[call] - call * most
    started = lax.fori_loop(0, (items + UNROLL - 1) // UNROLL, several, jnp.int32(0))
    sums = jnp.sum(acc_ref[...], axis=1)
    sums = sum(sums[:, k:k + 128] for k in range(0, side, 128))
    stats_ref[0] = stats_in_ref[0] + sums
    stats_ref[1] = stats_in_ref[1]

    def finish(n, carry):
        pltpu.make_async_copy(
            o_buf.at[0, :, pl.ds(0, side)], res_hbm.at[0, :, pl.ds(0, side)], o_sem
        ).wait()
        return carry

    lax.fori_loop(0, started, finish, 0)


def ladder(call, depth, shard_tiles, integrals, listing, state, arrived):
    residual, gathered, stats = state
    layout, fresh = tuple(arrived), tuple(arrived.values())
    own_tiles, rows, width = integrals.shape
    slots = own_tiles + BATCH
    irreps = stats.shape[1]
    smem = pl.BlockSpec(memory_space=pltpu.SMEM)
    vmem = pl.BlockSpec(memory_space=pltpu.VMEM)
    anywhere = pl.BlockSpec(memory_space=pl.ANY)
    out_bytes = 2 * slots * residual[0].size
    tiles = sum(source.shape[0] for source in fresh)
    return pl.pallas_call(
        functools.partial(ladder_kernel, call, depth, shard_tiles, layout),
        out_shape=(
            jax.ShapeDtypeStruct(residual.shape, residual.dtype),
            jax.ShapeDtypeStruct(gathered.shape, gathered.dtype),
            jax.ShapeDtypeStruct(stats.shape, stats.dtype),
        ),
        in_specs=[smem] * 7 + [vmem] * 2 + [anywhere, vmem] + [anywhere] * len(fresh),
        out_specs=(anywhere, vmem, vmem),
        scratch_shapes=[
            pltpu.VMEM((slots, rows, residual.shape[2]), jnp.bfloat16),
            pltpu.VMEM((irreps, 8, BATCH * rows), jnp.float32),
            pltpu.SemaphoreType.DMA((len(fresh),)),
            pltpu.SemaphoreType.DMA,
        ],
        input_output_aliases={9: 0, 10: 1},
        compiler_params=pltpu.CompilerParams(
            vmem_limit_bytes=out_bytes + 2 * integrals.size + 4 * gathered.size + 6 * 1024 * 1024
        ),
        cost_estimate=pl.CostEstimate(
            flops=residual.size * width * tiles // (4 * shard_tiles * depth),
            bytes_accessed=2 * residual.size * tiles // (4 * shard_tiles * depth),
            transcendentals=0,
        ),
        name=f"ladder_{call}",
    )(*listing, stats, integrals, residual, gathered, *fresh)


def per_device(amplitudes, ij_counts, integrals, ab_irrep):
    shard_tiles, rows, width = amplitudes.shape
    devices = lax.axis_size("vir")
    depth = devices // 4
    me = lax.axis_index("vir").astype(jnp.int32).reshape(1)
    ring = ring_of(depth)
    hop = []
    for d in range(devices):
        following = ring[(ring.index(d // 4) + 1) % depth]
        hop.append((d, following * 4 + d % 4))

    def shift_z(x):
        return lax.ppermute(x, "vir", hop)

    def swap(x, bits):
        return lax.ppermute(x, "vir", [(d, d ^ bits) for d in range(devices)])

    residual, gathered, stats, *listing = prepare(
        me, ij_counts, ab_irrep, depth, shard_tiles, rows, width
    )
    listing = (me, ij_counts, *listing)
    state = (residual, gathered, stats)

    a, b, c, d = [amplitudes], [], [], []
    for k in range(depth):
        if k:
            if k == 1:
                a[k], b[-1], c[-1], state = lax.optimization_barrier((a[k], b[-1], c[-1], state))
            else:
                c[-1], a[k], b[-1], d[-1], state = lax.optimization_barrier(
                    (c[-1], a[k], b[-1], d[-1], state)
                )
        b.append(swap(a[k], 2))
        if k < depth - 1:
            a.append(shift_z(a[k]))
        c.append(swap(a[k], 1))
        if k == 0:
            continue
        d.append(swap(b[k - 1], 1))
        arrived = {(k, 0, 0): a[k], (k - 1, 1, 0): b[k - 1], (k - 1, 0, 1): c[k - 1]}
        if k == 1:
            arrived[0, 0, 0] = a[0]
        else:
            arrived[k - 2, 1, 1] = d[k - 2]
        if k == depth - 1:
            arrived[k, 0, 1], arrived[k - 1, 1, 1] = c[k], d[k - 1]
        state = ladder(k - 1, depth, shard_tiles, integrals, listing, state, arrived)
    last, state = lax.optimization_barrier((b[-1], state))
    residual, _, stats = ladder(
        depth - 1, depth, shard_tiles, integrals, listing, state,
        {(depth - 1, 1, 0): last, (depth - 1, 1, 1): swap(last, 1)},
    )

    stats = sum([swap(stats, bits) for bits in (1, 2, 3)], stats)
    stats = sum([swap(stats, 4 * bits) for bits in range(1, depth)], stats)
    irrep_sums, ab_counts = jnp.sum(stats, axis=2)
    entries = ab_counts * ij_counts.astype(jnp.float32) * float(rows * rows)
    return residual, jnp.sqrt(irrep_sums / entries + 1e-06)


def solution(mesh):
    in_specs = (
        P(("groups", "vir"), None, None),
        P("groups"),
        P(("groups", "vir"), None, None),
        P(("groups", "vir")),
    )
    out_specs = (P(("groups", "vir"), None, None), P("groups"))
    return jax.shard_map(
        per_device, mesh=mesh, in_specs=in_specs, out_specs=out_specs, check_vma=False
    )
```

```python
import functools

import jax
import jax.numpy as jnp
from jax import lax
from jax.experimental import pallas as pl
from jax.experimental.pallas import tpu as pltpu
from jax.sharding import PartitionSpec as P

BATCH = 4
UNROLL = 4


def ring_of(depth):
    return [0, *range(1, depth, 2), *range(depth - 2 + depth % 2, 0, -2)]


def ring_place(z, depth):
    return jnp.where(z % 2 == 1, (z + 1) // 2, (depth - z // 2) % depth)


def ring_position(place, depth):
    return jnp.where(place <= depth // 2, jnp.maximum(2 * place - 1, 0), 2 * (depth - place))


def prepare_kernel(
    depth, shard_tiles,
    me_ref, counts_ref, irrep_ref,
    res_ref, gathered_ref, stats_ref, order_ref, offset_ref, stop_ref, end_ref, item_ref,
    blank_ref, next_ref, call_ref, blank_sem,
):
    own_tiles = irrep_ref.shape[0]
    irreps = counts_ref.shape[0]
    most = item_ref.shape[0] // depth
    blank_ref[...] = jnp.zeros(blank_ref.shape, blank_ref.dtype)
    group = blank_ref.shape[0]
    for l in range(0, own_tiles, group):
        pltpu.make_async_copy(blank_ref, res_ref.at[pl.ds(l, group)], blank_sem).start()

    for s in range(irreps):
        stop_ref[s] = 0
    for t in range(BATCH):
        order_ref[own_tiles + t] = 0

    def count(l, carry):
        s = irrep_ref[l]
        stop_ref[s] = stop_ref[s] + 1
        return carry

    lax.fori_loop(0, own_tiles, count, 0)
    first, offset = jnp.int32(0), jnp.int32(0)
    for s in range(irreps):
        next_ref[s] = first
        first = first + stop_ref[s]
        stop_ref[s] = first
        offset_ref[s] = offset
        offset = offset + counts_ref[s]

    def place(l, carry):
        s = irrep_ref[l]
        slot = next_ref[s]
        next_ref[s] = slot + 1
        order_ref[slot] = l
        return carry

    lax.fori_loop(0, own_tiles, place, 0)

    me = me_ref[0]
    z, y, core = me // 4, me // 2 % 2, me % 2
    for shard in range(4 * depth):
        lag = lax.rem(ring_place(z, depth) - ring_place(jnp.int32(shard // 4), depth) + depth, depth)
        same_core = core == shard % 2
        own_y = jnp.where(same_core, jnp.maximum(lag - 1, 0), jnp.minimum(lag, depth - 2))
        other_y = jnp.where(
            same_core | (lag == depth - 1), lag, jnp.minimum(lag + 1, depth - 2)
        )
        call_ref[shard] = jnp.where(y == shard // 2 % 2, own_y, other_y)

    for call in range(depth):
        end_ref[call] = call * most

    def symmetry(s, first):
        tiles, offset, stop = counts_ref[s], offset_ref[s], stop_ref[s]

        def block(j, carry):
            low = offset + j * BATCH
            high = offset + jnp.minimum(tiles, j * BATCH + BATCH) - 1
            call = jnp.maximum(call_ref[low // shard_tiles], call_ref[high // shard_tiles])
            word = (j * 256 + s) * 256 + first

            def batch(i, n):
                item_ref[n] = word + i * BATCH
                return n + 1

            end_ref[call] = lax.fori_loop(
                0, (stop - first + BATCH - 1) // BATCH, batch, end_ref[call]
            )
            return carry

        lax.fori_loop(0, (tiles + BATCH - 1) // BATCH, block, 0)
        return stop

    lax.fori_loop(0, irreps, symmetry, jnp.int32(0))
    for call in range(depth):
        end = end_ref[call]
        for spare in range(UNROLL - 1):
            item_ref[end + spare] = own_tiles

    spare = jnp.zeros((BATCH, *gathered_ref.shape[1:]), gathered_ref.dtype)
    gathered_ref[pl.ds(gathered_ref.shape[0] - BATCH, BATCH)] = spare
    shape = stats_ref.shape[1:]
    at_row = lax.broadcasted_iota(jnp.int32, shape, 0)
    at_lane = lax.broadcasted_iota(jnp.int32, shape, 1)
    sizes = jnp.zeros(shape, jnp.int32)
    first = jnp.int32(0)
    for s in range(irreps):
        sizes = jnp.where((at_row == s) & (at_lane == 0), stop_ref[s] - first, sizes)
        first = stop_ref[s]
    stats_ref[0] = jnp.zeros(shape, jnp.float32)
    stats_ref[1] = sizes.astype(jnp.float32)
    pltpu.make_async_copy(res_ref, res_ref, blank_sem).wait()


def prepare(me, counts, irrep, depth, shard_tiles, rows, width):
    own_tiles = irrep.shape[0]
    irreps = counts.shape[0]
    columns = shard_tiles * depth * rows
    all_tiles = 4 * shard_tiles * depth
    most = (all_tiles // BATCH + irreps) * (own_tiles // BATCH) + UNROLL
    smem = pl.BlockSpec(memory_space=pltpu.SMEM)
    vmem = pl.BlockSpec(memory_space=pltpu.VMEM)
    anywhere = pl.BlockSpec(memory_space=pl.ANY)
    return pl.pallas_call(
        functools.partial(prepare_kernel, depth, shard_tiles),
        out_shape=(
            jax.ShapeDtypeStruct((own_tiles, rows, columns), jnp.bfloat16),
            jax.ShapeDtypeStruct((all_tiles + BATCH, rows, width), jnp.bfloat16),
            jax.ShapeDtypeStruct((2, irreps, 128), jnp.float32),
            jax.ShapeDtypeStruct((own_tiles + BATCH,), jnp.int32),
            jax.ShapeDtypeStruct((irreps,), jnp.int32),
            jax.ShapeDtypeStruct((irreps,), jnp.int32),
            jax.ShapeDtypeStruct((depth,), jnp.int32),
            jax.ShapeDtypeStruct((depth * most,), jnp.int32),
        ),
        in_specs=[smem] * 3,
        out_specs=(anywhere, vmem, vmem, smem, smem, smem, smem, smem),
        scratch_shapes=[
            pltpu.VMEM((2, rows, columns), jnp.bfloat16),
            pltpu.SMEM((irreps,), jnp.int32),
            pltpu.SMEM((4 * depth,), jnp.int32),
            pltpu.SemaphoreType.DMA,
        ],
        compiler_params=pltpu.CompilerParams(
            vmem_limit_bytes=4 * all_tiles * rows * width + 4 * 1024 * 1024
        ),
        cost_estimate=pl.CostEstimate(
            flops=0, bytes_accessed=2 * own_tiles * rows * columns, transcendentals=0
        ),
        name="prepare",
    )(me, counts, irrep)


def ladder_kernel(
    call, depth, shard_tiles, layout,
    me_ref, counts_ref, order_ref, offset_ref, stop_ref, end_ref, item_ref,
    stats_in_ref, v_ref, res_in_ref, gathered_in_ref, *refs,
):
    del res_in_ref, gathered_in_ref
    fresh, refs = refs[:len(layout)], refs[len(layout):]
    res_hbm, gathered_ref, stats_ref, o_buf, acc_ref, a_sem, o_sem = refs
    rows, width = v_ref.shape[1:]
    side = BATCH * rows
    most = item_ref.shape[0] // depth

    me = me_ref[0]
    z, y, core = me // 4, me // 2 % 2, me % 2
    arrivals = []
    for source, (lag, other_y, other_core) in zip(fresh, layout):
        at = ring_position(lax.rem(ring_place(z, depth) - lag + depth, depth), depth)
        own_y = (1 - y) if other_y else y
        own_core = (1 - core) if other_core else core
        arrivals.append(pltpu.make_async_copy(
            source,
            gathered_ref.at[
                pl.ds(((at * 2 + own_y) * 2 + own_core) * shard_tiles, shard_tiles)
            ],
            a_sem.at[len(arrivals)],
        ))
    for arrival in arrivals:
        arrival.start()
    acc_ref[...] = jnp.zeros(acc_ref.shape, acc_ref.dtype)
    for arrival in arrivals:
        arrival.wait()

    col_at = lax.broadcasted_iota(jnp.int32, (1, side), 1)

    def item(n):
        word = item_ref[n]
        slot, group, block = word & 255, (word >> 8) & 255, word >> 16
        return slot, group, block, jnp.minimum(stop_ref[group] - slot, BATCH)

    def multiply(n):
        slot, group, block, _ = item(n)
        left = jnp.concatenate([v_ref[order_ref[slot + t]] for t in range(BATCH)])
        right = gathered_ref[pl.ds(offset_ref[group] + block * BATCH, BATCH)].reshape(side, width)
        return lax.dot_general(
            left, right, (((1,), (1,)), ((), ())), preferred_element_type=jnp.float32
        )

    def keep(n, values):
        slot, group, block, members = item(n)
        limit = (counts_ref[group] - block * BATCH) * rows
        values = jnp.where(col_at < limit, values, 0.0).reshape(BATCH, rows, side)
        columns = pl.ds(pl.multiple_of(block * side, side), side)
        o_buf[pl.ds(slot, BATCH), :, columns] = values.astype(jnp.bfloat16)
        squares = jnp.sum((values * values).reshape(BATCH, rows // 8, 8, side), axis=1)
        total = jnp.zeros((8, side), jnp.float32)
        for t in range(BATCH):
            total = total + jnp.where(t < members, squares[t], 0.0)
        acc_ref[group] += total

    def send(n, started):
        slot, _, block, members = item(n)
        members = jnp.maximum(members, 0)
        columns = pl.ds(pl.multiple_of(block * side, side), side)

        def one(t, carry):
            pltpu.make_async_copy(
                o_buf.at[slot + t, :, columns],
                res_hbm.at[order_ref[slot + t], :, columns],
                o_sem,
            ).start()
            return carry

        lax.fori_loop(0, members, one, 0)
        return started + members

    def several(u, started):
        first = call * most + u * UNROLL
        values = multiply(first)
        for n in range(1, UNROLL):
            following = multiply(first + n)
            keep(first + n - 1, values)
            values = following
        keep(first + UNROLL - 1, values)
        for n in range(UNROLL):
            started = send(first + n, started)
        return started

    items = end_ref[call] - call * most
    started = lax.fori_loop(0, (items + UNROLL - 1) // UNROLL, several, jnp.int32(0))
    sums = jnp.sum(acc_ref[...], axis=1)
    sums = sum(sums[:, k:k + 128] for k in range(0, side, 128))
    stats_ref[0] = stats_in_ref[0] + sums
    stats_ref[1] = stats_in_ref[1]

    def finish(n, carry):
        pltpu.make_async_copy(
            o_buf.at[0, :, pl.ds(0, side)], res_hbm.at[0, :, pl.ds(0, side)], o_sem
        ).wait()
        return carry

    lax.fori_loop(0, started, finish, 0)


def ladder(call, depth, shard_tiles, integrals, listing, state, arrived):
    residual, gathered, stats = state
    layout, fresh = tuple(arrived), tuple(arrived.values())
    own_tiles, rows, width = integrals.shape
    slots = own_tiles + BATCH
    irreps = stats.shape[1]
    smem = pl.BlockSpec(memory_space=pltpu.SMEM)
    vmem = pl.BlockSpec(memory_space=pltpu.VMEM)
    anywhere = pl.BlockSpec(memory_space=pl.ANY)
    out_bytes = 2 * slots * residual[0].size
    tiles = sum(source.shape[0] for source in fresh)
    return pl.pallas_call(
        functools.partial(ladder_kernel, call, depth, shard_tiles, layout),
        out_shape=(
            jax.ShapeDtypeStruct(residual.shape, residual.dtype),
            jax.ShapeDtypeStruct(gathered.shape, gathered.dtype),
            jax.ShapeDtypeStruct(stats.shape, stats.dtype),
        ),
        in_specs=[smem] * 7 + [vmem] * 2 + [anywhere, vmem] + [anywhere] * len(fresh),
        out_specs=(anywhere, vmem, vmem),
        scratch_shapes=[
            pltpu.VMEM((slots, rows, residual.shape[2]), jnp.bfloat16),
            pltpu.VMEM((irreps, 8, BATCH * rows), jnp.float32),
            pltpu.SemaphoreType.DMA((len(fresh),)),
            pltpu.SemaphoreType.DMA,
        ],
        input_output_aliases={9: 0, 10: 1},
        compiler_params=pltpu.CompilerParams(
            vmem_limit_bytes=out_bytes + 2 * integrals.size + 4 * gathered.size + 6 * 1024 * 1024
        ),
        cost_estimate=pl.CostEstimate(
            flops=residual.size * width * tiles // (4 * shard_tiles * depth),
            bytes_accessed=2 * residual.size * tiles // (4 * shard_tiles * depth),
            transcendentals=0,
        ),
        name=f"ladder_{call}",
    )(*listing, stats, integrals, residual, gathered, *fresh)


def per_device(amplitudes, ij_counts, integrals, ab_irrep):
    shard_tiles, rows, width = amplitudes.shape
    devices = lax.axis_size("vir")
    depth = devices // 4
    me = lax.axis_index("vir").astype(jnp.int32).reshape(1)
    ring = ring_of(depth)
    hop = []
    for d in range(devices):
        following = ring[(ring.index(d // 4) + 1) % depth]
        hop.append((d, following * 4 + d % 4))

    def shift_z(x):
        return lax.ppermute(x, "vir", hop)

    def swap(x, bits):
        return lax.ppermute(x, "vir", [(d, d ^ bits) for d in range(devices)])

    residual, gathered, stats, *listing = prepare(
        me, ij_counts, ab_irrep, depth, shard_tiles, rows, width
    )
    listing = (me, ij_counts, *listing)
    state = (residual, gathered, stats)

    a, b, c, d = [amplitudes], [], [], []
    for k in range(depth):
        if k:
            c[-1], a[k], state = lax.optimization_barrier((c[-1], a[k], state))
        b.append(swap(a[k], 2))
        if k < depth - 1:
            a.append(shift_z(a[k]))
        c.append(swap(a[k], 1))
        if k == 0:
            continue
        d.append(swap(b[k - 1], 1))
        arrived = {(k, 0, 0): a[k], (k - 1, 1, 0): b[k - 1], (k - 1, 0, 1): c[k - 1]}
        if k == 1:
            arrived[0, 0, 0] = a[0]
        else:
            arrived[k - 2, 1, 1] = d[k - 2]
        if k == depth - 1:
            arrived[k, 0, 1], arrived[k - 1, 1, 1] = c[k], d[k - 1]
        state = ladder(k - 1, depth, shard_tiles, integrals, listing, state, arrived)
    last, state = lax.optimization_barrier((b[-1], state))
    residual, _, stats = ladder(
        depth - 1, depth, shard_tiles, integrals, listing, state,
        {(depth - 1, 1, 0): last, (depth - 1, 1, 1): swap(last, 1)},
    )

    stats = sum([swap(stats, bits) for bits in (1, 2, 3)], stats)
    stats = sum([swap(stats, 4 * bits) for bits in range(1, depth)], stats)
    irrep_sums, ab_counts = jnp.sum(stats, axis=2)
    entries = ab_counts * ij_counts.astype(jnp.float32) * float(rows * rows)
    return residual, jnp.sqrt(irrep_sums / entries + 1e-06)


def solution(mesh):
    in_specs = (
        P(("groups", "vir"), None, None),
        P("groups"),
        P(("groups", "vir"), None, None),
        P(("groups", "vir")),
    )
    out_specs = (P(("groups", "vir"), None, None), P("groups"))
    return jax.shard_map(
        per_device, mesh=mesh, in_specs=in_specs, out_specs=out_specs, check_vma=False
    )
```

```python
import functools

import jax
import jax.numpy as jnp
import numpy as np
from jax import lax
from jax.experimental import pallas as pl
from jax.experimental.pallas import tpu as pltpu
from jax.sharding import PartitionSpec as P

BATCH = 4
UNROLL = 4


def ring_of(depth):
    return [0, *range(1, depth, 2), *range(depth - 2 + depth % 2, 0, -2)]


def ring_place(z, depth):
    return jnp.where(z % 2 == 1, (z + 1) // 2, (depth - z // 2) % depth)


def ring_position(place, depth):
    return jnp.where(place <= depth // 2, jnp.maximum(2 * place - 1, 0), 2 * (depth - place))


def call_of(depth, lag, other_y, other_core):
    if other_y:
        return min(lag + other_core, depth - 1)
    return lag if other_core else max(lag - 1, 0)


def prepare_kernel(
    depth, shard_tiles,
    me_ref, counts_ref, irrep_ref,
    res_ref, gathered_ref, stats_ref, order_ref, offset_ref, stop_ref, end_ref, item_ref,
    blank_ref, next_ref, call_ref, blank_sem,
):
    own_tiles = irrep_ref.shape[0]
    irreps = counts_ref.shape[0]
    calls = end_ref.shape[0]
    most = item_ref.shape[0] // calls
    blank_ref[...] = jnp.zeros(blank_ref.shape, blank_ref.dtype)
    group = blank_ref.shape[0]
    for l in range(0, own_tiles, group):
        pltpu.make_async_copy(blank_ref, res_ref.at[pl.ds(l, group)], blank_sem).start()

    for s in range(irreps):
        stop_ref[s] = 0
    for t in range(BATCH):
        order_ref[own_tiles + t] = 0

    def count(l, carry):
        s = irrep_ref[l]
        stop_ref[s] = stop_ref[s] + 1
        return carry

    lax.fori_loop(0, own_tiles, count, 0)
    first, offset = jnp.int32(0), jnp.int32(0)
    for s in range(irreps):
        next_ref[s] = first
        first = first + stop_ref[s]
        stop_ref[s] = first
        offset_ref[s] = offset
        offset = offset + counts_ref[s]

    def place(l, carry):
        s = irrep_ref[l]
        slot = next_ref[s]
        next_ref[s] = slot + 1
        order_ref[slot] = l
        return carry

    lax.fori_loop(0, own_tiles, place, 0)

    me = me_ref[0]
    z, y, core = me // 4, me // 2 % 2, me % 2
    for lag in range(depth):
        at = ring_position(lax.rem(ring_place(z, depth) - lag + depth, depth), depth)
        for other_y, other_core in np.ndindex(2, 2):
            shard = (at * 2 + (1 - y if other_y else y)) * 2 + (1 - core if other_core else core)
            call_ref[shard] = call_of(depth, lag, other_y, other_core)

    for call in range(calls):
        end_ref[call] = call * most

    def symmetry(s, first):
        tiles, offset, stop = counts_ref[s], offset_ref[s], stop_ref[s]

        def block(j, carry):
            low = offset + j * BATCH
            high = offset + jnp.minimum(tiles, j * BATCH + BATCH) - 1
            call = jnp.maximum(call_ref[low // shard_tiles], call_ref[high // shard_tiles])
            word = (j * 256 + s) * 256 + first

            def batch(i, n):
                item_ref[n] = word + i * BATCH
                return n + 1

            end_ref[call] = lax.fori_loop(
                0, (stop - first + BATCH - 1) // BATCH, batch, end_ref[call]
            )
            return carry

        lax.fori_loop(0, (tiles + BATCH - 1) // BATCH, block, 0)
        return stop

    lax.fori_loop(0, irreps, symmetry, jnp.int32(0))
    for call in range(calls):
        end = end_ref[call]
        for spare in range(UNROLL - 1):
            item_ref[end + spare] = own_tiles

    spare = jnp.zeros((BATCH, *gathered_ref.shape[1:]), gathered_ref.dtype)
    gathered_ref[pl.ds(gathered_ref.shape[0] - BATCH, BATCH)] = spare
    shape = stats_ref.shape[1:]
    at_row = lax.broadcasted_iota(jnp.int32, shape, 0)
    at_lane = lax.broadcasted_iota(jnp.int32, shape, 1)
    sizes = jnp.zeros(shape, jnp.int32)
    first = jnp.int32(0)
    for s in range(irreps):
        sizes = jnp.where((at_row == s) & (at_lane == 0), stop_ref[s] - first, sizes)
        first = stop_ref[s]
    stats_ref[0] = jnp.zeros(shape, jnp.float32)
    stats_ref[1] = sizes.astype(jnp.float32)
    pltpu.make_async_copy(res_ref, res_ref, blank_sem).wait()


def prepare(me, counts, irrep, depth, shard_tiles, rows, width):
    own_tiles = irrep.shape[0]
    irreps = counts.shape[0]
    columns = shard_tiles * depth * rows
    all_tiles = 4 * shard_tiles * depth
    most = (all_tiles // BATCH + irreps) * (own_tiles // BATCH) + UNROLL
    smem = pl.BlockSpec(memory_space=pltpu.SMEM)
    vmem = pl.BlockSpec(memory_space=pltpu.VMEM)
    anywhere = pl.BlockSpec(memory_space=pl.ANY)
    return pl.pallas_call(
        functools.partial(prepare_kernel, depth, shard_tiles),
        out_shape=(
            jax.ShapeDtypeStruct((own_tiles, rows, columns), jnp.bfloat16),
            jax.ShapeDtypeStruct((all_tiles + BATCH, rows, width), jnp.bfloat16),
            jax.ShapeDtypeStruct((2, irreps, 128), jnp.float32),
            jax.ShapeDtypeStruct((own_tiles + BATCH,), jnp.int32),
            jax.ShapeDtypeStruct((irreps,), jnp.int32),
            jax.ShapeDtypeStruct((irreps,), jnp.int32),
            jax.ShapeDtypeStruct((depth,), jnp.int32),
            jax.ShapeDtypeStruct((depth * most,), jnp.int32),
        ),
        in_specs=[smem] * 3,
        out_specs=(anywhere, vmem, vmem, smem, smem, smem, smem, smem),
        scratch_shapes=[
            pltpu.VMEM((2, rows, columns), jnp.bfloat16),
            pltpu.SMEM((irreps,), jnp.int32),
            pltpu.SMEM((4 * depth,), jnp.int32),
            pltpu.SemaphoreType.DMA,
        ],
        compiler_params=pltpu.CompilerParams(
            vmem_limit_bytes=4 * all_tiles * rows * width + 4 * 1024 * 1024
        ),
        cost_estimate=pl.CostEstimate(
            flops=0, bytes_accessed=2 * own_tiles * rows * columns, transcendentals=0
        ),
        name="prepare",
    )(me, counts, irrep)


def ladder_kernel(
    call, depth, shard_tiles, layout,
    me_ref, counts_ref, order_ref, offset_ref, stop_ref, end_ref, item_ref,
    stats_in_ref, v_ref, res_in_ref, gathered_in_ref, *refs,
):
    del res_in_ref, gathered_in_ref
    fresh, refs = refs[:len(layout)], refs[len(layout):]
    res_hbm, gathered_ref, stats_ref, o_buf, acc_ref, a_sem, o_sem = refs
    rows, width = v_ref.shape[1:]
    side = BATCH * rows
    most = item_ref.shape[0] // end_ref.shape[0]

    me = me_ref[0]
    z, y, core = me // 4, me // 2 % 2, me % 2
    arrivals = []
    for source, (lag, other_y, other_core, tile) in zip(fresh, layout):
        at = ring_position(lax.rem(ring_place(z, depth) - lag + depth, depth), depth)
        own_y = (1 - y) if other_y else y
        own_core = (1 - core) if other_core else core
        arrivals.append(pltpu.make_async_copy(
            source,
            gathered_ref.at[pl.ds(
                ((at * 2 + own_y) * 2 + own_core) * shard_tiles + tile, source.shape[0]
            )],
            a_sem.at[len(arrivals)],
        ))
    for arrival in arrivals:
        arrival.start()
    acc_ref[...] = jnp.zeros(acc_ref.shape, acc_ref.dtype)
    for arrival in arrivals:
        arrival.wait()

    col_at = lax.broadcasted_iota(jnp.int32, (1, side), 1)

    def item(n):
        word = item_ref[n]
        slot, group, block = word & 255, (word >> 8) & 255, word >> 16
        return slot, group, block, jnp.minimum(stop_ref[group] - slot, BATCH)

    def multiply(n):
        slot, group, block, _ = item(n)
        left = jnp.concatenate([v_ref[order_ref[slot + t]] for t in range(BATCH)])
        right = gathered_ref[pl.ds(offset_ref[group] + block * BATCH, BATCH)].reshape(side, width)
        return lax.dot_general(
            left, right, (((1,), (1,)), ((), ())), preferred_element_type=jnp.float32
        )

    def keep(n, values):
        slot, group, block, members = item(n)
        limit = (counts_ref[group] - block * BATCH) * rows
        values = jnp.where(col_at < limit, values, 0.0).reshape(BATCH, rows, side)
        columns = pl.ds(pl.multiple_of(block * side, side), side)
        o_buf[pl.ds(slot, BATCH), :, columns] = values.astype(jnp.bfloat16)
        squares = jnp.sum((values * values).reshape(BATCH, rows // 8, 8, side), axis=1)
        total = jnp.zeros((8, side), jnp.float32)
        for t in range(BATCH):
            total = total + jnp.where(t < members, squares[t], 0.0)
        acc_ref[group] += total

    def send(n, started):
        slot, _, block, members = item(n)
        members = jnp.maximum(members, 0)
        columns = pl.ds(pl.multiple_of(block * side, side), side)

        def one(t, carry):
            pltpu.make_async_copy(
                o_buf.at[slot + t, :, columns],
                res_hbm.at[order_ref[slot + t], :, columns],
                o_sem,
            ).start()
            return carry

        lax.fori_loop(0, members, one, 0)
        return started + members

    def several(u, started):
        first = call * most + u * UNROLL
        values = multiply(first)
        for n in range(1, UNROLL):
            following = multiply(first + n)
            keep(first + n - 1, values)
            values = following
        keep(first + UNROLL - 1, values)
        for n in range(UNROLL):
            started = send(first + n, started)
        return started

    items = end_ref[call] - call * most
    started = lax.fori_loop(0, (items + UNROLL - 1) // UNROLL, several, jnp.int32(0))
    sums = jnp.sum(acc_ref[...], axis=1)
    sums = sum(sums[:, k:k + 128] for k in range(0, side, 128))
    stats_ref[0] = stats_in_ref[0] + sums
    stats_ref[1] = stats_in_ref[1]

    def finish(n, carry):
        pltpu.make_async_copy(
            o_buf.at[0, :, pl.ds(0, side)], res_hbm.at[0, :, pl.ds(0, side)], o_sem
        ).wait()
        return carry

    lax.fori_loop(0, started, finish, 0)


def ladder(call, depth, shard_tiles, integrals, listing, state, arrived):
    residual, gathered, stats = state
    layout, fresh = tuple(arrived), tuple(arrived.values())
    own_tiles, rows, width = integrals.shape
    slots = own_tiles + BATCH
    irreps = stats.shape[1]
    smem = pl.BlockSpec(memory_space=pltpu.SMEM)
    vmem = pl.BlockSpec(memory_space=pltpu.VMEM)
    anywhere = pl.BlockSpec(memory_space=pl.ANY)
    out_bytes = 2 * slots * residual[0].size
    tiles = sum(source.shape[0] for source in fresh)
    return pl.pallas_call(
        functools.partial(ladder_kernel, call, depth, shard_tiles, layout),
        out_shape=(
            jax.ShapeDtypeStruct(residual.shape, residual.dtype),
            jax.ShapeDtypeStruct(gathered.shape, gathered.dtype),
            jax.ShapeDtypeStruct(stats.shape, stats.dtype),
        ),
        in_specs=[smem] * 7 + [vmem] * 2 + [anywhere, vmem] + [anywhere] * len(fresh),
        out_specs=(anywhere, vmem, vmem),
        scratch_shapes=[
            pltpu.VMEM((slots, rows, residual.shape[2]), jnp.bfloat16),
            pltpu.VMEM((irreps, 8, BATCH * rows), jnp.float32),
            pltpu.SemaphoreType.DMA((len(fresh),)),
            pltpu.SemaphoreType.DMA,
        ],
        input_output_aliases={9: 0, 10: 1},
        compiler_params=pltpu.CompilerParams(
            vmem_limit_bytes=out_bytes + 2 * integrals.size + 4 * gathered.size + 6 * 1024 * 1024
        ),
        cost_estimate=pl.CostEstimate(
            flops=residual.size * width * tiles // (4 * shard_tiles * depth),
            bytes_accessed=2 * residual.size * tiles // (4 * shard_tiles * depth),
            transcendentals=0,
        ),
        name=f"ladder_{call}",
    )(*listing, stats, integrals, residual, gathered, *fresh)


def per_device(amplitudes, ij_counts, integrals, ab_irrep):
    shard_tiles, rows, width = amplitudes.shape
    devices = lax.axis_size("vir")
    depth = devices // 4
    me = lax.axis_index("vir").astype(jnp.int32).reshape(1)
    ring = ring_of(depth)

    def shift_z(x, by):
        pairs = []
        for d in range(devices):
            target = ring[(ring.index(d // 4) + by) % depth]
            pairs.append((d, target * 4 + d % 4))
        return lax.ppermute(x, "vir", pairs)

    def swap(x, bits):
        return lax.ppermute(x, "vir", [(d, d ^ bits) for d in range(devices)])

    residual, gathered, stats, *listing = prepare(
        me, ij_counts, ab_irrep, depth, shard_tiles, rows, width
    )
    listing = (me, ij_counts, *listing)
    state = (residual, gathered, stats)

    a, b, c, d = [amplitudes], [], [], []
    for k in range(depth):
        if 0 < k < depth - 1:
            c[-1], a[k], state = lax.optimization_barrier((c[-1], a[k], state))
        if k < depth - 1:
            b.append(swap(a[k], 2))
            a.append(shift_z(a[k], 1))
        else:
            part = 3 * shard_tiles // 8
            c[-1], a[k], back, state = lax.optimization_barrier(
                (c[-1], a[k], b[0][part:], state)
            )
            last = {part: shift_z(back, -1), 0: swap(a[k][:part], 2)}
        c.append(swap(a[k], 1))
        if k == 0:
            continue
        fresh = {(k, 0, 0, 0): a[k], (k - 1, 0, 1, 0): c[k - 1], (k - 1, 1, 0, 0): b[k - 1]}
        if k == 1:
            fresh[0, 0, 0, 0] = a[0]
        else:
            fresh[k - 2, 1, 1, 0] = d[k - 2]
        if k < depth - 1:
            d.append(swap(b[k - 1], 1))
        state = ladder(k - 1, depth, shard_tiles, integrals, listing, state, fresh)
    b[-1], last, state = lax.optimization_barrier((b[-1], last, state))
    fresh = {(k, 0, 1, 0): c[k], (k - 1, 1, 1, 0): swap(b[k - 1], 1)}
    for tile, piece in last.items():
        fresh[k, 1, 0, tile], fresh[k, 1, 1, tile] = piece, swap(piece, 1)
    residual, _, stats = ladder(k, depth, shard_tiles, integrals, listing, state, fresh)

    stats = sum([swap(stats, bits) for bits in (1, 2, 3)], stats)
    stats = sum([swap(stats, 4 * bits) for bits in range(1, depth)], stats)
    irrep_sums, ab_counts = jnp.sum(stats, axis=2)
    entries = ab_counts * ij_counts.astype(jnp.float32) * float(rows * rows)
    return residual, jnp.sqrt(irrep_sums / entries + 1e-06)


def solution(mesh):
    in_specs = (
        P(("groups", "vir"), None, None),
        P("groups"),
        P(("groups", "vir"), None, None),
        P(("groups", "vir")),
    )
    out_specs = (P(("groups", "vir"), None, None), P("groups"))
    return jax.shard_map(
        per_device, mesh=mesh, in_specs=in_specs, out_specs=out_specs, check_vma=False
    )
```

```python
import functools

import jax
import jax.numpy as jnp
import numpy as np
from jax import lax
from jax.experimental import pallas as pl
from jax.experimental.pallas import tpu as pltpu
from jax.sharding import PartitionSpec as P

BATCH = 4
UNROLL = 4
MUTE = 1 << 28


def ring_of(depth):
    return [0, *range(1, depth, 2), *range(depth - 2 + depth % 2, 0, -2)]


def ring_place(z, depth):
    return jnp.where(z % 2 == 1, (z + 1) // 2, (depth - z // 2) % depth)


def ring_position(place, depth):
    return jnp.where(place <= depth // 2, jnp.maximum(2 * place - 1, 0), 2 * (depth - place))


def call_of(depth, lag, other_y, other_core):
    if other_y:
        return min(lag + other_core, depth - 1)
    return lag if other_core else max(lag - 1, 0)


def prepare_kernel(
    depth, shard_tiles,
    me_ref, counts_ref, irrep_ref,
    res_ref, gathered_ref, stats_ref, order_ref, offset_ref, stop_ref, end_ref, item_ref,
    next_ref, call_ref,
):
    own_tiles = irrep_ref.shape[0]
    irreps = counts_ref.shape[0]
    calls = end_ref.shape[0]
    most = item_ref.shape[0] // calls
    for s in range(irreps):
        stop_ref[s] = 0

    def count(l, carry):
        s = irrep_ref[l]
        stop_ref[s] = stop_ref[s] + 1
        return carry

    lax.fori_loop(0, own_tiles, count, 0)
    first, offset = jnp.int32(0), jnp.int32(0)
    for s in range(irreps):
        next_ref[s] = first
        first = first + stop_ref[s]
        stop_ref[s] = first
        offset_ref[s] = offset
        offset = offset + counts_ref[s]

    def place(l, carry):
        s = irrep_ref[l]
        slot = next_ref[s]
        next_ref[s] = slot + 1
        order_ref[slot] = l
        return carry

    lax.fori_loop(0, own_tiles, place, 0)

    me = me_ref[0]
    z, y, core = me // 4, me // 2 % 2, me % 2
    for lag in range(depth):
        at = ring_position(lax.rem(ring_place(z, depth) - lag + depth, depth), depth)
        for other_y, other_core in np.ndindex(2, 2):
            shard = (at * 2 + (1 - y if other_y else y)) * 2 + (1 - core if other_core else core)
            call_ref[shard] = call_of(depth, lag, other_y, other_core)

    for call in range(calls):
        end_ref[call] = call * most

    def symmetry(s, first):
        tiles, offset, stop = counts_ref[s], offset_ref[s], stop_ref[s]

        def block(j, carry):
            low = offset + j * BATCH
            high = offset + jnp.minimum(tiles, j * BATCH + BATCH) - 1
            call = jnp.maximum(call_ref[low // shard_tiles], call_ref[high // shard_tiles])
            word = (j * 256 + s) * 256 + first

            def batch(i, n):
                item_ref[n] = word + i * BATCH
                return n + 1

            end_ref[call] = lax.fori_loop(
                0, (stop - first + BATCH - 1) // BATCH, batch, end_ref[call]
            )
            return carry

        lax.fori_loop(0, (tiles + BATCH - 1) // BATCH, block, 0)
        return stop

    lax.fori_loop(0, irreps, symmetry, jnp.int32(0))
    for call in range(calls):
        end = end_ref[call]
        for spare in range(UNROLL - 1):
            item_ref[end + spare] = item_ref[jnp.maximum(end - 1, 0)] | MUTE

    def blank(l, carry):
        res_ref[l] = jnp.zeros(res_ref.shape[1:], res_ref.dtype)
        return carry

    lax.fori_loop(0, own_tiles, blank, 0)
    spare = jnp.zeros((BATCH, *gathered_ref.shape[1:]), gathered_ref.dtype)
    gathered_ref[pl.ds(gathered_ref.shape[0] - BATCH, BATCH)] = spare
    shape = stats_ref.shape[1:]
    at_row = lax.broadcasted_iota(jnp.int32, shape, 0)
    at_lane = lax.broadcasted_iota(jnp.int32, shape, 1)
    sizes = jnp.zeros(shape, jnp.int32)
    first = jnp.int32(0)
    for s in range(irreps):
        sizes = jnp.where((at_row == s) & (at_lane == 0), stop_ref[s] - first, sizes)
        first = stop_ref[s]
    stats_ref[0] = jnp.zeros(shape, jnp.float32)
    stats_ref[1] = sizes.astype(jnp.float32)


def prepare(me, counts, irrep, depth, shard_tiles, rows, width):
    own_tiles = irrep.shape[0]
    irreps = counts.shape[0]
    columns = shard_tiles * depth * rows
    all_tiles = 4 * shard_tiles * depth
    most = (all_tiles // BATCH + irreps) * (own_tiles // BATCH) + UNROLL
    smem = pl.BlockSpec(memory_space=pltpu.SMEM)
    vmem = pl.BlockSpec(memory_space=pltpu.VMEM)
    return pl.pallas_call(
        functools.partial(prepare_kernel, depth, shard_tiles),
        out_shape=(
            jax.ShapeDtypeStruct((own_tiles, rows, columns), jnp.bfloat16),
            jax.ShapeDtypeStruct((all_tiles + BATCH, rows, width), jnp.bfloat16),
            jax.ShapeDtypeStruct((2, irreps, 128), jnp.float32),
            jax.ShapeDtypeStruct((own_tiles,), jnp.int32),
            jax.ShapeDtypeStruct((irreps,), jnp.int32),
            jax.ShapeDtypeStruct((irreps,), jnp.int32),
            jax.ShapeDtypeStruct((depth,), jnp.int32),
            jax.ShapeDtypeStruct((depth * most,), jnp.int32),
        ),
        in_specs=[smem] * 3,
        out_specs=(vmem, vmem, vmem, smem, smem, smem, smem, smem),
        scratch_shapes=[
            pltpu.SMEM((irreps,), jnp.int32),
            pltpu.SMEM((4 * depth,), jnp.int32),
        ],
        compiler_params=pltpu.CompilerParams(
            vmem_limit_bytes=2 * all_tiles * rows * width + 2 * own_tiles * rows * columns
            + 4 * 1024 * 1024
        ),
        cost_estimate=pl.CostEstimate(
            flops=0, bytes_accessed=2 * own_tiles * rows * columns, transcendentals=0
        ),
        name="prepare",
    )(me, counts, irrep)


def ladder_kernel(
    call, depth, shard_tiles, layout,
    me_ref, counts_ref, order_ref, offset_ref, stop_ref, end_ref, item_ref,
    stats_in_ref, v_ref, res_in_ref, gathered_in_ref, *refs,
):
    del res_in_ref, gathered_in_ref
    fresh, refs = refs[:len(layout)], refs[len(layout):]
    res_ref, gathered_ref, stats_ref, acc_ref, a_sem = refs
    rows, width = v_ref.shape[1:]
    side = BATCH * rows
    most = item_ref.shape[0] // end_ref.shape[0]

    me = me_ref[0]
    z, y, core = me // 4, me // 2 % 2, me % 2
    arrivals = []
    for source, (lag, other_y, other_core, tile) in zip(fresh, layout):
        at = ring_position(lax.rem(ring_place(z, depth) - lag + depth, depth), depth)
        own_y = (1 - y) if other_y else y
        own_core = (1 - core) if other_core else core
        arrivals.append(pltpu.make_async_copy(
            source,
            gathered_ref.at[pl.ds(
                ((at * 2 + own_y) * 2 + own_core) * shard_tiles + tile, source.shape[0]
            )],
            a_sem.at[len(arrivals)],
        ))
    for arrival in arrivals:
        arrival.start()
    acc_ref[...] = jnp.zeros(acc_ref.shape, acc_ref.dtype)
    for arrival in arrivals:
        arrival.wait()

    col_at = lax.broadcasted_iota(jnp.int32, (1, side), 1)

    def item(n):
        word = item_ref[n]
        slot, group, block = word & 255, (word >> 8) & 255, (word >> 16) & 255
        members = stop_ref[group] - slot
        tiles = [order_ref[slot + jnp.minimum(t, members - 1)] for t in range(BATCH)]
        return group, block, tiles, jnp.where(word >= MUTE, 0, members)

    def multiply(n):
        group, block, tiles, _ = item(n)
        left = jnp.concatenate([v_ref[tile] for tile in tiles])
        right = gathered_ref[pl.ds(offset_ref[group] + block * BATCH, BATCH)].reshape(side, width)
        return lax.dot_general(
            left, right, (((1,), (1,)), ((), ())), preferred_element_type=jnp.float32
        )

    def keep(n, values):
        group, block, tiles, members = item(n)
        limit = (counts_ref[group] - block * BATCH) * rows
        values = jnp.where(col_at < limit, values, 0.0).reshape(BATCH, rows, side)
        columns = pl.ds(pl.multiple_of(block * side, side), side)
        total = jnp.zeros((8, side), jnp.float32)
        for t in range(BATCH):
            res_ref[tiles[t], :, columns] = values[t].astype(jnp.bfloat16)
            squares = jnp.sum((values[t] * values[t]).reshape(rows // 8, 8, side), axis=0)
            total = total + jnp.where(t < members, squares, 0.0)
        acc_ref[group] += total

    def several(u, carry):
        first = call * most + u * UNROLL
        values = multiply(first)
        for n in range(1, UNROLL):
            following = multiply(first + n)
            keep(first + n - 1, values)
            values = following
        keep(first + UNROLL - 1, values)
        return carry

    items = end_ref[call] - call * most
    lax.fori_loop(0, (items + UNROLL - 1) // UNROLL, several, 0)
    sums = jnp.sum(acc_ref[...], axis=1)
    sums = sum(sums[:, k:k + 128] for k in range(0, side, 128))
    stats_ref[0] = stats_in_ref[0] + sums
    stats_ref[1] = stats_in_ref[1]


def ladder(call, depth, shard_tiles, integrals, listing, state, arrived):
    residual, gathered, stats = state
    layout, fresh = tuple(arrived), tuple(arrived.values())
    rows, width = integrals.shape[1:]
    irreps = stats.shape[1]
    smem = pl.BlockSpec(memory_space=pltpu.SMEM)
    vmem = pl.BlockSpec(memory_space=pltpu.VMEM)
    anywhere = pl.BlockSpec(memory_space=pl.ANY)
    tiles = sum(source.shape[0] for source in fresh)
    return pl.pallas_call(
        functools.partial(ladder_kernel, call, depth, shard_tiles, layout),
        out_shape=(
            jax.ShapeDtypeStruct(residual.shape, residual.dtype),
            jax.ShapeDtypeStruct(gathered.shape, gathered.dtype),
            jax.ShapeDtypeStruct(stats.shape, stats.dtype),
        ),
        in_specs=[smem] * 7 + [vmem] * 4 + [anywhere] * len(fresh),
        out_specs=(vmem, vmem, vmem),
        scratch_shapes=[
            pltpu.VMEM((irreps, 8, BATCH * rows), jnp.float32),
            pltpu.SemaphoreType.DMA((len(fresh),)),
        ],
        input_output_aliases={9: 0, 10: 1},
        compiler_params=pltpu.CompilerParams(
            vmem_limit_bytes=2 * (residual.size + integrals.size + gathered.size) + 6 * 1024 * 1024
        ),
        cost_estimate=pl.CostEstimate(
            flops=residual.size * width * tiles // (4 * shard_tiles * depth),
            bytes_accessed=2 * residual.size * tiles // (4 * shard_tiles * depth),
            transcendentals=0,
        ),
        name=f"ladder_{call}",
    )(*listing, stats, integrals, residual, gathered, *fresh)


def deliver_kernel(held_ref, out_ref, sem):
    copy = pltpu.make_async_copy(held_ref, out_ref, sem)
    copy.start()
    copy.wait()


def deliver(held):
    return pl.pallas_call(
        deliver_kernel,
        out_shape=jax.ShapeDtypeStruct(held.shape, held.dtype),
        in_specs=[pl.BlockSpec(memory_space=pltpu.VMEM)],
        out_specs=pl.BlockSpec(memory_space=pl.ANY),
        scratch_shapes=[pltpu.SemaphoreType.DMA],
        compiler_params=pltpu.CompilerParams(vmem_limit_bytes=2 * held.size + 1024 * 1024),
        name="deliver",
    )(held)


def per_device(amplitudes, ij_counts, integrals, ab_irrep):
    shard_tiles, rows, width = amplitudes.shape
    devices = lax.axis_size("vir")
    depth = devices // 4
    me = lax.axis_index("vir").astype(jnp.int32).reshape(1)
    ring = ring_of(depth)

    def shift_z(x, by):
        pairs = []
        for d in range(devices):
            target = ring[(ring.index(d // 4) + by) % depth]
            pairs.append((d, target * 4 + d % 4))
        return lax.ppermute(x, "vir", pairs)

    def swap(x, bits):
        return lax.ppermute(x, "vir", [(d, d ^ bits) for d in range(devices)])

    residual, gathered, stats, *listing = prepare(
        me, ij_counts, ab_irrep, depth, shard_tiles, rows, width
    )
    listing = (me, ij_counts, *listing)
    state = (residual, gathered, stats)

    a, b, c, d = [amplitudes], [], [], []
    for k in range(depth):
        if 0 < k < depth - 1:
            a[k], c[-1], state = lax.optimization_barrier((a[k], c[-1], state))
        if k < depth - 1:
            b.append(swap(a[k], 2))
            a.append(shift_z(a[k], 1))
        else:
            part = 3 * shard_tiles // 8
            c[-1], a[k], back, state = lax.optimization_barrier(
                (c[-1], a[k], b[0][part:], state)
            )
            last = {part: shift_z(back, -1), 0: swap(a[k][:part], 2)}
        c.append(swap(a[k], 1))
        if k == 0:
            continue
        fresh = {(k, 0, 0, 0): a[k], (k - 1, 1, 0, 0): b[k - 1], (k - 1, 0, 1, 0): c[k - 1]}
        if k == 1:
            fresh[0, 0, 0, 0] = a[0]
        else:
            fresh[k - 2, 1, 1, 0] = d[k - 2]
        if k < depth - 1:
            d.append(swap(b[k - 1], 1))
        state = ladder(k - 1, depth, shard_tiles, integrals, listing, state, fresh)
    b[-1], last, state = lax.optimization_barrier((b[-1], last, state))
    fresh = {(k, 0, 1, 0): c[k], (k - 1, 1, 1, 0): swap(b[k - 1], 1)}
    for tile, piece in last.items():
        fresh[k, 1, 0, tile], fresh[k, 1, 1, tile] = piece, swap(piece, 1)
    residual, _, stats = ladder(k, depth, shard_tiles, integrals, listing, state, fresh)

    stats = sum([swap(stats, bits) for bits in (1, 2, 3)], stats)
    stats = sum([swap(stats, 4 * bits) for bits in range(1, depth)], stats)
    irrep_sums, ab_counts = jnp.sum(stats, axis=2)
    entries = ab_counts * ij_counts.astype(jnp.float32) * float(rows * rows)
    return deliver(residual), jnp.sqrt(irrep_sums / entries + 1e-06)


def solution(mesh):
    in_specs = (
        P(("groups", "vir"), None, None),
        P("groups"),
        P(("groups", "vir"), None, None),
        P(("groups", "vir")),
    )
    out_specs = (P(("groups", "vir"), None, None), P("groups"))
    return jax.shard_map(
        per_device, mesh=mesh, in_specs=in_specs, out_specs=out_specs, check_vma=False
    )
```

```python
import functools

import jax
import jax.numpy as jnp
import numpy as np
from jax import lax
from jax.experimental import pallas as pl
from jax.experimental.pallas import tpu as pltpu
from jax.sharding import PartitionSpec as P

BATCH = 4
UNROLL = 4
MUTE = 1 << 28


def ring_of(depth):
    return [0, *range(1, depth, 2), *range(depth - 2 + depth % 2, 0, -2)]


def ring_place(z, depth):
    return jnp.where(z % 2 == 1, (z + 1) // 2, (depth - z // 2) % depth)


def ring_position(place, depth):
    return jnp.where(place <= depth // 2, jnp.maximum(2 * place - 1, 0), 2 * (depth - place))


def call_of(depth, lag, other_y, other_core):
    if other_y and other_core:
        return lag + 1 if lag < depth - 2 else depth
    return lag if other_y or other_core else max(lag - 1, 0)


def prepare_kernel(
    depth, shard_tiles,
    me_ref, counts_ref, irrep_ref,
    res_ref, gathered_ref, stats_ref, order_ref, offset_ref, stop_ref, end_ref, item_ref,
    next_ref, call_ref,
):
    own_tiles = irrep_ref.shape[0]
    irreps = counts_ref.shape[0]
    calls = end_ref.shape[0]
    most = item_ref.shape[0] // calls
    for s in range(irreps):
        stop_ref[s] = 0

    def count(l, carry):
        s = irrep_ref[l]
        stop_ref[s] = stop_ref[s] + 1
        return carry

    lax.fori_loop(0, own_tiles, count, 0)
    first, offset = jnp.int32(0), jnp.int32(0)
    for s in range(irreps):
        next_ref[s] = first
        first = first + stop_ref[s]
        stop_ref[s] = first
        offset_ref[s] = offset
        offset = offset + counts_ref[s]

    def place(l, carry):
        s = irrep_ref[l]
        slot = next_ref[s]
        next_ref[s] = slot + 1
        order_ref[slot] = l
        return carry

    lax.fori_loop(0, own_tiles, place, 0)

    me = me_ref[0]
    z, y, core = me // 4, me // 2 % 2, me % 2
    for lag in range(depth):
        at = ring_position(lax.rem(ring_place(z, depth) - lag + depth, depth), depth)
        for other_y, other_core in np.ndindex(2, 2):
            shard = (at * 2 + (1 - y if other_y else y)) * 2 + (1 - core if other_core else core)
            call_ref[shard] = call_of(depth, lag, other_y, other_core)

    for call in range(calls):
        end_ref[call] = call * most

    def symmetry(s, first):
        tiles, offset, stop = counts_ref[s], offset_ref[s], stop_ref[s]

        def block(j, carry):
            low = offset + j * BATCH
            high = offset + jnp.minimum(tiles, j * BATCH + BATCH) - 1
            call = jnp.maximum(call_ref[low // shard_tiles], call_ref[high // shard_tiles])
            word = (j * 256 + s) * 256 + first

            def batch(i, n):
                item_ref[n] = word + i * BATCH
                return n + 1

            end_ref[call] = lax.fori_loop(
                0, (stop - first + BATCH - 1) // BATCH, batch, end_ref[call]
            )
            return carry

        lax.fori_loop(0, (tiles + BATCH - 1) // BATCH, block, 0)
        return stop

    lax.fori_loop(0, irreps, symmetry, jnp.int32(0))
    for call in range(calls):
        end = end_ref[call]
        for spare in range(UNROLL - 1):
            item_ref[end + spare] = item_ref[jnp.maximum(end - 1, 0)] | MUTE

    def blank(l, carry):
        res_ref[l] = jnp.zeros(res_ref.shape[1:], res_ref.dtype)
        return carry

    lax.fori_loop(0, own_tiles, blank, 0)
    spare = jnp.zeros((BATCH, *gathered_ref.shape[1:]), gathered_ref.dtype)
    gathered_ref[pl.ds(gathered_ref.shape[0] - BATCH, BATCH)] = spare
    shape = stats_ref.shape[1:]
    at_row = lax.broadcasted_iota(jnp.int32, shape, 0)
    at_lane = lax.broadcasted_iota(jnp.int32, shape, 1)
    sizes = jnp.zeros(shape, jnp.int32)
    first = jnp.int32(0)
    for s in range(irreps):
        sizes = jnp.where((at_row == s) & (at_lane == 0), stop_ref[s] - first, sizes)
        first = stop_ref[s]
    stats_ref[0] = jnp.zeros(shape, jnp.float32)
    stats_ref[1] = sizes.astype(jnp.float32)


def prepare(me, counts, irrep, depth, shard_tiles, rows, width):
    own_tiles = irrep.shape[0]
    irreps = counts.shape[0]
    columns = shard_tiles * depth * rows
    all_tiles = 4 * shard_tiles * depth
    most = (all_tiles // BATCH + irreps) * (own_tiles // BATCH) + UNROLL
    smem = pl.BlockSpec(memory_space=pltpu.SMEM)
    vmem = pl.BlockSpec(memory_space=pltpu.VMEM)
    return pl.pallas_call(
        functools.partial(prepare_kernel, depth, shard_tiles),
        out_shape=(
            jax.ShapeDtypeStruct((own_tiles, rows, columns), jnp.bfloat16),
            jax.ShapeDtypeStruct((all_tiles + BATCH, rows, width), jnp.bfloat16),
            jax.ShapeDtypeStruct((2, irreps, 128), jnp.float32),
            jax.ShapeDtypeStruct((own_tiles,), jnp.int32),
            jax.ShapeDtypeStruct((irreps,), jnp.int32),
            jax.ShapeDtypeStruct((irreps,), jnp.int32),
            jax.ShapeDtypeStruct((depth + 1,), jnp.int32),
            jax.ShapeDtypeStruct(((depth + 1) * most,), jnp.int32),
        ),
        in_specs=[smem] * 3,
        out_specs=(vmem, vmem, vmem, smem, smem, smem, smem, smem),
        scratch_shapes=[
            pltpu.SMEM((irreps,), jnp.int32),
            pltpu.SMEM((4 * depth,), jnp.int32),
        ],
        compiler_params=pltpu.CompilerParams(
            vmem_limit_bytes=2 * all_tiles * rows * width + 2 * own_tiles * rows * columns
            + 4 * 1024 * 1024
        ),
        cost_estimate=pl.CostEstimate(
            flops=0, bytes_accessed=2 * own_tiles * rows * columns, transcendentals=0
        ),
        name="prepare",
    )(me, counts, irrep)


def ladder_kernel(
    call, depth, shard_tiles, layout,
    me_ref, counts_ref, order_ref, offset_ref, stop_ref, end_ref, item_ref,
    stats_in_ref, v_ref, res_in_ref, gathered_in_ref, *refs,
):
    del res_in_ref, gathered_in_ref
    fresh, refs = refs[:len(layout)], refs[len(layout):]
    res_ref, gathered_ref, stats_ref, acc_ref, a_sem = refs
    rows, width = v_ref.shape[1:]
    side = BATCH * rows
    most = item_ref.shape[0] // end_ref.shape[0]

    me = me_ref[0]
    z, y, core = me // 4, me // 2 % 2, me % 2
    arrivals = []
    for source, (lag, other_y, other_core, tile) in zip(fresh, layout):
        at = ring_position(lax.rem(ring_place(z, depth) - lag + depth, depth), depth)
        own_y = (1 - y) if other_y else y
        own_core = (1 - core) if other_core else core
        arrivals.append(pltpu.make_async_copy(
            source,
            gathered_ref.at[pl.ds(
                ((at * 2 + own_y) * 2 + own_core) * shard_tiles + tile, source.shape[0]
            )],
            a_sem.at[len(arrivals)],
        ))
    for arrival in arrivals:
        arrival.start()
    acc_ref[...] = jnp.zeros(acc_ref.shape, acc_ref.dtype)
    for arrival in arrivals:
        arrival.wait()

    col_at = lax.broadcasted_iota(jnp.int32, (1, side), 1)

    def item(n):
        word = item_ref[n]
        slot, group, block = word & 255, (word >> 8) & 255, (word >> 16) & 255
        members = stop_ref[group] - slot
        tiles = [order_ref[slot + jnp.minimum(t, members - 1)] for t in range(BATCH)]
        return group, block, tiles, jnp.where(word >= MUTE, 0, members)

    def multiply(n):
        group, block, tiles, _ = item(n)
        left = jnp.concatenate([v_ref[tile] for tile in tiles])
        right = gathered_ref[pl.ds(offset_ref[group] + block * BATCH, BATCH)].reshape(side, width)
        return lax.dot_general(
            left, right, (((1,), (1,)), ((), ())), preferred_element_type=jnp.float32
        )

    def keep(n, values):
        group, block, tiles, members = item(n)
        limit = (counts_ref[group] - block * BATCH) * rows
        values = jnp.where(col_at < limit, values, 0.0).reshape(BATCH, rows, side)
        columns = pl.ds(pl.multiple_of(block * side, side), side)
        total = jnp.zeros((8, side), jnp.float32)
        for t in range(BATCH):
            res_ref[tiles[t], :, columns] = values[t].astype(jnp.bfloat16)
            squares = jnp.sum((values[t] * values[t]).reshape(rows // 8, 8, side), axis=0)
            total = total + jnp.where(t < members, squares, 0.0)
        acc_ref[group] += total

    def several(u, carry):
        first = call * most + u * UNROLL
        values = multiply(first)
        for n in range(1, UNROLL):
            following = multiply(first + n)
            keep(first + n - 1, values)
            values = following
        keep(first + UNROLL - 1, values)
        return carry

    items = end_ref[call] - call * most
    lax.fori_loop(0, (items + UNROLL - 1) // UNROLL, several, 0)
    sums = jnp.sum(acc_ref[...], axis=1)
    sums = sum(sums[:, k:k + 128] for k in range(0, side, 128))
    stats_ref[0] = stats_in_ref[0] + sums
    stats_ref[1] = stats_in_ref[1]


def ladder(call, depth, shard_tiles, integrals, listing, state, arrived):
    residual, gathered, stats = state
    layout, fresh = tuple(arrived), tuple(arrived.values())
    rows, width = integrals.shape[1:]
    irreps = stats.shape[1]
    smem = pl.BlockSpec(memory_space=pltpu.SMEM)
    vmem = pl.BlockSpec(memory_space=pltpu.VMEM)
    anywhere = pl.BlockSpec(memory_space=pl.ANY)
    tiles = sum(source.shape[0] for source in fresh)
    return pl.pallas_call(
        functools.partial(ladder_kernel, call, depth, shard_tiles, layout),
        out_shape=(
            jax.ShapeDtypeStruct(residual.shape, residual.dtype),
            jax.ShapeDtypeStruct(gathered.shape, gathered.dtype),
            jax.ShapeDtypeStruct(stats.shape, stats.dtype),
        ),
        in_specs=[smem] * 7 + [vmem] * 4 + [anywhere] * len(fresh),
        out_specs=(vmem, vmem, vmem),
        scratch_shapes=[
            pltpu.VMEM((irreps, 8, BATCH * rows), jnp.float32),
            pltpu.SemaphoreType.DMA((len(fresh),)),
        ],
        input_output_aliases={9: 0, 10: 1},
        compiler_params=pltpu.CompilerParams(
            vmem_limit_bytes=2 * (residual.size + integrals.size + gathered.size) + 6 * 1024 * 1024
        ),
        cost_estimate=pl.CostEstimate(
            flops=residual.size * width * tiles // (4 * shard_tiles * depth),
            bytes_accessed=2 * residual.size * tiles // (4 * shard_tiles * depth),
            transcendentals=0,
        ),
        name=f"ladder_{call}",
    )(*listing, stats, integrals, residual, gathered, *fresh)


def deliver_kernel(part, held_ref, *refs):
    out_ref, sem = refs[-2:]
    tiles = held_ref.shape[0] // 2
    copy = pltpu.make_async_copy(
        held_ref.at[pl.ds(part * tiles, tiles)], out_ref.at[pl.ds(part * tiles, tiles)], sem
    )
    copy.start()
    copy.wait()


def deliver(held, part, *out):
    anywhere = pl.BlockSpec(memory_space=pl.ANY)
    return pl.pallas_call(
        functools.partial(deliver_kernel, part),
        out_shape=jax.ShapeDtypeStruct(held.shape, held.dtype),
        in_specs=[pl.BlockSpec(memory_space=pltpu.VMEM)] + [anywhere] * len(out),
        out_specs=anywhere,
        scratch_shapes=[pltpu.SemaphoreType.DMA],
        input_output_aliases={1: 0} if out else {},
        compiler_params=pltpu.CompilerParams(vmem_limit_bytes=2 * held.size + 1024 * 1024),
        name=f"deliver_{part}",
    )(held, *out)


def per_device(amplitudes, ij_counts, integrals, ab_irrep):
    shard_tiles, rows, width = amplitudes.shape
    devices = lax.axis_size("vir")
    depth = devices // 4
    me = lax.axis_index("vir").astype(jnp.int32).reshape(1)
    ring = ring_of(depth)

    def shift_z(x, by):
        pairs = []
        for d in range(devices):
            target = ring[(ring.index(d // 4) + by) % depth]
            pairs.append((d, target * 4 + d % 4))
        return lax.ppermute(x, "vir", pairs)

    def swap(x, bits):
        return lax.ppermute(x, "vir", [(d, d ^ bits) for d in range(devices)])

    residual, gathered, stats, *listing = prepare(
        me, ij_counts, ab_irrep, depth, shard_tiles, rows, width
    )
    listing = (me, ij_counts, *listing)
    state = (residual, gathered, stats)

    a, b, c, d = [amplitudes], [], [], []
    for k in range(depth):
        if 0 < k < depth - 1:
            a[k], c[-1], state = lax.optimization_barrier((a[k], c[-1], state))
        if k < depth - 1:
            b.append(swap(a[k], 2))
            a.append(shift_z(a[k], 1))
        else:
            part = 3 * shard_tiles // 8
            c[-1], a[k], back, state = lax.optimization_barrier(
                (c[-1], a[k], b[0][part:], state)
            )
            last = {part: shift_z(back, -1), 0: swap(a[k][:part], 2)}
        c.append(swap(a[k], 1))
        if k == 0:
            continue
        fresh = {(k, 0, 0, 0): a[k], (k - 1, 1, 0, 0): b[k - 1], (k - 1, 0, 1, 0): c[k - 1]}
        if k == 1:
            fresh[0, 0, 0, 0] = a[0]
        else:
            fresh[k - 2, 1, 1, 0] = d[k - 2]
        if k < depth - 1:
            d.append(swap(b[k - 1], 1))
        state = ladder(k - 1, depth, shard_tiles, integrals, listing, state, fresh)
    b[-1], last, state = lax.optimization_barrier((b[-1], last, state))
    first, second = {(k, 0, 1, 0): c[k]}, {(k - 1, 1, 1, 0): swap(b[k - 1], 1)}
    for tile, piece in last.items():
        first[k, 1, 0, tile], second[k, 1, 1, tile] = piece, swap(piece, 1)
    for number, fresh in ((k, first), (k + 1, second)):
        state = ladder(number, depth, shard_tiles, integrals, listing, state, fresh)

    residual, _, stats = state
    out = deliver(residual, 0)
    stats = sum([swap(stats, bits) for bits in (1, 2, 3)], stats)
    stats, residual, out = lax.optimization_barrier((stats, residual, out))
    out = deliver(residual, 1, out)
    stats = sum([swap(stats, 4 * bits) for bits in range(1, depth)], stats)
    irrep_sums, ab_counts = jnp.sum(stats, axis=2)
    entries = ab_counts * ij_counts.astype(jnp.float32) * float(rows * rows)
    return out, jnp.sqrt(irrep_sums / entries + 1e-06)


def solution(mesh):
    in_specs = (
        P(("groups", "vir"), None, None),
        P("groups"),
        P(("groups", "vir"), None, None),
        P(("groups", "vir")),
    )
    out_specs = (P(("groups", "vir"), None, None), P("groups"))
    return jax.shard_map(
        per_device, mesh=mesh, in_specs=in_specs, out_specs=out_specs, check_vma=False
    )
```

```python
import functools

import jax
import jax.numpy as jnp
import numpy as np
from jax import lax
from jax.experimental import pallas as pl
from jax.experimental.pallas import tpu as pltpu
from jax.sharding import PartitionSpec as P

BATCH = 4
UNROLL = 4
MUTE = 1 << 28


def ring_of(depth):
    return [0, *range(1, depth, 2), *range(depth - 2 + depth % 2, 0, -2)]


def ring_place(z, depth):
    return jnp.where(z % 2 == 1, (z + 1) // 2, (depth - z // 2) % depth)


def ring_position(place, depth):
    return jnp.where(place <= depth // 2, jnp.maximum(2 * place - 1, 0), 2 * (depth - place))


def call_of(depth, lag, other_y, other_core):
    if other_y:
        return depth if other_core and lag >= depth - 2 else lag + other_core
    return min(lag, depth - 2) if other_core else max(lag - 1, 0)


def prepare_kernel(
    depth, shard_tiles,
    me_ref, counts_ref, irrep_ref,
    res_ref, gathered_ref, stats_ref, order_ref, offset_ref, stop_ref, end_ref, item_ref,
    next_ref, call_ref,
):
    own_tiles = irrep_ref.shape[0]
    irreps = counts_ref.shape[0]
    calls = end_ref.shape[0]
    most = item_ref.shape[0] // calls
    for s in range(irreps):
        stop_ref[s] = 0

    def count(l, carry):
        s = irrep_ref[l]
        stop_ref[s] = stop_ref[s] + 1
        return carry

    lax.fori_loop(0, own_tiles, count, 0)
    first, offset = jnp.int32(0), jnp.int32(0)
    for s in range(irreps):
        next_ref[s] = first
        first = first + stop_ref[s]
        stop_ref[s] = first
        offset_ref[s] = offset
        offset = offset + counts_ref[s]

    def place(l, carry):
        s = irrep_ref[l]
        slot = next_ref[s]
        next_ref[s] = slot + 1
        order_ref[slot] = l
        return carry

    lax.fori_loop(0, own_tiles, place, 0)

    me = me_ref[0]
    z, y, core = me // 4, me // 2 % 2, me % 2
    for lag in range(depth):
        at = ring_position(lax.rem(ring_place(z, depth) - lag + depth, depth), depth)
        for other_y, other_core in np.ndindex(2, 2):
            shard = (at * 2 + (1 - y if other_y else y)) * 2 + (1 - core if other_core else core)
            call_ref[shard] = call_of(depth, lag, other_y, other_core)

    for call in range(calls):
        end_ref[call] = call * most

    def symmetry(s, first):
        tiles, offset, stop = counts_ref[s], offset_ref[s], stop_ref[s]

        def block(j, carry):
            low = offset + j * BATCH
            high = offset + jnp.minimum(tiles, j * BATCH + BATCH) - 1
            call = jnp.maximum(call_ref[low // shard_tiles], call_ref[high // shard_tiles])
            word = (j * 256 + s) * 256 + first

            def batch(i, n):
                item_ref[n] = word + i * BATCH
                return n + 1

            end_ref[call] = lax.fori_loop(
                0, (stop - first + BATCH - 1) // BATCH, batch, end_ref[call]
            )
            return carry

        lax.fori_loop(0, (tiles + BATCH - 1) // BATCH, block, 0)
        return stop

    lax.fori_loop(0, irreps, symmetry, jnp.int32(0))
    for call in range(calls):
        end = end_ref[call]
        for spare in range(UNROLL - 1):
            item_ref[end + spare] = item_ref[jnp.maximum(end - 1, 0)] | MUTE

    def blank(l, carry):
        res_ref[l] = jnp.zeros(res_ref.shape[1:], res_ref.dtype)
        return carry

    lax.fori_loop(0, own_tiles, blank, 0)
    spare = jnp.zeros((BATCH, *gathered_ref.shape[1:]), gathered_ref.dtype)
    gathered_ref[pl.ds(gathered_ref.shape[0] - BATCH, BATCH)] = spare
    shape = stats_ref.shape[1:]
    at_row = lax.broadcasted_iota(jnp.int32, shape, 0)
    at_lane = lax.broadcasted_iota(jnp.int32, shape, 1)
    sizes = jnp.zeros(shape, jnp.int32)
    first = jnp.int32(0)
    for s in range(irreps):
        sizes = jnp.where((at_row == s) & (at_lane == 0), stop_ref[s] - first, sizes)
        first = stop_ref[s]
    stats_ref[0] = jnp.zeros(shape, jnp.float32)
    stats_ref[1] = sizes.astype(jnp.float32)


def prepare(me, counts, irrep, depth, shard_tiles, rows, width):
    own_tiles = irrep.shape[0]
    irreps = counts.shape[0]
    columns = shard_tiles * depth * rows
    all_tiles = 4 * shard_tiles * depth
    most = (all_tiles // BATCH + irreps) * (own_tiles // BATCH) + UNROLL
    smem = pl.BlockSpec(memory_space=pltpu.SMEM)
    vmem = pl.BlockSpec(memory_space=pltpu.VMEM)
    return pl.pallas_call(
        functools.partial(prepare_kernel, depth, shard_tiles),
        out_shape=(
            jax.ShapeDtypeStruct((own_tiles, rows, columns), jnp.bfloat16),
            jax.ShapeDtypeStruct((all_tiles + BATCH, rows, width), jnp.bfloat16),
            jax.ShapeDtypeStruct((2, irreps, 128), jnp.float32),
            jax.ShapeDtypeStruct((own_tiles,), jnp.int32),
            jax.ShapeDtypeStruct((irreps,), jnp.int32),
            jax.ShapeDtypeStruct((irreps,), jnp.int32),
            jax.ShapeDtypeStruct((depth + 1,), jnp.int32),
            jax.ShapeDtypeStruct(((depth + 1) * most,), jnp.int32),
        ),
        in_specs=[smem] * 3,
        out_specs=(vmem, vmem, vmem, smem, smem, smem, smem, smem),
        scratch_shapes=[
            pltpu.SMEM((irreps,), jnp.int32),
            pltpu.SMEM((4 * depth,), jnp.int32),
        ],
        compiler_params=pltpu.CompilerParams(
            vmem_limit_bytes=2 * all_tiles * rows * width + 2 * own_tiles * rows * columns
            + 4 * 1024 * 1024
        ),
        cost_estimate=pl.CostEstimate(
            flops=0, bytes_accessed=2 * own_tiles * rows * columns, transcendentals=0
        ),
        name="prepare",
    )(me, counts, irrep)


def ladder_kernel(
    call, depth, shard_tiles, layout,
    me_ref, counts_ref, order_ref, offset_ref, stop_ref, end_ref, item_ref,
    stats_in_ref, v_ref, res_in_ref, gathered_in_ref, *refs,
):
    del res_in_ref, gathered_in_ref
    fresh, refs = refs[:len(layout)], refs[len(layout):]
    res_ref, gathered_ref, stats_ref, acc_ref, a_sem = refs
    rows, width = v_ref.shape[1:]
    side = BATCH * rows
    most = item_ref.shape[0] // end_ref.shape[0]

    me = me_ref[0]
    z, y, core = me // 4, me // 2 % 2, me % 2
    arrivals = []
    for source, (lag, other_y, other_core, tile) in zip(fresh, layout):
        at = ring_position(lax.rem(ring_place(z, depth) - lag + depth, depth), depth)
        own_y = (1 - y) if other_y else y
        own_core = (1 - core) if other_core else core
        arrivals.append(pltpu.make_async_copy(
            source,
            gathered_ref.at[pl.ds(
                ((at * 2 + own_y) * 2 + own_core) * shard_tiles + tile, source.shape[0]
            )],
            a_sem.at[len(arrivals)],
        ))
    for arrival in arrivals:
        arrival.start()
    acc_ref[...] = jnp.zeros(acc_ref.shape, acc_ref.dtype)
    for arrival in arrivals:
        arrival.wait()

    col_at = lax.broadcasted_iota(jnp.int32, (1, side), 1)

    def item(n):
        word = item_ref[n]
        slot, group, block = word & 255, (word >> 8) & 255, (word >> 16) & 255
        members = stop_ref[group] - slot
        tiles = [order_ref[slot + jnp.minimum(t, members - 1)] for t in range(BATCH)]
        return group, block, tiles, jnp.where(word >= MUTE, 0, members)

    def multiply(n):
        group, block, tiles, _ = item(n)
        left = jnp.concatenate([v_ref[tile] for tile in tiles])
        right = gathered_ref[pl.ds(offset_ref[group] + block * BATCH, BATCH)].reshape(side, width)
        return lax.dot_general(
            left, right, (((1,), (1,)), ((), ())), preferred_element_type=jnp.float32
        )

    def keep(n, values):
        group, block, tiles, members = item(n)
        limit = (counts_ref[group] - block * BATCH) * rows
        values = jnp.where(col_at < limit, values, 0.0).reshape(BATCH, rows, side)
        columns = pl.ds(pl.multiple_of(block * side, side), side)
        total = jnp.zeros((8, side), jnp.float32)
        for t in range(BATCH):
            res_ref[tiles[t], :, columns] = values[t].astype(jnp.bfloat16)
            squares = jnp.sum((values[t] * values[t]).reshape(rows // 8, 8, side), axis=0)
            total = total + jnp.where(t < members, squares, 0.0)
        acc_ref[group] += total

    def several(u, carry):
        first = call * most + u * UNROLL
        values = multiply(first)
        for n in range(1, UNROLL):
            following = multiply(first + n)
            keep(first + n - 1, values)
            values = following
        keep(first + UNROLL - 1, values)
        return carry

    items = end_ref[call] - call * most
    lax.fori_loop(0, (items + UNROLL - 1) // UNROLL, several, 0)
    sums = jnp.sum(acc_ref[...], axis=1)
    sums = sum(sums[:, k:k + 128] for k in range(0, side, 128))
    stats_ref[0] = stats_in_ref[0] + sums
    stats_ref[1] = stats_in_ref[1]


def ladder(call, depth, shard_tiles, integrals, listing, state, arrived):
    residual, gathered, stats = state
    layout, fresh = tuple(arrived), tuple(arrived.values())
    rows, width = integrals.shape[1:]
    irreps = stats.shape[1]
    smem = pl.BlockSpec(memory_space=pltpu.SMEM)
    vmem = pl.BlockSpec(memory_space=pltpu.VMEM)
    anywhere = pl.BlockSpec(memory_space=pl.ANY)
    tiles = sum(source.shape[0] for source in fresh)
    return pl.pallas_call(
        functools.partial(ladder_kernel, call, depth, shard_tiles, layout),
        out_shape=(
            jax.ShapeDtypeStruct(residual.shape, residual.dtype),
            jax.ShapeDtypeStruct(gathered.shape, gathered.dtype),
            jax.ShapeDtypeStruct(stats.shape, stats.dtype),
        ),
        in_specs=[smem] * 7 + [vmem] * 4 + [anywhere] * len(fresh),
        out_specs=(vmem, vmem, vmem),
        scratch_shapes=[
            pltpu.VMEM((irreps, 8, BATCH * rows), jnp.float32),
            pltpu.SemaphoreType.DMA((len(fresh),)),
        ],
        input_output_aliases={9: 0, 10: 1},
        compiler_params=pltpu.CompilerParams(
            vmem_limit_bytes=2 * (residual.size + integrals.size + gathered.size) + 6 * 1024 * 1024
        ),
        cost_estimate=pl.CostEstimate(
            flops=residual.size * width * tiles // (4 * shard_tiles * depth),
            bytes_accessed=2 * residual.size * tiles // (4 * shard_tiles * depth),
            transcendentals=0,
        ),
        name=f"ladder_{call}",
    )(*listing, stats, integrals, residual, gathered, *fresh)


def deliver_kernel(part, held_ref, *refs):
    out_ref, sem = refs[-2:]
    tiles = held_ref.shape[0] // 2
    copy = pltpu.make_async_copy(
        held_ref.at[pl.ds(part * tiles, tiles)], out_ref.at[pl.ds(part * tiles, tiles)], sem
    )
    copy.start()
    copy.wait()


def deliver(held, part, *out):
    anywhere = pl.BlockSpec(memory_space=pl.ANY)
    return pl.pallas_call(
        functools.partial(deliver_kernel, part),
        out_shape=jax.ShapeDtypeStruct(held.shape, held.dtype),
        in_specs=[pl.BlockSpec(memory_space=pltpu.VMEM)] + [anywhere] * len(out),
        out_specs=anywhere,
        scratch_shapes=[pltpu.SemaphoreType.DMA],
        input_output_aliases={1: 0} if out else {},
        compiler_params=pltpu.CompilerParams(vmem_limit_bytes=2 * held.size + 1024 * 1024),
        name=f"deliver_{part}",
    )(held, *out)


def per_device(amplitudes, ij_counts, integrals, ab_irrep):
    shard_tiles, rows, width = amplitudes.shape
    devices = lax.axis_size("vir")
    depth = devices // 4
    me = lax.axis_index("vir").astype(jnp.int32).reshape(1)
    ring = ring_of(depth)

    def shift_z(x, by):
        pairs = []
        for d in range(devices):
            target = ring[(ring.index(d // 4) + by) % depth]
            pairs.append((d, target * 4 + d % 4))
        return lax.ppermute(x, "vir", pairs)

    def swap(x, bits):
        return lax.ppermute(x, "vir", [(d, d ^ bits) for d in range(devices)])

    residual, gathered, stats, *listing = prepare(
        me, ij_counts, ab_irrep, depth, shard_tiles, rows, width
    )
    listing = (me, ij_counts, *listing)
    state = (residual, gathered, stats)

    a, b, c, d = [amplitudes], [], [], []
    for k in range(depth):
        if 0 < k < depth - 1:
            a[k], c[-1], state = lax.optimization_barrier((a[k], c[-1], state))
        if k < depth - 1:
            b.append(swap(a[k], 2))
            a.append(shift_z(a[k], 1))
        else:
            part = shard_tiles // 2
            c[-1], a[k], back, state = lax.optimization_barrier(
                (c[-1], a[k], b[0][part:], state)
            )
            last = {part: shift_z(back, -1), 0: swap(a[k][:part], 2)}
        c.append(swap(a[k], 1))
        if k == 0:
            continue
        fresh = {(k, 0, 0, 0): a[k], (k - 1, 1, 0, 0): b[k - 1], (k - 1, 0, 1, 0): c[k - 1]}
        if k == 1:
            fresh[0, 0, 0, 0] = a[0]
        else:
            fresh[k - 2, 1, 1, 0] = d[k - 2]
        if k < depth - 1:
            d.append(swap(b[k - 1], 1))
        else:
            fresh[k, 0, 1, 0] = c[k]
        state = ladder(k - 1, depth, shard_tiles, integrals, listing, state, fresh)
    b[-1], last, state = lax.optimization_barrier((b[-1], last, state))
    first, second = {}, {(k - 1, 1, 1, 0): swap(b[k - 1], 1)}
    for tile, piece in last.items():
        first[k, 1, 0, tile], second[k, 1, 1, tile] = piece, swap(piece, 1)
    for number, fresh in ((k, first), (k + 1, second)):
        state = ladder(number, depth, shard_tiles, integrals, listing, state, fresh)

    residual, _, stats = state
    out = deliver(residual, 0)
    stats = sum([swap(stats, bits) for bits in (1, 2, 3)], stats)
    stats, residual, out = lax.optimization_barrier((stats, residual, out))
    out = deliver(residual, 1, out)
    stats = sum([swap(stats, 4 * bits) for bits in range(1, depth)], stats)
    irrep_sums, ab_counts = jnp.sum(stats, axis=2)
    entries = ab_counts * ij_counts.astype(jnp.float32) * float(rows * rows)
    return out, jnp.sqrt(irrep_sums / entries + 1e-06)


def solution(mesh):
    in_specs = (
        P(("groups", "vir"), None, None),
        P("groups"),
        P(("groups", "vir"), None, None),
        P(("groups", "vir")),
    )
    out_specs = (P(("groups", "vir"), None, None), P("groups"))
    return jax.shard_map(
        per_device, mesh=mesh, in_specs=in_specs, out_specs=out_specs, check_vma=False
    )
```

```python
import functools

import jax
import jax.numpy as jnp
import numpy as np
from jax import lax
from jax.experimental import pallas as pl
from jax.experimental.pallas import tpu as pltpu
from jax.sharding import PartitionSpec as P

BATCH = 4
UNROLL = 4
MUTE = 1 << 28


def ring_of(depth):
    return [0, *range(1, depth, 2), *range(depth - 2 + depth % 2, 0, -2)]


def ring_place(z, depth):
    return jnp.where(z % 2 == 1, (z + 1) // 2, (depth - z // 2) % depth)


def ring_position(place, depth):
    return jnp.where(place <= depth // 2, jnp.maximum(2 * place - 1, 0), 2 * (depth - place))


def call_of(depth, lag, other_y, other_core):
    if other_y:
        return lag + other_core
    return min(lag, depth - 2) if other_core else max(lag - 1, 0)


def prepare_kernel(
    depth, shard_tiles,
    me_ref, counts_ref, irrep_ref,
    res_ref, gathered_ref, stats_ref, order_ref, offset_ref, stop_ref, end_ref, item_ref,
    next_ref, call_ref,
):
    own_tiles = irrep_ref.shape[0]
    irreps = counts_ref.shape[0]
    calls = end_ref.shape[0]
    most = item_ref.shape[0] // calls
    for s in range(irreps):
        stop_ref[s] = 0

    def count(l, carry):
        s = irrep_ref[l]
        stop_ref[s] = stop_ref[s] + 1
        return carry

    lax.fori_loop(0, own_tiles, count, 0)
    first, offset = jnp.int32(0), jnp.int32(0)
    for s in range(irreps):
        next_ref[s] = first
        first = first + stop_ref[s]
        stop_ref[s] = first
        offset_ref[s] = offset
        offset = offset + counts_ref[s]

    def place(l, carry):
        s = irrep_ref[l]
        slot = next_ref[s]
        next_ref[s] = slot + 1
        order_ref[slot] = l
        return carry

    lax.fori_loop(0, own_tiles, place, 0)

    me = me_ref[0]
    z, y, core = me // 4, me // 2 % 2, me % 2
    for lag in range(depth):
        at = ring_position(lax.rem(ring_place(z, depth) - lag + depth, depth), depth)
        for other_y, other_core in np.ndindex(2, 2):
            shard = (at * 2 + (1 - y if other_y else y)) * 2 + (1 - core if other_core else core)
            call_ref[shard] = call_of(depth, lag, other_y, other_core)

    for call in range(calls):
        end_ref[call] = call * most

    def symmetry(s, first):
        tiles, offset, stop = counts_ref[s], offset_ref[s], stop_ref[s]

        def block(j, carry):
            low = offset + j * BATCH
            high = offset + jnp.minimum(tiles, j * BATCH + BATCH) - 1
            call = jnp.maximum(call_ref[low // shard_tiles], call_ref[high // shard_tiles])
            word = (j * 256 + s) * 256 + first

            def batch(i, n):
                item_ref[n] = word + i * BATCH
                return n + 1

            end_ref[call] = lax.fori_loop(
                0, (stop - first + BATCH - 1) // BATCH, batch, end_ref[call]
            )
            return carry

        lax.fori_loop(0, (tiles + BATCH - 1) // BATCH, block, 0)
        return stop

    lax.fori_loop(0, irreps, symmetry, jnp.int32(0))
    for call in range(calls):
        end = end_ref[call]
        for spare in range(UNROLL - 1):
            item_ref[end + spare] = item_ref[jnp.maximum(end - 1, 0)] | MUTE

    def blank(l, carry):
        res_ref[l] = jnp.zeros(res_ref.shape[1:], res_ref.dtype)
        return carry

    lax.fori_loop(0, own_tiles, blank, 0)
    spare = jnp.zeros((BATCH, *gathered_ref.shape[1:]), gathered_ref.dtype)
    gathered_ref[pl.ds(gathered_ref.shape[0] - BATCH, BATCH)] = spare
    shape = stats_ref.shape[1:]
    at_row = lax.broadcasted_iota(jnp.int32, shape, 0)
    at_lane = lax.broadcasted_iota(jnp.int32, shape, 1)
    sizes = jnp.zeros(shape, jnp.int32)
    first = jnp.int32(0)
    for s in range(irreps):
        sizes = jnp.where((at_row == s) & (at_lane == 0), stop_ref[s] - first, sizes)
        first = stop_ref[s]
    stats_ref[0] = jnp.zeros(shape, jnp.float32)
    stats_ref[1] = sizes.astype(jnp.float32)


def prepare(me, counts, irrep, depth, shard_tiles, rows, width):
    own_tiles = irrep.shape[0]
    irreps = counts.shape[0]
    columns = shard_tiles * depth * rows
    all_tiles = 4 * shard_tiles * depth
    most = (all_tiles // BATCH + irreps) * (own_tiles // BATCH) + UNROLL
    smem = pl.BlockSpec(memory_space=pltpu.SMEM)
    vmem = pl.BlockSpec(memory_space=pltpu.VMEM)
    return pl.pallas_call(
        functools.partial(prepare_kernel, depth, shard_tiles),
        out_shape=(
            jax.ShapeDtypeStruct((own_tiles, rows, columns), jnp.bfloat16),
            jax.ShapeDtypeStruct((all_tiles + BATCH, rows, width), jnp.bfloat16),
            jax.ShapeDtypeStruct((2, irreps, 128), jnp.float32),
            jax.ShapeDtypeStruct((own_tiles,), jnp.int32),
            jax.ShapeDtypeStruct((irreps,), jnp.int32),
            jax.ShapeDtypeStruct((irreps,), jnp.int32),
            jax.ShapeDtypeStruct((depth + 1,), jnp.int32),
            jax.ShapeDtypeStruct(((depth + 1) * most,), jnp.int32),
        ),
        in_specs=[smem] * 3,
        out_specs=(vmem, vmem, vmem, smem, smem, smem, smem, smem),
        scratch_shapes=[
            pltpu.SMEM((irreps,), jnp.int32),
            pltpu.SMEM((4 * depth,), jnp.int32),
        ],
        compiler_params=pltpu.CompilerParams(
            vmem_limit_bytes=2 * all_tiles * rows * width + 2 * own_tiles * rows * columns
            + 4 * 1024 * 1024
        ),
        cost_estimate=pl.CostEstimate(
            flops=0, bytes_accessed=2 * own_tiles * rows * columns, transcendentals=0
        ),
        name="prepare",
    )(me, counts, irrep)


def ladder_kernel(
    call, depth, shard_tiles, layout,
    me_ref, counts_ref, order_ref, offset_ref, stop_ref, end_ref, item_ref,
    stats_in_ref, v_ref, res_in_ref, gathered_in_ref, *refs,
):
    del res_in_ref, gathered_in_ref
    fresh, refs = refs[:len(layout)], refs[len(layout):]
    res_ref, gathered_ref, stats_ref, acc_ref, a_sem = refs
    rows, width = v_ref.shape[1:]
    side = BATCH * rows
    most = item_ref.shape[0] // end_ref.shape[0]

    me = me_ref[0]
    z, y, core = me // 4, me // 2 % 2, me % 2
    arrivals = []
    for source, (lag, other_y, other_core, tile) in zip(fresh, layout):
        at = ring_position(lax.rem(ring_place(z, depth) - lag + depth, depth), depth)
        own_y = (1 - y) if other_y else y
        own_core = (1 - core) if other_core else core
        arrivals.append(pltpu.make_async_copy(
            source,
            gathered_ref.at[pl.ds(
                ((at * 2 + own_y) * 2 + own_core) * shard_tiles + tile, source.shape[0]
            )],
            a_sem.at[len(arrivals)],
        ))
    for arrival in arrivals:
        arrival.start()
    acc_ref[...] = jnp.zeros(acc_ref.shape, acc_ref.dtype)
    for arrival in arrivals:
        arrival.wait()

    col_at = lax.broadcasted_iota(jnp.int32, (1, side), 1)

    def item(n):
        word = item_ref[n]
        slot, group, block = word & 255, (word >> 8) & 255, (word >> 16) & 255
        members = stop_ref[group] - slot
        tiles = [order_ref[slot + jnp.minimum(t, members - 1)] for t in range(BATCH)]
        return group, block, tiles, jnp.where(word >= MUTE, 0, members)

    def multiply(n):
        group, block, tiles, _ = item(n)
        left = jnp.concatenate([v_ref[tile] for tile in tiles])
        right = gathered_ref[pl.ds(offset_ref[group] + block * BATCH, BATCH)].reshape(side, width)
        return lax.dot_general(
            left, right, (((1,), (1,)), ((), ())), preferred_element_type=jnp.float32
        )

    def keep(n, values):
        group, block, tiles, members = item(n)
        limit = (counts_ref[group] - block * BATCH) * rows
        values = jnp.where(col_at < limit, values, 0.0).reshape(BATCH, rows, side)
        columns = pl.ds(pl.multiple_of(block * side, side), side)
        total = jnp.zeros((8, side), jnp.float32)
        for t in range(BATCH):
            res_ref[tiles[t], :, columns] = values[t].astype(jnp.bfloat16)
            squares = jnp.sum((values[t] * values[t]).reshape(rows // 8, 8, side), axis=0)
            total = total + jnp.where(t < members, squares, 0.0)
        acc_ref[group] += total

    def several(u, carry):
        first = call * most + u * UNROLL
        values = multiply(first)
        for n in range(1, UNROLL):
            following = multiply(first + n)
            keep(first + n - 1, values)
            values = following
        keep(first + UNROLL - 1, values)
        return carry

    items = end_ref[call] - call * most
    lax.fori_loop(0, (items + UNROLL - 1) // UNROLL, several, 0)
    sums = jnp.sum(acc_ref[...], axis=1)
    sums = sum(sums[:, k:k + 128] for k in range(0, side, 128))
    stats_ref[0] = stats_in_ref[0] + sums
    stats_ref[1] = stats_in_ref[1]


def ladder(call, depth, shard_tiles, integrals, listing, state, arrived):
    residual, gathered, stats = state
    layout, fresh = tuple(arrived), tuple(arrived.values())
    rows, width = integrals.shape[1:]
    irreps = stats.shape[1]
    smem = pl.BlockSpec(memory_space=pltpu.SMEM)
    vmem = pl.BlockSpec(memory_space=pltpu.VMEM)
    anywhere = pl.BlockSpec(memory_space=pl.ANY)
    tiles = sum(source.shape[0] for source in fresh)
    return pl.pallas_call(
        functools.partial(ladder_kernel, call, depth, shard_tiles, layout),
        out_shape=(
            jax.ShapeDtypeStruct(residual.shape, residual.dtype),
            jax.ShapeDtypeStruct(gathered.shape, gathered.dtype),
            jax.ShapeDtypeStruct(stats.shape, stats.dtype),
        ),
        in_specs=[smem] * 7 + [vmem] * 4 + [anywhere] * len(fresh),
        out_specs=(vmem, vmem, vmem),
        scratch_shapes=[
            pltpu.VMEM((irreps, 8, BATCH * rows), jnp.float32),
            pltpu.SemaphoreType.DMA((len(fresh),)),
        ],
        input_output_aliases={9: 0, 10: 1},
        compiler_params=pltpu.CompilerParams(
            vmem_limit_bytes=2 * (residual.size + integrals.size + gathered.size) + 6 * 1024 * 1024
        ),
        cost_estimate=pl.CostEstimate(
            flops=residual.size * width * tiles // (4 * shard_tiles * depth),
            bytes_accessed=2 * residual.size * tiles // (4 * shard_tiles * depth),
            transcendentals=0,
        ),
        name=f"ladder_{call}",
    )(*listing, stats, integrals, residual, gathered, *fresh)


def deliver_kernel(part, held_ref, *refs):
    out_ref, sem = refs[-2:]
    tiles = held_ref.shape[0] // 2
    copy = pltpu.make_async_copy(
        held_ref.at[pl.ds(part * tiles, tiles)], out_ref.at[pl.ds(part * tiles, tiles)], sem
    )
    copy.start()
    copy.wait()


def deliver(held, part, *out):
    anywhere = pl.BlockSpec(memory_space=pl.ANY)
    return pl.pallas_call(
        functools.partial(deliver_kernel, part),
        out_shape=jax.ShapeDtypeStruct(held.shape, held.dtype),
        in_specs=[pl.BlockSpec(memory_space=pltpu.VMEM)] + [anywhere] * len(out),
        out_specs=anywhere,
        scratch_shapes=[pltpu.SemaphoreType.DMA],
        input_output_aliases={1: 0} if out else {},
        compiler_params=pltpu.CompilerParams(vmem_limit_bytes=2 * held.size + 1024 * 1024),
        name=f"deliver_{part}",
    )(held, *out)


def per_device(amplitudes, ij_counts, integrals, ab_irrep):
    shard_tiles, rows, width = amplitudes.shape
    devices = lax.axis_size("vir")
    depth = devices // 4
    me = lax.axis_index("vir").astype(jnp.int32).reshape(1)
    ring = ring_of(depth)

    def shift_z(x, by):
        pairs = []
        for d in range(devices):
            target = ring[(ring.index(d // 4) + by) % depth]
            pairs.append((d, target * 4 + d % 4))
        return lax.ppermute(x, "vir", pairs)

    def swap(x, bits):
        return lax.ppermute(x, "vir", [(d, d ^ bits) for d in range(devices)])

    residual, gathered, stats, *listing = prepare(
        me, ij_counts, ab_irrep, depth, shard_tiles, rows, width
    )
    listing = (me, ij_counts, *listing)
    state = (residual, gathered, stats)

    a, b, c, d = [amplitudes], [], [], []
    for k in range(depth):
        if 0 < k < depth - 1:
            a[k], c[-1], state = lax.optimization_barrier((a[k], c[-1], state))
        if k < depth - 1:
            b.append(swap(a[k], 2))
            a.append(shift_z(a[k], 1))
        else:
            part = 3 * shard_tiles // 8
            c[-1], a[k], back, state = lax.optimization_barrier(
                (c[-1], a[k], b[0][part:], state)
            )
            last = {part: shift_z(back, -1), 0: swap(a[k][:part], 2)}
        c.append(swap(a[k], 1))
        if k == 0:
            continue
        fresh = {(k, 0, 0, 0): a[k], (k - 1, 1, 0, 0): b[k - 1], (k - 1, 0, 1, 0): c[k - 1]}
        if k == 1:
            fresh[0, 0, 0, 0] = a[0]
        else:
            fresh[k - 2, 1, 1, 0] = d[k - 2]
        if k < depth - 1:
            d.append(swap(b[k - 1], 1))
        else:
            fresh[k, 0, 1, 0] = c[k]
        state = ladder(k - 1, depth, shard_tiles, integrals, listing, state, fresh)
    b[-1], last[0], state = lax.optimization_barrier((b[-1], last[0], state))
    first, second = {(k - 1, 1, 1, 0): swap(b[-1], 1)}, {(k, 1, 1, 0): swap(last[0], 1)}
    last[part], state = lax.optimization_barrier((last[part], state))
    second[k, 1, 1, part] = swap(last[part], 1)
    for tile, piece in last.items():
        first[k, 1, 0, tile] = piece
    for number, fresh in ((k, first), (k + 1, second)):
        state = ladder(number, depth, shard_tiles, integrals, listing, state, fresh)

    residual, _, stats = state
    out = deliver(residual, 0)
    stats = sum([swap(stats, bits) for bits in (1, 2, 3)], stats)
    stats, residual, out = lax.optimization_barrier((stats, residual, out))
    out = deliver(residual, 1, out)
    stats = sum([swap(stats, 4 * bits) for bits in range(1, depth)], stats)
    irrep_sums, ab_counts = jnp.sum(stats, axis=2)
    entries = ab_counts * ij_counts.astype(jnp.float32) * float(rows * rows)
    return out, jnp.sqrt(irrep_sums / entries + 1e-06)


def solution(mesh):
    in_specs = (
        P(("groups", "vir"), None, None),
        P("groups"),
        P(("groups", "vir"), None, None),
        P(("groups", "vir")),
    )
    out_specs = (P(("groups", "vir"), None, None), P("groups"))
    return jax.shard_map(
        per_device, mesh=mesh, in_specs=in_specs, out_specs=out_specs, check_vma=False
    )
```

```python
import functools

import jax
import jax.numpy as jnp
import numpy as np
from jax import lax
from jax.experimental import pallas as pl
from jax.experimental.pallas import tpu as pltpu
from jax.sharding import PartitionSpec as P

BATCH = 4
UNROLL = 4
MUTE = 1 << 28


def ring_of(depth):
    return [0, *range(1, depth, 2), *range(depth - 2 + depth % 2, 0, -2)]


def ring_place(z, depth):
    return jnp.where(z % 2 == 1, (z + 1) // 2, (depth - z // 2) % depth)


def ring_position(place, depth):
    return jnp.where(place <= depth // 2, jnp.maximum(2 * place - 1, 0), 2 * (depth - place))


def call_of(depth, lag, other_y, other_core):
    if other_y:
        return lag + other_core
    return min(lag, depth - 2) if other_core else max(lag - 1, 0)


def prepare_kernel(
    depth, shard_tiles,
    me_ref, counts_ref, irrep_ref,
    res_ref, gathered_ref, stats_ref, order_ref, offset_ref, stop_ref, end_ref, item_ref, late_ref,
    next_ref, call_ref, last_ref,
):
    own_tiles = irrep_ref.shape[0]
    irreps = counts_ref.shape[0]
    calls = end_ref.shape[0]
    most = item_ref.shape[0] // calls
    for s in range(irreps):
        stop_ref[s] = 0
        last_ref[s] = 0

    def count(l, carry):
        s = irrep_ref[l]
        stop_ref[s] = stop_ref[s] + 1
        return carry

    lax.fori_loop(0, own_tiles, count, 0)
    first, offset = jnp.int32(0), jnp.int32(0)
    for s in range(irreps):
        next_ref[s] = first
        first = first + stop_ref[s]
        stop_ref[s] = first
        offset_ref[s] = offset
        offset = offset + counts_ref[s]

    def place(l, carry):
        s = irrep_ref[l]
        slot = next_ref[s]
        next_ref[s] = slot + 1
        order_ref[slot] = l
        return carry

    lax.fori_loop(0, own_tiles, place, 0)

    me = me_ref[0]
    z, y, core = me // 4, me // 2 % 2, me % 2
    for lag in range(depth):
        at = ring_position(lax.rem(ring_place(z, depth) - lag + depth, depth), depth)
        for other_y, other_core in np.ndindex(2, 2):
            shard = (at * 2 + (1 - y if other_y else y)) * 2 + (1 - core if other_core else core)
            call_ref[shard] = call_of(depth, lag, other_y, other_core)

    for call in range(calls):
        end_ref[call] = call * most

    def symmetry(s, first):
        tiles, offset, stop = counts_ref[s], offset_ref[s], stop_ref[s]

        def block(j, carry):
            low = offset + j * BATCH
            high = offset + jnp.minimum(tiles, j * BATCH + BATCH) - 1
            call = jnp.maximum(call_ref[low // shard_tiles], call_ref[high // shard_tiles])
            word = (j * 256 + s) * 256 + first
            last_ref[s] = jnp.maximum(last_ref[s], call)

            def batch(i, n):
                item_ref[n] = word + i * BATCH
                return n + 1

            end_ref[call] = lax.fori_loop(
                0, (stop - first + BATCH - 1) // BATCH, batch, end_ref[call]
            )
            return carry

        lax.fori_loop(0, (tiles + BATCH - 1) // BATCH, block, 0)
        return stop

    lax.fori_loop(0, irreps, symmetry, jnp.int32(0))
    for call in range(calls):
        end = end_ref[call]
        for spare in range(UNROLL - 1):
            item_ref[end + spare] = item_ref[jnp.maximum(end - 1, 0)] | MUTE

    def blank(l, carry):
        res_ref[l] = jnp.zeros(res_ref.shape[1:], res_ref.dtype)
        late_ref[l] = jnp.where(last_ref[irrep_ref[l]] >= depth - 1, 1, 0)
        return carry

    lax.fori_loop(0, own_tiles, blank, 0)
    spare = jnp.zeros((BATCH, *gathered_ref.shape[1:]), gathered_ref.dtype)
    gathered_ref[pl.ds(gathered_ref.shape[0] - BATCH, BATCH)] = spare
    shape = stats_ref.shape[1:]
    at_row = lax.broadcasted_iota(jnp.int32, shape, 0)
    at_lane = lax.broadcasted_iota(jnp.int32, shape, 1)
    sizes = jnp.zeros(shape, jnp.int32)
    first = jnp.int32(0)
    for s in range(irreps):
        sizes = jnp.where((at_row == s) & (at_lane == 0), stop_ref[s] - first, sizes)
        first = stop_ref[s]
    stats_ref[0] = jnp.zeros(shape, jnp.float32)
    stats_ref[1] = sizes.astype(jnp.float32)


def prepare(me, counts, irrep, depth, shard_tiles, rows, width):
    own_tiles = irrep.shape[0]
    irreps = counts.shape[0]
    columns = shard_tiles * depth * rows
    all_tiles = 4 * shard_tiles * depth
    most = (all_tiles // BATCH + irreps) * (own_tiles // BATCH) + UNROLL
    smem = pl.BlockSpec(memory_space=pltpu.SMEM)
    vmem = pl.BlockSpec(memory_space=pltpu.VMEM)
    return pl.pallas_call(
        functools.partial(prepare_kernel, depth, shard_tiles),
        out_shape=(
            jax.ShapeDtypeStruct((own_tiles, rows, columns), jnp.bfloat16),
            jax.ShapeDtypeStruct((all_tiles + BATCH, rows, width), jnp.bfloat16),
            jax.ShapeDtypeStruct((2, irreps, 128), jnp.float32),
            jax.ShapeDtypeStruct((own_tiles,), jnp.int32),
            jax.ShapeDtypeStruct((irreps,), jnp.int32),
            jax.ShapeDtypeStruct((irreps,), jnp.int32),
            jax.ShapeDtypeStruct((depth + 1,), jnp.int32),
            jax.ShapeDtypeStruct(((depth + 1) * most,), jnp.int32),
            jax.ShapeDtypeStruct((own_tiles,), jnp.int32),
        ),
        in_specs=[smem] * 3,
        out_specs=(vmem, vmem, vmem, smem, smem, smem, smem, smem, smem),
        scratch_shapes=[
            pltpu.SMEM((irreps,), jnp.int32),
            pltpu.SMEM((4 * depth,), jnp.int32),
            pltpu.SMEM((irreps,), jnp.int32),
        ],
        compiler_params=pltpu.CompilerParams(
            vmem_limit_bytes=2 * all_tiles * rows * width + 2 * own_tiles * rows * columns
            + 4 * 1024 * 1024
        ),
        cost_estimate=pl.CostEstimate(
            flops=0, bytes_accessed=2 * own_tiles * rows * columns, transcendentals=0
        ),
        name="prepare",
    )(me, counts, irrep)


def ladder_kernel(
    call, depth, shard_tiles, layout,
    me_ref, counts_ref, order_ref, offset_ref, stop_ref, end_ref, item_ref,
    stats_in_ref, v_ref, res_in_ref, gathered_in_ref, *refs,
):
    del res_in_ref, gathered_in_ref
    fresh, refs = refs[:len(layout)], refs[len(layout):]
    res_ref, gathered_ref, stats_ref, acc_ref, a_sem = refs
    rows, width = v_ref.shape[1:]
    side = BATCH * rows
    most = item_ref.shape[0] // end_ref.shape[0]

    me = me_ref[0]
    z, y, core = me // 4, me // 2 % 2, me % 2
    arrivals = []
    for source, (lag, other_y, other_core, tile) in zip(fresh, layout):
        at = ring_position(lax.rem(ring_place(z, depth) - lag + depth, depth), depth)
        own_y = (1 - y) if other_y else y
        own_core = (1 - core) if other_core else core
        arrivals.append(pltpu.make_async_copy(
            source,
            gathered_ref.at[pl.ds(
                ((at * 2 + own_y) * 2 + own_core) * shard_tiles + tile, source.shape[0]
            )],
            a_sem.at[len(arrivals)],
        ))
    for arrival in arrivals:
        arrival.start()
    acc_ref[...] = jnp.zeros(acc_ref.shape, acc_ref.dtype)
    for arrival in arrivals:
        arrival.wait()

    col_at = lax.broadcasted_iota(jnp.int32, (1, side), 1)

    def item(n):
        word = item_ref[n]
        slot, group, block = word & 255, (word >> 8) & 255, (word >> 16) & 255
        members = stop_ref[group] - slot
        tiles = [order_ref[slot + jnp.minimum(t, members - 1)] for t in range(BATCH)]
        return group, block, tiles, jnp.where(word >= MUTE, 0, members)

    def multiply(n):
        group, block, tiles, _ = item(n)
        left = jnp.concatenate([v_ref[tile] for tile in tiles])
        right = gathered_ref[pl.ds(offset_ref[group] + block * BATCH, BATCH)].reshape(side, width)
        return lax.dot_general(
            left, right, (((1,), (1,)), ((), ())), preferred_element_type=jnp.float32
        )

    def keep(n, values):
        group, block, tiles, members = item(n)
        limit = (counts_ref[group] - block * BATCH) * rows
        values = jnp.where(col_at < limit, values, 0.0).reshape(BATCH, rows, side)
        columns = pl.ds(pl.multiple_of(block * side, side), side)
        total = jnp.zeros((8, side), jnp.float32)
        for t in range(BATCH):
            res_ref[tiles[t], :, columns] = values[t].astype(jnp.bfloat16)
            squares = jnp.sum((values[t] * values[t]).reshape(rows // 8, 8, side), axis=0)
            total = total + jnp.where(t < members, squares, 0.0)
        acc_ref[group] += total

    def several(u, carry):
        first = call * most + u * UNROLL
        values = multiply(first)
        for n in range(1, UNROLL):
            following = multiply(first + n)
            keep(first + n - 1, values)
            values = following
        keep(first + UNROLL - 1, values)
        return carry

    items = end_ref[call] - call * most
    lax.fori_loop(0, (items + UNROLL - 1) // UNROLL, several, 0)
    sums = jnp.sum(acc_ref[...], axis=1)
    sums = sum(sums[:, k:k + 128] for k in range(0, side, 128))
    stats_ref[0] = stats_in_ref[0] + sums
    stats_ref[1] = stats_in_ref[1]


def ladder(call, depth, shard_tiles, integrals, listing, state, arrived):
    residual, gathered, stats = state
    layout, fresh = tuple(arrived), tuple(arrived.values())
    rows, width = integrals.shape[1:]
    irreps = stats.shape[1]
    smem = pl.BlockSpec(memory_space=pltpu.SMEM)
    vmem = pl.BlockSpec(memory_space=pltpu.VMEM)
    anywhere = pl.BlockSpec(memory_space=pl.ANY)
    tiles = sum(source.shape[0] for source in fresh)
    return pl.pallas_call(
        functools.partial(ladder_kernel, call, depth, shard_tiles, layout),
        out_shape=(
            jax.ShapeDtypeStruct(residual.shape, residual.dtype),
            jax.ShapeDtypeStruct(gathered.shape, gathered.dtype),
            jax.ShapeDtypeStruct(stats.shape, stats.dtype),
        ),
        in_specs=[smem] * 7 + [vmem] * 4 + [anywhere] * len(fresh),
        out_specs=(vmem, vmem, vmem),
        scratch_shapes=[
            pltpu.VMEM((irreps, 8, BATCH * rows), jnp.float32),
            pltpu.SemaphoreType.DMA((len(fresh),)),
        ],
        input_output_aliases={9: 0, 10: 1},
        compiler_params=pltpu.CompilerParams(
            vmem_limit_bytes=2 * (residual.size + integrals.size + gathered.size) + 6 * 1024 * 1024
        ),
        cost_estimate=pl.CostEstimate(
            flops=residual.size * width * tiles // (4 * shard_tiles * depth),
            bytes_accessed=2 * residual.size * tiles // (4 * shard_tiles * depth),
            transcendentals=0,
        ),
        name=f"ladder_{call}",
    )(*listing, stats, integrals, residual, gathered, *fresh)


def deliver_kernel(part, late_ref, held_ref, *refs):
    out_ref, sem = refs[-2:]

    def send(l, started):
        mine = late_ref[l] == part

        @pl.when(mine)
        def _():
            pltpu.make_async_copy(held_ref.at[l], out_ref.at[l], sem).start()

        return started + jnp.where(mine, 1, 0)

    def wait(n, carry):
        pltpu.make_async_copy(held_ref.at[0], out_ref.at[0], sem).wait()
        return carry

    lax.fori_loop(0, lax.fori_loop(0, held_ref.shape[0], send, 0), wait, 0)


def deliver(held, late, part, *out):
    anywhere = pl.BlockSpec(memory_space=pl.ANY)
    return pl.pallas_call(
        functools.partial(deliver_kernel, part),
        out_shape=jax.ShapeDtypeStruct(held.shape, held.dtype),
        in_specs=[pl.BlockSpec(memory_space=pltpu.SMEM), pl.BlockSpec(memory_space=pltpu.VMEM)]
        + [anywhere] * len(out),
        out_specs=anywhere,
        scratch_shapes=[pltpu.SemaphoreType.DMA],
        input_output_aliases={2: 0} if out else {},
        compiler_params=pltpu.CompilerParams(vmem_limit_bytes=2 * held.size + 1024 * 1024),
        name=f"deliver_{part}",
    )(late, held, *out)


def per_device(amplitudes, ij_counts, integrals, ab_irrep):
    shard_tiles, rows, width = amplitudes.shape
    devices = lax.axis_size("vir")
    depth = devices // 4
    me = lax.axis_index("vir").astype(jnp.int32).reshape(1)
    ring = ring_of(depth)

    def shift_z(x, by):
        pairs = []
        for d in range(devices):
            target = ring[(ring.index(d // 4) + by) % depth]
            pairs.append((d, target * 4 + d % 4))
        return lax.ppermute(x, "vir", pairs)

    def swap(x, bits):
        return lax.ppermute(x, "vir", [(d, d ^ bits) for d in range(devices)])

    residual, gathered, stats, *listing, late = prepare(
        me, ij_counts, ab_irrep, depth, shard_tiles, rows, width
    )
    listing = (me, ij_counts, *listing)
    state = (residual, gathered, stats)

    a, b, c, d = [amplitudes], [], [], []
    for k in range(depth):
        if 0 < k < depth - 1:
            a[k], c[-1], state = lax.optimization_barrier((a[k], c[-1], state))
        if k < depth - 1:
            b.append(swap(a[k], 2))
            a.append(shift_z(a[k], 1))
        else:
            part = 3 * shard_tiles // 8
            c[-1], a[k], back, state = lax.optimization_barrier(
                (c[-1], a[k], b[0][part:], state)
            )
            last = {part: shift_z(back, -1), 0: swap(a[k][:part], 2)}
        c.append(swap(a[k], 1))
        if k == 0:
            continue
        fresh = {(k, 0, 0, 0): a[k], (k - 1, 1, 0, 0): b[k - 1], (k - 1, 0, 1, 0): c[k - 1]}
        if k == 1:
            fresh[0, 0, 0, 0] = a[0]
        else:
            fresh[k - 2, 1, 1, 0] = d[k - 2]
        if k < depth - 1:
            d.append(swap(b[k - 1], 1))
        else:
            fresh[k, 0, 1, 0] = c[k]
        state = ladder(k - 1, depth, shard_tiles, integrals, listing, state, fresh)
    out = deliver(state[0], late, 0)
    b[-1], last[0], out, state = lax.optimization_barrier((b[-1], last[0], out, state))
    first, second = {(k - 1, 1, 1, 0): swap(b[-1], 1)}, {(k, 1, 1, 0): swap(last[0], 1)}
    last[part], state = lax.optimization_barrier((last[part], state))
    second[k, 1, 1, part] = swap(last[part], 1)
    for tile, piece in last.items():
        first[k, 1, 0, tile] = piece
    for number, fresh in ((k, first), (k + 1, second)):
        state = ladder(number, depth, shard_tiles, integrals, listing, state, fresh)

    residual, _, stats = state
    stats = sum([swap(stats, bits) for bits in (1, 2, 3)], stats)
    stats, residual, out = lax.optimization_barrier((stats, residual, out))
    out = deliver(residual, late, 1, out)
    stats = sum([swap(stats, 4 * bits) for bits in range(1, depth)], stats)
    irrep_sums, ab_counts = jnp.sum(stats, axis=2)
    entries = ab_counts * ij_counts.astype(jnp.float32) * float(rows * rows)
    return out, jnp.sqrt(irrep_sums / entries + 1e-06)


def solution(mesh):
    in_specs = (
        P(("groups", "vir"), None, None),
        P("groups"),
        P(("groups", "vir"), None, None),
        P(("groups", "vir")),
    )
    out_specs = (P(("groups", "vir"), None, None), P("groups"))
    return jax.shard_map(
        per_device, mesh=mesh, in_specs=in_specs, out_specs=out_specs, check_vma=False
    )
```

```python
import functools

import jax
import jax.numpy as jnp
import numpy as np
from jax import lax
from jax.experimental import pallas as pl
from jax.experimental.pallas import tpu as pltpu
from jax.sharding import PartitionSpec as P

BATCH = 4
UNROLL = 4
MUTE = 1 << 28


def ring_of(depth):
    return [0, *range(1, depth, 2), *range(depth - 2 + depth % 2, 0, -2)]


def ring_place(z, depth):
    return jnp.where(z % 2 == 1, (z + 1) // 2, (depth - z // 2) % depth)


def ring_position(place, depth):
    return jnp.where(place <= depth // 2, jnp.maximum(2 * place - 1, 0), 2 * (depth - place))


def call_of(depth, lag, other_y, other_core):
    if other_y:
        return lag + other_core
    return min(lag, depth - 2) if other_core else max(lag - 1, 0)


def prepare_kernel(
    depth, shard_tiles,
    me_ref, counts_ref, irrep_ref,
    res_ref, gathered_ref, stats_ref, order_ref, offset_ref, stop_ref, end_ref, item_ref,
    next_ref, call_ref,
):
    own_tiles = irrep_ref.shape[0]
    irreps = counts_ref.shape[0]
    calls = end_ref.shape[0]
    most = item_ref.shape[0] // calls
    for s in range(irreps):
        stop_ref[s] = 0

    def count(l, carry):
        s = irrep_ref[l]
        stop_ref[s] = stop_ref[s] + 1
        return carry

    lax.fori_loop(0, own_tiles, count, 0)
    first, offset = jnp.int32(0), jnp.int32(0)
    for s in range(irreps):
        next_ref[s] = first
        first = first + stop_ref[s]
        stop_ref[s] = first
        offset_ref[s] = offset
        offset = offset + counts_ref[s]

    def place(l, carry):
        s = irrep_ref[l]
        slot = next_ref[s]
        next_ref[s] = slot + 1
        order_ref[slot] = l
        return carry

    lax.fori_loop(0, own_tiles, place, 0)

    me = me_ref[0]
    z, y, core = me // 4, me // 2 % 2, me % 2
    for lag in range(depth):
        at = ring_position(lax.rem(ring_place(z, depth) - lag + depth, depth), depth)
        for other_y, other_core in np.ndindex(2, 2):
            shard = (at * 2 + (1 - y if other_y else y)) * 2 + (1 - core if other_core else core)
            call_ref[shard] = call_of(depth, lag, other_y, other_core)

    for call in range(calls):
        end_ref[call] = call * most

    def symmetry(s, first):
        tiles, offset, stop = counts_ref[s], offset_ref[s], stop_ref[s]

        def block(j, carry):
            low = offset + j * BATCH
            high = offset + jnp.minimum(tiles, j * BATCH + BATCH) - 1
            call = jnp.maximum(call_ref[low // shard_tiles], call_ref[high // shard_tiles])
            word = (j * 256 + s) * 256 + first

            def batch(i, n):
                item_ref[n] = word + i * BATCH
                return n + 1

            end_ref[call] = lax.fori_loop(
                0, (stop - first + BATCH - 1) // BATCH, batch, end_ref[call]
            )
            return carry

        lax.fori_loop(0, (tiles + BATCH - 1) // BATCH, block, 0)
        return stop

    lax.fori_loop(0, irreps, symmetry, jnp.int32(0))
    for call in range(calls):
        end = end_ref[call]
        for spare in range(UNROLL - 1):
            item_ref[end + spare] = item_ref[jnp.maximum(end - 1, 0)] | MUTE

    def blank(l, carry):
        res_ref[l] = jnp.zeros(res_ref.shape[1:], res_ref.dtype)
        return carry

    lax.fori_loop(0, own_tiles, blank, 0)
    spare = jnp.zeros((BATCH, *gathered_ref.shape[1:]), gathered_ref.dtype)
    gathered_ref[pl.ds(gathered_ref.shape[0] - BATCH, BATCH)] = spare
    shape = stats_ref.shape[1:]
    at_row = lax.broadcasted_iota(jnp.int32, shape, 0)
    at_lane = lax.broadcasted_iota(jnp.int32, shape, 1)
    sizes = jnp.zeros(shape, jnp.int32)
    first = jnp.int32(0)
    for s in range(irreps):
        sizes = jnp.where((at_row == s) & (at_lane == 0), stop_ref[s] - first, sizes)
        first = stop_ref[s]
    stats_ref[0] = jnp.zeros(shape, jnp.float32)
    stats_ref[1] = sizes.astype(jnp.float32)


def prepare(me, counts, irrep, depth, shard_tiles, rows, width):
    own_tiles = irrep.shape[0]
    irreps = counts.shape[0]
    columns = shard_tiles * depth * rows
    all_tiles = 4 * shard_tiles * depth
    most = (all_tiles // BATCH + irreps) * (own_tiles // BATCH) + UNROLL
    smem = pl.BlockSpec(memory_space=pltpu.SMEM)
    vmem = pl.BlockSpec(memory_space=pltpu.VMEM)
    return pl.pallas_call(
        functools.partial(prepare_kernel, depth, shard_tiles),
        out_shape=(
            jax.ShapeDtypeStruct((own_tiles, rows, columns), jnp.bfloat16),
            jax.ShapeDtypeStruct((all_tiles + BATCH, rows, width), jnp.bfloat16),
            jax.ShapeDtypeStruct((2, irreps, 128), jnp.float32),
            jax.ShapeDtypeStruct((own_tiles,), jnp.int32),
            jax.ShapeDtypeStruct((irreps,), jnp.int32),
            jax.ShapeDtypeStruct((irreps,), jnp.int32),
            jax.ShapeDtypeStruct((depth + 1,), jnp.int32),
            jax.ShapeDtypeStruct(((depth + 1) * most,), jnp.int32),
        ),
        in_specs=[smem] * 3,
        out_specs=(vmem, vmem, vmem, smem, smem, smem, smem, smem),
        scratch_shapes=[
            pltpu.SMEM((irreps,), jnp.int32),
            pltpu.SMEM((4 * depth,), jnp.int32),
        ],
        compiler_params=pltpu.CompilerParams(
            vmem_limit_bytes=2 * all_tiles * rows * width + 2 * own_tiles * rows * columns
            + 4 * 1024 * 1024
        ),
        cost_estimate=pl.CostEstimate(
            flops=0, bytes_accessed=2 * own_tiles * rows * columns, transcendentals=0
        ),
        name="prepare",
    )(me, counts, irrep)


def ladder_kernel(
    call, depth, shard_tiles, layout,
    me_ref, counts_ref, order_ref, offset_ref, stop_ref, end_ref, item_ref,
    stats_in_ref, v_ref, res_in_ref, gathered_in_ref, *refs,
):
    del res_in_ref, gathered_in_ref
    fresh, refs = refs[:len(layout)], refs[len(layout):]
    res_ref, gathered_ref, stats_ref, acc_ref, a_sem = refs
    rows, width = v_ref.shape[1:]
    side = BATCH * rows
    most = item_ref.shape[0] // end_ref.shape[0]

    me = me_ref[0]
    z, y, core = me // 4, me // 2 % 2, me % 2
    arrivals = []
    for source, (lag, other_y, other_core, tile) in zip(fresh, layout):
        at = ring_position(lax.rem(ring_place(z, depth) - lag + depth, depth), depth)
        own_y = (1 - y) if other_y else y
        own_core = (1 - core) if other_core else core
        arrivals.append(pltpu.make_async_copy(
            source,
            gathered_ref.at[pl.ds(
                ((at * 2 + own_y) * 2 + own_core) * shard_tiles + tile, source.shape[0]
            )],
            a_sem.at[len(arrivals)],
        ))
    for arrival in arrivals:
        arrival.start()
    acc_ref[...] = jnp.zeros(acc_ref.shape, acc_ref.dtype)
    for arrival in arrivals:
        arrival.wait()

    col_at = lax.broadcasted_iota(jnp.int32, (1, side), 1)

    def item(n):
        word = item_ref[n]
        slot, group, block = word & 255, (word >> 8) & 255, (word >> 16) & 255
        members = stop_ref[group] - slot
        tiles = [order_ref[slot + jnp.minimum(t, members - 1)] for t in range(BATCH)]
        return group, block, tiles, jnp.where(word >= MUTE, 0, members)

    def multiply(n):
        group, block, tiles, _ = item(n)
        left = jnp.concatenate([v_ref[tile] for tile in tiles])
        right = gathered_ref[pl.ds(offset_ref[group] + block * BATCH, BATCH)].reshape(side, width)
        return lax.dot_general(
            left, right, (((1,), (1,)), ((), ())), preferred_element_type=jnp.float32
        )

    def keep(n, values):
        group, block, tiles, members = item(n)
        limit = (counts_ref[group] - block * BATCH) * rows
        values = jnp.where(col_at < limit, values, 0.0).reshape(BATCH, rows, side)
        columns = pl.ds(pl.multiple_of(block * side, side), side)
        total = jnp.zeros((8, side), jnp.float32)
        for t in range(BATCH):
            res_ref[tiles[t], :, columns] = values[t].astype(jnp.bfloat16)
            squares = jnp.sum((values[t] * values[t]).reshape(rows // 8, 8, side), axis=0)
            total = total + jnp.where(t < members, squares, 0.0)
        acc_ref[group] += total

    def several(u, carry):
        first = call * most + u * UNROLL
        values = multiply(first)
        for n in range(1, UNROLL):
            following = multiply(first + n)
            keep(first + n - 1, values)
            values = following
        keep(first + UNROLL - 1, values)
        return carry

    items = end_ref[call] - call * most
    lax.fori_loop(0, (items + UNROLL - 1) // UNROLL, several, 0)
    sums = jnp.sum(acc_ref[...], axis=1)
    sums = sum(sums[:, k:k + 128] for k in range(0, side, 128))
    stats_ref[0] = stats_in_ref[0] + sums
    stats_ref[1] = stats_in_ref[1]


def ladder(call, depth, shard_tiles, integrals, listing, state, arrived):
    residual, gathered, stats = state
    layout, fresh = tuple(arrived), tuple(arrived.values())
    rows, width = integrals.shape[1:]
    irreps = stats.shape[1]
    smem = pl.BlockSpec(memory_space=pltpu.SMEM)
    vmem = pl.BlockSpec(memory_space=pltpu.VMEM)
    anywhere = pl.BlockSpec(memory_space=pl.ANY)
    tiles = sum(source.shape[0] for source in fresh)
    return pl.pallas_call(
        functools.partial(ladder_kernel, call, depth, shard_tiles, layout),
        out_shape=(
            jax.ShapeDtypeStruct(residual.shape, residual.dtype),
            jax.ShapeDtypeStruct(gathered.shape, gathered.dtype),
            jax.ShapeDtypeStruct(stats.shape, stats.dtype),
        ),
        in_specs=[smem] * 7 + [vmem] * 4 + [anywhere] * len(fresh),
        out_specs=(vmem, vmem, vmem),
        scratch_shapes=[
            pltpu.VMEM((irreps, 8, BATCH * rows), jnp.float32),
            pltpu.SemaphoreType.DMA((len(fresh),)),
        ],
        input_output_aliases={9: 0, 10: 1},
        compiler_params=pltpu.CompilerParams(
            vmem_limit_bytes=2 * (residual.size + integrals.size + gathered.size) + 6 * 1024 * 1024
        ),
        cost_estimate=pl.CostEstimate(
            flops=residual.size * width * tiles // (4 * shard_tiles * depth),
            bytes_accessed=2 * residual.size * tiles // (4 * shard_tiles * depth),
            transcendentals=0,
        ),
        name=f"ladder_{call}",
    )(*listing, stats, integrals, residual, gathered, *fresh)


def deliver_kernel(part, held_ref, *refs):
    out_ref, sem = refs[-2:]
    tiles = held_ref.shape[0] // 2 // sem.shape[0]
    copies = []
    for n in range(sem.shape[0]):
        at = pl.ds((part * sem.shape[0] + n) * tiles, tiles)
        copies.append(pltpu.make_async_copy(held_ref.at[at], out_ref.at[at], sem.at[n]))
        copies[-1].start()
    for copy in copies:
        copy.wait()


def deliver(held, part, *out):
    anywhere = pl.BlockSpec(memory_space=pl.ANY)
    return pl.pallas_call(
        functools.partial(deliver_kernel, part),
        out_shape=jax.ShapeDtypeStruct(held.shape, held.dtype),
        in_specs=[pl.BlockSpec(memory_space=pltpu.VMEM)] + [anywhere] * len(out),
        out_specs=anywhere,
        scratch_shapes=[pltpu.SemaphoreType.DMA((8,))],
        input_output_aliases={1: 0} if out else {},
        compiler_params=pltpu.CompilerParams(vmem_limit_bytes=2 * held.size + 1024 * 1024),
        name=f"deliver_{part}",
    )(held, *out)


def per_device(amplitudes, ij_counts, integrals, ab_irrep):
    shard_tiles, rows, width = amplitudes.shape
    devices = lax.axis_size("vir")
    depth = devices // 4
    me = lax.axis_index("vir").astype(jnp.int32).reshape(1)
    ring = ring_of(depth)

    def shift_z(x, by):
        pairs = []
        for d in range(devices):
            target = ring[(ring.index(d // 4) + by) % depth]
            pairs.append((d, target * 4 + d % 4))
        return lax.ppermute(x, "vir", pairs)

    def swap(x, bits):
        return lax.ppermute(x, "vir", [(d, d ^ bits) for d in range(devices)])

    residual, gathered, stats, *listing = prepare(
        me, ij_counts, ab_irrep, depth, shard_tiles, rows, width
    )
    listing = (me, ij_counts, *listing)
    state = (residual, gathered, stats)

    a, b, c, d = [amplitudes], [], [], []
    for k in range(depth):
        if 0 < k < depth - 1:
            a[k], c[-1], state = lax.optimization_barrier((a[k], c[-1], state))
        if k < depth - 1:
            b.append(swap(a[k], 2))
            a.append(shift_z(a[k], 1))
        else:
            part = shard_tiles // 2
            c[-1], a[k], back, state = lax.optimization_barrier(
                (c[-1], a[k], b[0][part:], state)
            )
            last = {part: shift_z(back, -1), 0: swap(a[k][:part], 2)}
        c.append(swap(a[k], 1))
        if k == 0:
            continue
        fresh = {(k, 0, 0, 0): a[k], (k - 1, 1, 0, 0): b[k - 1], (k - 1, 0, 1, 0): c[k - 1]}
        if k == 1:
            fresh[0, 0, 0, 0] = a[0]
        else:
            fresh[k - 2, 1, 1, 0] = d[k - 2]
        if k < depth - 1:
            d.append(swap(b[k - 1], 1))
        else:
            fresh[k, 0, 1, 0] = c[k]
        state = ladder(k - 1, depth, shard_tiles, integrals, listing, state, fresh)
    b[-1], last[0], state = lax.optimization_barrier((b[-1], last[0], state))
    first, second = {}, {(k, 1, 1, 0): swap(last[0], 1)}
    for tile in (0, part):
        first[k - 1, 1, 1, tile] = swap(b[-1][tile:tile + part], 1)
    last[part], state = lax.optimization_barrier((last[part], state))
    second[k, 1, 1, part] = swap(last[part], 1)
    for tile, piece in last.items():
        first[k, 1, 0, tile] = piece
    for number, fresh in ((k, first), (k + 1, second)):
        state = ladder(number, depth, shard_tiles, integrals, listing, state, fresh)

    residual, _, stats = state
    out = deliver(residual, 0)
    stats = sum([swap(stats, bits) for bits in (1, 2, 3)], stats)
    stats, residual, out = lax.optimization_barrier((stats, residual, out))
    out = deliver(residual, 1, out)
    stats = sum([swap(stats, 4 * bits) for bits in range(1, depth)], stats)
    irrep_sums, ab_counts = jnp.sum(stats, axis=2)
    entries = ab_counts * ij_counts.astype(jnp.float32) * float(rows * rows)
    return out, jnp.sqrt(irrep_sums / entries + 1e-06)


def solution(mesh):
    in_specs = (
        P(("groups", "vir"), None, None),
        P("groups"),
        P(("groups", "vir"), None, None),
        P(("groups", "vir")),
    )
    out_specs = (P(("groups", "vir"), None, None), P("groups"))
    return jax.shard_map(
        per_device, mesh=mesh, in_specs=in_specs, out_specs=out_specs, check_vma=False
    )
```

```python
import functools

import jax
import jax.numpy as jnp
import numpy as np
from jax import lax
from jax.experimental import pallas as pl
from jax.experimental.pallas import tpu as pltpu
from jax.sharding import PartitionSpec as P

BATCH = 4
UNROLL = 4
MUTE = 1 << 28


def ring_of(depth):
    return [0, *range(1, depth, 2), *range(depth - 2 + depth % 2, 0, -2)]


def ring_place(z, depth):
    return jnp.where(z % 2 == 1, (z + 1) // 2, (depth - z // 2) % depth)


def ring_position(place, depth):
    return jnp.where(place <= depth // 2, jnp.maximum(2 * place - 1, 0), 2 * (depth - place))


def call_of(depth, lag, other_y, other_core):
    if other_y:
        return lag + other_core
    return min(lag, depth - 2) if other_core else max(lag - 1, 0)


def prepare_kernel(
    depth, shard_tiles,
    me_ref, counts_ref, irrep_ref,
    res_ref, gathered_ref, stats_ref, order_ref, offset_ref, stop_ref, end_ref, item_ref,
    next_ref, call_ref,
):
    own_tiles = irrep_ref.shape[0]
    irreps = counts_ref.shape[0]
    calls = end_ref.shape[0]
    most = item_ref.shape[0] // calls
    for s in range(irreps):
        stop_ref[s] = 0

    def count(l, carry):
        s = irrep_ref[l]
        stop_ref[s] = stop_ref[s] + 1
        return carry

    lax.fori_loop(0, own_tiles, count, 0)
    first, offset = jnp.int32(0), jnp.int32(0)
    for s in range(irreps):
        next_ref[s] = first
        first = first + stop_ref[s]
        stop_ref[s] = first
        offset_ref[s] = offset
        offset = offset + counts_ref[s]

    def place(l, carry):
        s = irrep_ref[l]
        slot = next_ref[s]
        next_ref[s] = slot + 1
        order_ref[slot] = l
        return carry

    lax.fori_loop(0, own_tiles, place, 0)

    me = me_ref[0]
    z, y, core = me // 4, me // 2 % 2, me % 2
    for lag in range(depth):
        at = ring_position(lax.rem(ring_place(z, depth) - lag + depth, depth), depth)
        for other_y, other_core in np.ndindex(2, 2):
            shard = (at * 2 + (1 - y if other_y else y)) * 2 + (1 - core if other_core else core)
            call_ref[shard] = call_of(depth, lag, other_y, other_core)

    for call in range(calls):
        end_ref[call] = call * most

    def symmetry(s, first):
        tiles, offset, stop = counts_ref[s], offset_ref[s], stop_ref[s]

        def block(j, carry):
            low = offset + j * BATCH
            high = offset + jnp.minimum(tiles, j * BATCH + BATCH) - 1
            call = jnp.maximum(call_ref[low // shard_tiles], call_ref[high // shard_tiles])
            word = (j * 256 + s) * 256 + first

            def batch(i, n):
                item_ref[n] = word + i * BATCH
                return n + 1

            end_ref[call] = lax.fori_loop(
                0, (stop - first + BATCH - 1) // BATCH, batch, end_ref[call]
            )
            return carry

        lax.fori_loop(0, (tiles + BATCH - 1) // BATCH, block, 0)
        return stop

    lax.fori_loop(0, irreps, symmetry, jnp.int32(0))
    for call in range(calls):
        end = end_ref[call]
        for spare in range(UNROLL - 1):
            item_ref[end + spare] = item_ref[jnp.maximum(end - 1, 0)] | MUTE

    def blank(l, carry):
        res_ref[l] = jnp.zeros(res_ref.shape[1:], res_ref.dtype)
        return carry

    lax.fori_loop(0, own_tiles, blank, 0)
    spare = jnp.zeros((BATCH, *gathered_ref.shape[1:]), gathered_ref.dtype)
    gathered_ref[pl.ds(gathered_ref.shape[0] - BATCH, BATCH)] = spare
    shape = stats_ref.shape[1:]
    at_row = lax.broadcasted_iota(jnp.int32, shape, 0)
    at_lane = lax.broadcasted_iota(jnp.int32, shape, 1)
    sizes = jnp.zeros(shape, jnp.int32)
    first = jnp.int32(0)
    for s in range(irreps):
        sizes = jnp.where((at_row == s) & (at_lane == 0), stop_ref[s] - first, sizes)
        first = stop_ref[s]
    stats_ref[0] = jnp.zeros(shape, jnp.float32)
    stats_ref[1] = sizes.astype(jnp.float32)


def prepare(me, counts, irrep, depth, shard_tiles, rows, width):
    own_tiles = irrep.shape[0]
    irreps = counts.shape[0]
    columns = shard_tiles * depth * rows
    all_tiles = 4 * shard_tiles * depth
    most = (all_tiles // BATCH + irreps) * (own_tiles // BATCH) + UNROLL
    smem = pl.BlockSpec(memory_space=pltpu.SMEM)
    vmem = pl.BlockSpec(memory_space=pltpu.VMEM)
    return pl.pallas_call(
        functools.partial(prepare_kernel, depth, shard_tiles),
        out_shape=(
            jax.ShapeDtypeStruct((own_tiles, rows, columns), jnp.bfloat16),
            jax.ShapeDtypeStruct((all_tiles + BATCH, rows, width), jnp.bfloat16),
            jax.ShapeDtypeStruct((2, irreps, 128), jnp.float32),
            jax.ShapeDtypeStruct((own_tiles,), jnp.int32),
            jax.ShapeDtypeStruct((irreps,), jnp.int32),
            jax.ShapeDtypeStruct((irreps,), jnp.int32),
            jax.ShapeDtypeStruct((depth + 1,), jnp.int32),
            jax.ShapeDtypeStruct(((depth + 1) * most,), jnp.int32),
        ),
        in_specs=[smem] * 3,
        out_specs=(vmem, vmem, vmem, smem, smem, smem, smem, smem),
        scratch_shapes=[
            pltpu.SMEM((irreps,), jnp.int32),
            pltpu.SMEM((4 * depth,), jnp.int32),
        ],
        compiler_params=pltpu.CompilerParams(
            vmem_limit_bytes=2 * all_tiles * rows * width + 2 * own_tiles * rows * columns
            + 4 * 1024 * 1024
        ),
        cost_estimate=pl.CostEstimate(
            flops=0, bytes_accessed=2 * own_tiles * rows * columns, transcendentals=0
        ),
        name="prepare",
    )(me, counts, irrep)


def ladder_kernel(
    call, depth, shard_tiles, layout,
    me_ref, counts_ref, order_ref, offset_ref, stop_ref, end_ref, item_ref,
    stats_in_ref, v_ref, res_in_ref, gathered_in_ref, *refs,
):
    del res_in_ref, gathered_in_ref
    fresh, refs = refs[:len(layout)], refs[len(layout):]
    res_ref, gathered_ref, stats_ref, acc_ref, a_sem = refs
    rows, width = v_ref.shape[1:]
    side = BATCH * rows
    most = item_ref.shape[0] // end_ref.shape[0]

    me = me_ref[0]
    z, y, core = me // 4, me // 2 % 2, me % 2
    arrivals = []
    for source, (lag, other_y, other_core, tile) in zip(fresh, layout):
        at = ring_position(lax.rem(ring_place(z, depth) - lag + depth, depth), depth)
        own_y = (1 - y) if other_y else y
        own_core = (1 - core) if other_core else core
        arrivals.append(pltpu.make_async_copy(
            source,
            gathered_ref.at[pl.ds(
                ((at * 2 + own_y) * 2 + own_core) * shard_tiles + tile, source.shape[0]
            )],
            a_sem.at[len(arrivals)],
        ))
    for arrival in arrivals:
        arrival.start()
    acc_ref[...] = jnp.zeros(acc_ref.shape, acc_ref.dtype)
    for arrival in arrivals:
        arrival.wait()

    col_at = lax.broadcasted_iota(jnp.int32, (1, side), 1)

    def item(n):
        word = item_ref[n]
        slot, group, block = word & 255, (word >> 8) & 255, (word >> 16) & 255
        members = stop_ref[group] - slot
        tiles = [order_ref[slot + jnp.minimum(t, members - 1)] for t in range(BATCH)]
        return group, block, tiles, jnp.where(word >= MUTE, 0, members)

    def multiply(n):
        group, block, tiles, _ = item(n)
        left = jnp.concatenate([v_ref[tile] for tile in tiles])
        right = gathered_ref[pl.ds(offset_ref[group] + block * BATCH, BATCH)].reshape(side, width)
        return lax.dot_general(
            left, right, (((1,), (1,)), ((), ())), preferred_element_type=jnp.float32
        )

    def keep(n, values):
        group, block, tiles, members = item(n)
        limit = (counts_ref[group] - block * BATCH) * rows
        values = jnp.where(col_at < limit, values, 0.0).reshape(BATCH, rows, side)
        columns = pl.ds(pl.multiple_of(block * side, side), side)
        total = jnp.zeros((8, side), jnp.float32)
        for t in range(BATCH):
            res_ref[tiles[t], :, columns] = values[t].astype(jnp.bfloat16)
            squares = jnp.sum((values[t] * values[t]).reshape(rows // 8, 8, side), axis=0)
            total = total + jnp.where(t < members, squares, 0.0)
        acc_ref[group] += total

    def several(u, carry):
        first = call * most + u * UNROLL
        values = multiply(first)
        for n in range(1, UNROLL):
            following = multiply(first + n)
            keep(first + n - 1, values)
            values = following
        keep(first + UNROLL - 1, values)
        return carry

    items = end_ref[call] - call * most
    lax.fori_loop(0, (items + UNROLL - 1) // UNROLL, several, 0)
    sums = jnp.sum(acc_ref[...], axis=1)
    sums = sum(sums[:, k:k + 128] for k in range(0, side, 128))
    stats_ref[0] = stats_in_ref[0] + sums
    stats_ref[1] = stats_in_ref[1]


def ladder(call, depth, shard_tiles, integrals, listing, state, arrived):
    residual, gathered, stats = state
    layout, fresh = tuple(arrived), tuple(arrived.values())
    rows, width = integrals.shape[1:]
    irreps = stats.shape[1]
    smem = pl.BlockSpec(memory_space=pltpu.SMEM)
    vmem = pl.BlockSpec(memory_space=pltpu.VMEM)
    anywhere = pl.BlockSpec(memory_space=pl.ANY)
    tiles = sum(source.shape[0] for source in fresh)
    return pl.pallas_call(
        functools.partial(ladder_kernel, call, depth, shard_tiles, layout),
        out_shape=(
            jax.ShapeDtypeStruct(residual.shape, residual.dtype),
            jax.ShapeDtypeStruct(gathered.shape, gathered.dtype),
            jax.ShapeDtypeStruct(stats.shape, stats.dtype),
        ),
        in_specs=[smem] * 7 + [vmem] * 4 + [anywhere] * len(fresh),
        out_specs=(vmem, vmem, vmem),
        scratch_shapes=[
            pltpu.VMEM((irreps, 8, BATCH * rows), jnp.float32),
            pltpu.SemaphoreType.DMA((len(fresh),)),
        ],
        input_output_aliases={9: 0, 10: 1},
        compiler_params=pltpu.CompilerParams(
            vmem_limit_bytes=2 * (residual.size + integrals.size + gathered.size) + 6 * 1024 * 1024
        ),
        cost_estimate=pl.CostEstimate(
            flops=residual.size * width * tiles // (4 * shard_tiles * depth),
            bytes_accessed=2 * residual.size * tiles // (4 * shard_tiles * depth),
            transcendentals=0,
        ),
        name=f"ladder_{call}",
    )(*listing, stats, integrals, residual, gathered, *fresh)


def deliver_kernel(part, held_ref, *refs):
    out_ref, sem = refs[-2:]
    tiles = held_ref.shape[0] // 2
    copy = pltpu.make_async_copy(
        held_ref.at[pl.ds(part * tiles, tiles)], out_ref.at[pl.ds(part * tiles, tiles)], sem
    )
    copy.start()
    copy.wait()


def deliver(held, part, *out):
    anywhere = pl.BlockSpec(memory_space=pl.ANY)
    return pl.pallas_call(
        functools.partial(deliver_kernel, part),
        out_shape=jax.ShapeDtypeStruct(held.shape, held.dtype),
        in_specs=[pl.BlockSpec(memory_space=pltpu.VMEM)] + [anywhere] * len(out),
        out_specs=anywhere,
        scratch_shapes=[pltpu.SemaphoreType.DMA],
        input_output_aliases={1: 0} if out else {},
        compiler_params=pltpu.CompilerParams(vmem_limit_bytes=2 * held.size + 1024 * 1024),
        name=f"deliver_{part}",
    )(held, *out)


def per_device(amplitudes, ij_counts, integrals, ab_irrep):
    shard_tiles, rows, width = amplitudes.shape
    devices = lax.axis_size("vir")
    depth = devices // 4
    me = lax.axis_index("vir").astype(jnp.int32).reshape(1)
    ring = ring_of(depth)

    def shift_z(x, by):
        pairs = []
        for d in range(devices):
            target = ring[(ring.index(d // 4) + by) % depth]
            pairs.append((d, target * 4 + d % 4))
        return lax.ppermute(x, "vir", pairs)

    def swap(x, bits):
        return lax.ppermute(x, "vir", [(d, d ^ bits) for d in range(devices)])

    residual, gathered, stats, *listing = prepare(
        me, ij_counts, ab_irrep, depth, shard_tiles, rows, width
    )
    listing = (me, ij_counts, *listing)
    state = (residual, gathered, stats)

    a, b, c, d = [amplitudes], [], [], []
    for k in range(depth):
        if 0 < k < depth - 1:
            a[k], c[-1], state = lax.optimization_barrier((a[k], c[-1], state))
        if k < depth - 1:
            b.append(swap(a[k], 2))
            a.append(shift_z(a[k], 1))
        else:
            part = shard_tiles // 2
            c[-1], a[k], back, state = lax.optimization_barrier(
                (c[-1], a[k], b[0][part:], state)
            )
            last = {part: shift_z(back, -1), 0: swap(a[k][:part], 2)}
        c.append(swap(a[k], 1))
        if k == 0:
            continue
        fresh = {(k, 0, 0, 0): a[k], (k - 1, 1, 0, 0): b[k - 1], (k - 1, 0, 1, 0): c[k - 1]}
        if k == 1:
            fresh[0, 0, 0, 0] = a[0]
        else:
            fresh[k - 2, 1, 1, 0] = d[k - 2]
        if k < depth - 1:
            d.append(swap(b[k - 1], 1))
        else:
            fresh[k, 0, 1, 0] = c[k]
        state = ladder(k - 1, depth, shard_tiles, integrals, listing, state, fresh)
    b[-1], last[0], state = lax.optimization_barrier((b[-1], last[0], state))
    first, second = {}, {(k, 1, 1, 0): swap(last[0], 1)}
    for tile in (0, part):
        first[k - 1, 1, 1, tile] = swap(b[-1][tile:tile + part], 1)
    last[part], state = lax.optimization_barrier((last[part], state))
    second[k, 1, 1, part] = swap(last[part], 1)
    for tile, piece in last.items():
        first[k, 1, 0, tile] = piece
    for number, fresh in ((k, first), (k + 1, second)):
        state = ladder(number, depth, shard_tiles, integrals, listing, state, fresh)

    residual, _, stats = state
    out = deliver(residual, 0)
    stats = sum([swap(stats, bits) for bits in (3, 2, 1)], stats)
    stats, residual, out = lax.optimization_barrier((stats, residual, out))
    out = deliver(residual, 1, out)
    stats = sum([swap(stats, 4 * bits) for bits in range(depth - 1, 0, -1)], stats)
    irrep_sums, ab_counts = jnp.sum(stats, axis=2)
    entries = ab_counts * ij_counts.astype(jnp.float32) * float(rows * rows)
    return out, jnp.sqrt(irrep_sums / entries + 1e-06)


def solution(mesh):
    in_specs = (
        P(("groups", "vir"), None, None),
        P("groups"),
        P(("groups", "vir"), None, None),
        P(("groups", "vir")),
    )
    out_specs = (P(("groups", "vir"), None, None), P("groups"))
    return jax.shard_map(
        per_device, mesh=mesh, in_specs=in_specs, out_specs=out_specs, check_vma=False
    )
```

```python
import functools

import jax
import jax.numpy as jnp
import numpy as np
from jax import lax
from jax.experimental import pallas as pl
from jax.experimental.pallas import tpu as pltpu
from jax.sharding import PartitionSpec as P

BATCH = 4
UNROLL = 4
MUTE = 1 << 28


def ring_of(depth):
    return [0, *range(1, depth, 2), *range(depth - 2 + depth % 2, 0, -2)]


def ring_place(z, depth):
    return jnp.where(z % 2 == 1, (z + 1) // 2, (depth - z // 2) % depth)


def ring_position(place, depth):
    return jnp.where(place <= depth // 2, jnp.maximum(2 * place - 1, 0), 2 * (depth - place))


def call_of(depth, lag, other_y, other_core):
    if other_y:
        return lag + other_core
    return min(lag, depth - 2) if other_core else max(lag - 1, 0)


def prepare_kernel(
    depth, shard_tiles,
    me_ref, counts_ref, irrep_ref,
    res_ref, gathered_ref, stats_ref, order_ref, offset_ref, stop_ref, end_ref, item_ref,
    next_ref, call_ref,
):
    own_tiles = irrep_ref.shape[0]
    irreps = counts_ref.shape[0]
    calls = end_ref.shape[0]
    most = item_ref.shape[0] // calls
    for s in range(irreps):
        stop_ref[s] = 0

    def count(l, carry):
        s = irrep_ref[l]
        stop_ref[s] = stop_ref[s] + 1
        return carry

    lax.fori_loop(0, own_tiles, count, 0)
    first, offset = jnp.int32(0), jnp.int32(0)
    for s in range(irreps):
        next_ref[s] = first
        first = first + stop_ref[s]
        stop_ref[s] = first
        offset_ref[s] = offset
        offset = offset + counts_ref[s]

    def place(l, carry):
        s = irrep_ref[l]
        slot = next_ref[s]
        next_ref[s] = slot + 1
        order_ref[slot] = l
        return carry

    lax.fori_loop(0, own_tiles, place, 0)

    me = me_ref[0]
    z, y, core = me // 4, me // 2 % 2, me % 2
    for lag in range(depth):
        at = ring_position(lax.rem(ring_place(z, depth) - lag + depth, depth), depth)
        for other_y, other_core in np.ndindex(2, 2):
            shard = (at * 2 + (1 - y if other_y else y)) * 2 + (1 - core if other_core else core)
            call_ref[shard] = call_of(depth, lag, other_y, other_core)

    for call in range(calls):
        end_ref[call] = call * most

    def symmetry(s, first):
        tiles, offset, stop = counts_ref[s], offset_ref[s], stop_ref[s]

        def block(j, carry):
            low = offset + j * BATCH
            high = offset + jnp.minimum(tiles, j * BATCH + BATCH) - 1
            call = jnp.maximum(call_ref[low // shard_tiles], call_ref[high // shard_tiles])
            word = (j * 256 + s) * 256 + first

            def batch(i, n):
                item_ref[n] = word + i * BATCH
                return n + 1

            end_ref[call] = lax.fori_loop(
                0, (stop - first + BATCH - 1) // BATCH, batch, end_ref[call]
            )
            return carry

        lax.fori_loop(0, (tiles + BATCH - 1) // BATCH, block, 0)
        return stop

    lax.fori_loop(0, irreps, symmetry, jnp.int32(0))
    for call in range(calls):
        end = end_ref[call]
        for spare in range(UNROLL - 1):
            item_ref[end + spare] = item_ref[jnp.maximum(end - 1, 0)] | MUTE

    def blank(l, carry):
        res_ref[l] = jnp.zeros(res_ref.shape[1:], res_ref.dtype)
        return carry

    lax.fori_loop(0, own_tiles, blank, 0)
    spare = jnp.zeros((BATCH, *gathered_ref.shape[1:]), gathered_ref.dtype)
    gathered_ref[pl.ds(gathered_ref.shape[0] - BATCH, BATCH)] = spare
    shape = stats_ref.shape[1:]
    at_row = lax.broadcasted_iota(jnp.int32, shape, 0)
    at_lane = lax.broadcasted_iota(jnp.int32, shape, 1)
    sizes = jnp.zeros(shape, jnp.int32)
    first = jnp.int32(0)
    for s in range(irreps):
        sizes = jnp.where((at_row == s) & (at_lane == 0), stop_ref[s] - first, sizes)
        first = stop_ref[s]
    stats_ref[0] = jnp.zeros(shape, jnp.float32)
    stats_ref[1] = sizes.astype(jnp.float32)


def prepare(me, counts, irrep, depth, shard_tiles, rows, width):
    own_tiles = irrep.shape[0]
    irreps = counts.shape[0]
    columns = shard_tiles * depth * rows
    all_tiles = 4 * shard_tiles * depth
    most = (all_tiles // BATCH + irreps) * (own_tiles // BATCH) + UNROLL
    smem = pl.BlockSpec(memory_space=pltpu.SMEM)
    vmem = pl.BlockSpec(memory_space=pltpu.VMEM)
    return pl.pallas_call(
        functools.partial(prepare_kernel, depth, shard_tiles),
        out_shape=(
            jax.ShapeDtypeStruct((own_tiles, rows, columns), jnp.bfloat16),
            jax.ShapeDtypeStruct((all_tiles + BATCH, rows, width), jnp.bfloat16),
            jax.ShapeDtypeStruct((2, irreps, 128), jnp.float32),
            jax.ShapeDtypeStruct((own_tiles,), jnp.int32),
            jax.ShapeDtypeStruct((irreps,), jnp.int32),
            jax.ShapeDtypeStruct((irreps,), jnp.int32),
            jax.ShapeDtypeStruct((depth + 1,), jnp.int32),
            jax.ShapeDtypeStruct(((depth + 1) * most,), jnp.int32),
        ),
        in_specs=[smem] * 3,
        out_specs=(vmem, vmem, vmem, smem, smem, smem, smem, smem),
        scratch_shapes=[
            pltpu.SMEM((irreps,), jnp.int32),
            pltpu.SMEM((4 * depth,), jnp.int32),
        ],
        compiler_params=pltpu.CompilerParams(
            vmem_limit_bytes=2 * all_tiles * rows * width + 2 * own_tiles * rows * columns
            + 4 * 1024 * 1024
        ),
        cost_estimate=pl.CostEstimate(
            flops=0, bytes_accessed=2 * own_tiles * rows * columns, transcendentals=0
        ),
        name="prepare",
    )(me, counts, irrep)


def ladder_kernel(
    call, depth, shard_tiles, layout,
    me_ref, counts_ref, order_ref, offset_ref, stop_ref, end_ref, item_ref,
    stats_in_ref, v_ref, res_in_ref, gathered_in_ref, *refs,
):
    del res_in_ref, gathered_in_ref
    fresh, refs = refs[:len(layout)], refs[len(layout):]
    res_ref, gathered_ref, stats_ref, acc_ref, a_sem = refs
    rows, width = v_ref.shape[1:]
    side = BATCH * rows
    most = item_ref.shape[0] // end_ref.shape[0]

    me = me_ref[0]
    z, y, core = me // 4, me // 2 % 2, me % 2
    arrivals = []
    for source, (lag, other_y, other_core, tile) in zip(fresh, layout):
        at = ring_position(lax.rem(ring_place(z, depth) - lag + depth, depth), depth)
        own_y = (1 - y) if other_y else y
        own_core = (1 - core) if other_core else core
        arrivals.append(pltpu.make_async_copy(
            source,
            gathered_ref.at[pl.ds(
                ((at * 2 + own_y) * 2 + own_core) * shard_tiles + tile, source.shape[0]
            )],
            a_sem.at[len(arrivals)],
        ))
    for arrival in arrivals:
        arrival.start()
    acc_ref[...] = jnp.zeros(acc_ref.shape, acc_ref.dtype)
    for arrival in arrivals:
        arrival.wait()

    col_at = lax.broadcasted_iota(jnp.int32, (1, side), 1)

    def item(n):
        word = item_ref[n]
        slot, group, block = word & 255, (word >> 8) & 255, (word >> 16) & 255
        members = stop_ref[group] - slot
        tiles = [order_ref[slot + jnp.minimum(t, members - 1)] for t in range(BATCH)]
        return group, block, tiles, jnp.where(word >= MUTE, 0, members)

    def multiply(n):
        group, block, tiles, _ = item(n)
        left = jnp.concatenate([v_ref[tile] for tile in tiles])
        right = gathered_ref[pl.ds(offset_ref[group] + block * BATCH, BATCH)].reshape(side, width)
        return lax.dot_general(
            left, right, (((1,), (1,)), ((), ())), preferred_element_type=jnp.float32
        )

    def keep(n, values):
        group, block, tiles, members = item(n)
        limit = (counts_ref[group] - block * BATCH) * rows
        values = jnp.where(col_at < limit, values, 0.0).reshape(BATCH, rows, side)
        columns = pl.ds(pl.multiple_of(block * side, side), side)
        total = jnp.zeros((8, side), jnp.float32)
        for t in range(BATCH):
            res_ref[tiles[t], :, columns] = values[t].astype(jnp.bfloat16)
            squares = jnp.sum((values[t] * values[t]).reshape(rows // 8, 8, side), axis=0)
            total = total + jnp.where(t < members, squares, 0.0)
        acc_ref[group] += total

    def several(u, carry):
        first = call * most + u * UNROLL
        values = multiply(first)
        for n in range(1, UNROLL):
            following = multiply(first + n)
            keep(first + n - 1, values)
            values = following
        keep(first + UNROLL - 1, values)
        return carry

    items = end_ref[call] - call * most
    lax.fori_loop(0, (items + UNROLL - 1) // UNROLL, several, 0)
    sums = jnp.sum(acc_ref[...], axis=1)
    sums = sum(sums[:, k:k + 128] for k in range(0, side, 128))
    stats_ref[0] = stats_in_ref[0] + sums
    stats_ref[1] = stats_in_ref[1]


def ladder(call, depth, shard_tiles, integrals, listing, state, arrived):
    residual, gathered, stats = state
    layout, fresh = tuple(arrived), tuple(arrived.values())
    rows, width = integrals.shape[1:]
    irreps = stats.shape[1]
    smem = pl.BlockSpec(memory_space=pltpu.SMEM)
    vmem = pl.BlockSpec(memory_space=pltpu.VMEM)
    anywhere = pl.BlockSpec(memory_space=pl.ANY)
    tiles = sum(source.shape[0] for source in fresh)
    return pl.pallas_call(
        functools.partial(ladder_kernel, call, depth, shard_tiles, layout),
        out_shape=(
            jax.ShapeDtypeStruct(residual.shape, residual.dtype),
            jax.ShapeDtypeStruct(gathered.shape, gathered.dtype),
            jax.ShapeDtypeStruct(stats.shape, stats.dtype),
        ),
        in_specs=[smem] * 7 + [vmem] * 4 + [anywhere] * len(fresh),
        out_specs=(vmem, vmem, vmem),
        scratch_shapes=[
            pltpu.VMEM((irreps, 8, BATCH * rows), jnp.float32),
            pltpu.SemaphoreType.DMA((len(fresh),)),
        ],
        input_output_aliases={9: 0, 10: 1},
        compiler_params=pltpu.CompilerParams(
            vmem_limit_bytes=2 * (residual.size + integrals.size + gathered.size) + 6 * 1024 * 1024
        ),
        cost_estimate=pl.CostEstimate(
            flops=residual.size * width * tiles // (4 * shard_tiles * depth),
            bytes_accessed=2 * residual.size * tiles // (4 * shard_tiles * depth),
            transcendentals=0,
        ),
        name=f"ladder_{call}",
    )(*listing, stats, integrals, residual, gathered, *fresh)


def deliver_kernel(part, held_ref, *refs):
    out_ref, sem = refs[-2:]
    tiles = held_ref.shape[0] // 2
    copy = pltpu.make_async_copy(
        held_ref.at[pl.ds(part * tiles, tiles)], out_ref.at[pl.ds(part * tiles, tiles)], sem
    )
    copy.start()
    copy.wait()


def deliver(held, part, *out):
    anywhere = pl.BlockSpec(memory_space=pl.ANY)
    return pl.pallas_call(
        functools.partial(deliver_kernel, part),
        out_shape=jax.ShapeDtypeStruct(held.shape, held.dtype),
        in_specs=[pl.BlockSpec(memory_space=pltpu.VMEM)] + [anywhere] * len(out),
        out_specs=anywhere,
        scratch_shapes=[pltpu.SemaphoreType.DMA],
        input_output_aliases={1: 0} if out else {},
        compiler_params=pltpu.CompilerParams(vmem_limit_bytes=2 * held.size + 1024 * 1024),
        name=f"deliver_{part}",
    )(held, *out)


def per_device(amplitudes, ij_counts, integrals, ab_irrep):
    shard_tiles, rows, width = amplitudes.shape
    devices = lax.axis_size("vir")
    depth = devices // 4
    me = lax.axis_index("vir").astype(jnp.int32).reshape(1)
    ring = ring_of(depth)

    def shift_z(x, by):
        pairs = []
        for d in range(devices):
            target = ring[(ring.index(d // 4) + by) % depth]
            pairs.append((d, target * 4 + d % 4))
        return lax.ppermute(x, "vir", pairs)

    def swap(x, bits):
        return lax.ppermute(x, "vir", [(d, d ^ bits) for d in range(devices)])

    residual, gathered, stats, *listing = prepare(
        me, ij_counts, ab_irrep, depth, shard_tiles, rows, width
    )
    listing = (me, ij_counts, *listing)
    state = (residual, gathered, stats)

    a, b, c, d = [amplitudes], [], [], []
    for k in range(depth):
        if 0 < k < depth - 1:
            a[k], c[-1], state = lax.optimization_barrier((a[k], c[-1], state))
        if k < depth - 1:
            b.append(swap(a[k], 2))
            a.append(shift_z(a[k], 1))
        else:
            part = shard_tiles // 2
            a[k], c[-1], back, state = lax.optimization_barrier(
                (a[k], c[-1], b[0][part:], state)
            )
            last = {part: shift_z(back, -1), 0: swap(a[k][:part], 2)}
        c.append(swap(a[k], 1))
        if k == 0:
            continue
        fresh = {(k, 0, 0, 0): a[k], (k - 1, 1, 0, 0): b[k - 1], (k - 1, 0, 1, 0): c[k - 1]}
        if k == 1:
            fresh[0, 0, 0, 0] = a[0]
        else:
            fresh[k - 2, 1, 1, 0] = d[k - 2]
        if k < depth - 1:
            d.append(swap(b[k - 1], 1))
        else:
            fresh[k, 0, 1, 0] = c[k]
        state = ladder(k - 1, depth, shard_tiles, integrals, listing, state, fresh)
    b[-1], last[0], state = lax.optimization_barrier((b[-1], last[0], state))
    first, second = {}, {(k, 1, 1, 0): swap(last[0], 1)}
    for tile in (0, part):
        first[k - 1, 1, 1, tile] = swap(b[-1][tile:tile + part], 1)
    last[part], state = lax.optimization_barrier((last[part], state))
    second[k, 1, 1, part] = swap(last[part], 1)
    for tile, piece in last.items():
        first[k, 1, 0, tile] = piece
    for number, fresh in ((k, first), (k + 1, second)):
        state = ladder(number, depth, shard_tiles, integrals, listing, state, fresh)

    residual, _, stats = state
    out = deliver(residual, 0)
    stats = sum([swap(stats, 4 * bits) for bits in range(depth - 1, 0, -1)], stats)
    stats, residual, out = lax.optimization_barrier((stats, residual, out))
    out = deliver(residual, 1, out)
    stats = sum([swap(stats, bits) for bits in (3, 2, 1)], stats)
    irrep_sums, ab_counts = jnp.sum(stats, axis=2)
    entries = ab_counts * ij_counts.astype(jnp.float32) * float(rows * rows)
    return out, jnp.sqrt(irrep_sums / entries + 1e-06)


def solution(mesh):
    in_specs = (
        P(("groups", "vir"), None, None),
        P("groups"),
        P(("groups", "vir"), None, None),
        P(("groups", "vir")),
    )
    out_specs = (P(("groups", "vir"), None, None), P("groups"))
    return jax.shard_map(
        per_device, mesh=mesh, in_specs=in_specs, out_specs=out_specs, check_vma=False
    )
```

```python
import functools

import jax
import jax.numpy as jnp
import numpy as np
from jax import lax
from jax.experimental import pallas as pl
from jax.experimental.pallas import tpu as pltpu
from jax.sharding import PartitionSpec as P

BATCH = 4
UNROLL = 4
MUTE = 1 << 28


def ring_of(depth):
    return [0, *range(1, depth, 2), *range(depth - 2 + depth % 2, 0, -2)]


def ring_place(z, depth):
    return jnp.where(z % 2 == 1, (z + 1) // 2, (depth - z // 2) % depth)


def ring_position(place, depth):
    return jnp.where(place <= depth // 2, jnp.maximum(2 * place - 1, 0), 2 * (depth - place))


def call_of(depth, lag, other_y, other_core):
    if other_y:
        return lag + other_core
    return min(lag, depth - 2) if other_core else max(lag - 1, 0)


def prepare_kernel(
    depth, shard_tiles,
    me_ref, counts_ref, irrep_ref,
    res_ref, gathered_ref, stats_ref, order_ref, offset_ref, stop_ref, end_ref, item_ref,
    next_ref, call_ref,
):
    own_tiles = irrep_ref.shape[0]
    irreps = counts_ref.shape[0]
    calls = end_ref.shape[0]
    most = item_ref.shape[0] // calls
    for s in range(irreps):
        stop_ref[s] = 0

    def count(l, carry):
        s = irrep_ref[l]
        stop_ref[s] = stop_ref[s] + 1
        return carry

    lax.fori_loop(0, own_tiles, count, 0)
    first, offset = jnp.int32(0), jnp.int32(0)
    for s in range(irreps):
        next_ref[s] = first
        first = first + stop_ref[s]
        stop_ref[s] = first
        offset_ref[s] = offset
        offset = offset + counts_ref[s]

    def place(l, carry):
        s = irrep_ref[l]
        slot = next_ref[s]
        next_ref[s] = slot + 1
        order_ref[slot] = l
        return carry

    lax.fori_loop(0, own_tiles, place, 0)

    me = me_ref[0]
    z, y, core = me // 4, me // 2 % 2, me % 2
    for lag in range(depth):
        at = ring_position(lax.rem(ring_place(z, depth) - lag + depth, depth), depth)
        for other_y, other_core in np.ndindex(2, 2):
            shard = (at * 2 + (1 - y if other_y else y)) * 2 + (1 - core if other_core else core)
            call_ref[shard] = call_of(depth, lag, other_y, other_core)

    for call in range(calls):
        end_ref[call] = call * most

    def symmetry(s, first):
        tiles, offset, stop = counts_ref[s], offset_ref[s], stop_ref[s]

        def block(j, carry):
            low = offset + j * BATCH
            high = offset + jnp.minimum(tiles, j * BATCH + BATCH) - 1
            call = jnp.maximum(call_ref[low // shard_tiles], call_ref[high // shard_tiles])
            word = (j * 256 + s) * 256 + first

            def batch(i, n):
                item_ref[n] = word + i * BATCH
                return n + 1

            end_ref[call] = lax.fori_loop(
                0, (stop - first + BATCH - 1) // BATCH, batch, end_ref[call]
            )
            return carry

        lax.fori_loop(0, (tiles + BATCH - 1) // BATCH, block, 0)
        return stop

    lax.fori_loop(0, irreps, symmetry, jnp.int32(0))
    for call in range(calls):
        end = end_ref[call]
        for spare in range(UNROLL - 1):
            item_ref[end + spare] = item_ref[jnp.maximum(end - 1, 0)] | MUTE

    def blank(l, carry):
        res_ref[l] = jnp.zeros(res_ref.shape[1:], res_ref.dtype)
        return carry

    lax.fori_loop(0, own_tiles, blank, 0)
    spare = jnp.zeros((BATCH, *gathered_ref.shape[1:]), gathered_ref.dtype)
    gathered_ref[pl.ds(gathered_ref.shape[0] - BATCH, BATCH)] = spare
    shape = stats_ref.shape[1:]
    at_row = lax.broadcasted_iota(jnp.int32, shape, 0)
    at_lane = lax.broadcasted_iota(jnp.int32, shape, 1)
    sizes = jnp.zeros(shape, jnp.int32)
    first = jnp.int32(0)
    for s in range(irreps):
        sizes = jnp.where((at_row == s) & (at_lane == 0), stop_ref[s] - first, sizes)
        first = stop_ref[s]
    stats_ref[0] = jnp.zeros(shape, jnp.float32)
    stats_ref[1] = sizes.astype(jnp.float32)


def prepare(me, counts, irrep, depth, shard_tiles, rows, width):
    own_tiles = irrep.shape[0]
    irreps = counts.shape[0]
    columns = shard_tiles * depth * rows
    all_tiles = 4 * shard_tiles * depth
    most = (all_tiles // BATCH + irreps) * (own_tiles // BATCH) + UNROLL
    smem = pl.BlockSpec(memory_space=pltpu.SMEM)
    vmem = pl.BlockSpec(memory_space=pltpu.VMEM)
    return pl.pallas_call(
        functools.partial(prepare_kernel, depth, shard_tiles),
        out_shape=(
            jax.ShapeDtypeStruct((own_tiles, rows, columns), jnp.bfloat16),
            jax.ShapeDtypeStruct((all_tiles + BATCH, rows, width), jnp.bfloat16),
            jax.ShapeDtypeStruct((2, irreps, 128), jnp.float32),
            jax.ShapeDtypeStruct((own_tiles,), jnp.int32),
            jax.ShapeDtypeStruct((irreps,), jnp.int32),
            jax.ShapeDtypeStruct((irreps,), jnp.int32),
            jax.ShapeDtypeStruct((depth + 1,), jnp.int32),
            jax.ShapeDtypeStruct(((depth + 1) * most,), jnp.int32),
        ),
        in_specs=[smem] * 3,
        out_specs=(vmem, vmem, vmem, smem, smem, smem, smem, smem),
        scratch_shapes=[
            pltpu.SMEM((irreps,), jnp.int32),
            pltpu.SMEM((4 * depth,), jnp.int32),
        ],
        compiler_params=pltpu.CompilerParams(
            vmem_limit_bytes=2 * all_tiles * rows * width + 2 * own_tiles * rows * columns
            + 4 * 1024 * 1024
        ),
        cost_estimate=pl.CostEstimate(
            flops=0, bytes_accessed=2 * own_tiles * rows * columns, transcendentals=0
        ),
        name="prepare",
    )(me, counts, irrep)


def ladder_kernel(
    call, depth, shard_tiles, layout,
    me_ref, counts_ref, order_ref, offset_ref, stop_ref, end_ref, item_ref,
    stats_in_ref, v_ref, res_in_ref, gathered_in_ref, *refs,
):
    del res_in_ref, gathered_in_ref
    fresh, refs = refs[:len(layout)], refs[len(layout):]
    res_ref, gathered_ref, stats_ref, acc_ref, a_sem = refs
    rows, width = v_ref.shape[1:]
    side = BATCH * rows
    most = item_ref.shape[0] // end_ref.shape[0]

    me = me_ref[0]
    z, y, core = me // 4, me // 2 % 2, me % 2
    arrivals = []
    for source, (lag, other_y, other_core, tile) in zip(fresh, layout):
        at = ring_position(lax.rem(ring_place(z, depth) - lag + depth, depth), depth)
        own_y = (1 - y) if other_y else y
        own_core = (1 - core) if other_core else core
        arrivals.append(pltpu.make_async_copy(
            source,
            gathered_ref.at[pl.ds(
                ((at * 2 + own_y) * 2 + own_core) * shard_tiles + tile, source.shape[0]
            )],
            a_sem.at[len(arrivals)],
        ))
    for arrival in arrivals:
        arrival.start()
    acc_ref[...] = jnp.zeros(acc_ref.shape, acc_ref.dtype)
    for arrival in arrivals:
        arrival.wait()

    col_at = lax.broadcasted_iota(jnp.int32, (1, side), 1)

    def item(n):
        word = item_ref[n]
        slot, group, block = word & 255, (word >> 8) & 255, (word >> 16) & 255
        members = stop_ref[group] - slot
        tiles = [order_ref[slot + jnp.minimum(t, members - 1)] for t in range(BATCH)]
        return group, block, tiles, jnp.where(word >= MUTE, 0, members)

    def multiply(n):
        group, block, tiles, _ = item(n)
        left = jnp.concatenate([v_ref[tile] for tile in tiles])
        right = gathered_ref[pl.ds(offset_ref[group] + block * BATCH, BATCH)].reshape(side, width)
        return lax.dot_general(
            left, right, (((1,), (1,)), ((), ())), preferred_element_type=jnp.float32
        )

    def keep(n, values):
        group, block, tiles, members = item(n)
        limit = (counts_ref[group] - block * BATCH) * rows
        values = jnp.where(col_at < limit, values, 0.0).reshape(BATCH, rows, side)
        columns = pl.ds(pl.multiple_of(block * side, side), side)
        total = jnp.zeros((8, side), jnp.float32)
        for t in range(BATCH):
            res_ref[tiles[t], :, columns] = values[t].astype(jnp.bfloat16)
            squares = jnp.sum((values[t] * values[t]).reshape(rows // 8, 8, side), axis=0)
            total = total + jnp.where(t < members, squares, 0.0)
        acc_ref[group] += total

    def several(u, carry):
        first = call * most + u * UNROLL
        values = multiply(first)
        for n in range(1, UNROLL):
            following = multiply(first + n)
            keep(first + n - 1, values)
            values = following
        keep(first + UNROLL - 1, values)
        return carry

    items = end_ref[call] - call * most
    lax.fori_loop(0, (items + UNROLL - 1) // UNROLL, several, 0)
    sums = jnp.sum(acc_ref[...], axis=1)
    sums = sum(sums[:, k:k + 128] for k in range(0, side, 128))
    stats_ref[0] = stats_in_ref[0] + sums
    stats_ref[1] = stats_in_ref[1]


def ladder(call, depth, shard_tiles, integrals, listing, state, arrived):
    residual, gathered, stats = state
    layout, fresh = tuple(arrived), tuple(arrived.values())
    rows, width = integrals.shape[1:]
    irreps = stats.shape[1]
    smem = pl.BlockSpec(memory_space=pltpu.SMEM)
    vmem = pl.BlockSpec(memory_space=pltpu.VMEM)
    anywhere = pl.BlockSpec(memory_space=pl.ANY)
    tiles = sum(source.shape[0] for source in fresh)
    return pl.pallas_call(
        functools.partial(ladder_kernel, call, depth, shard_tiles, layout),
        out_shape=(
            jax.ShapeDtypeStruct(residual.shape, residual.dtype),
            jax.ShapeDtypeStruct(gathered.shape, gathered.dtype),
            jax.ShapeDtypeStruct(stats.shape, stats.dtype),
        ),
        in_specs=[smem] * 7 + [vmem] * 4 + [anywhere] * len(fresh),
        out_specs=(vmem, vmem, vmem),
        scratch_shapes=[
            pltpu.VMEM((irreps, 8, BATCH * rows), jnp.float32),
            pltpu.SemaphoreType.DMA((len(fresh),)),
        ],
        input_output_aliases={9: 0, 10: 1},
        compiler_params=pltpu.CompilerParams(
            vmem_limit_bytes=2 * (residual.size + integrals.size + gathered.size) + 6 * 1024 * 1024
        ),
        cost_estimate=pl.CostEstimate(
            flops=residual.size * width * tiles // (4 * shard_tiles * depth),
            bytes_accessed=2 * residual.size * tiles // (4 * shard_tiles * depth),
            transcendentals=0,
        ),
        name=f"ladder_{call}",
    )(*listing, stats, integrals, residual, gathered, *fresh)


def deliver_kernel(part, held_ref, *refs):
    out_ref, sem = refs[-2:]
    tiles = held_ref.shape[0] // 2
    copy = pltpu.make_async_copy(
        held_ref.at[pl.ds(part * tiles, tiles)], out_ref.at[pl.ds(part * tiles, tiles)], sem
    )
    copy.start()
    copy.wait()


def deliver(held, part, *out):
    anywhere = pl.BlockSpec(memory_space=pl.ANY)
    return pl.pallas_call(
        functools.partial(deliver_kernel, part),
        out_shape=jax.ShapeDtypeStruct(held.shape, held.dtype),
        in_specs=[pl.BlockSpec(memory_space=pltpu.VMEM)] + [anywhere] * len(out),
        out_specs=anywhere,
        scratch_shapes=[pltpu.SemaphoreType.DMA],
        input_output_aliases={1: 0} if out else {},
        compiler_params=pltpu.CompilerParams(vmem_limit_bytes=2 * held.size + 1024 * 1024),
        name=f"deliver_{part}",
    )(held, *out)


def per_device(amplitudes, ij_counts, integrals, ab_irrep):
    shard_tiles, rows, width = amplitudes.shape
    devices = lax.axis_size("vir")
    depth = devices // 4
    me = lax.axis_index("vir").astype(jnp.int32).reshape(1)
    ring = ring_of(depth)

    def shift_z(x, by):
        pairs = []
        for d in range(devices):
            target = ring[(ring.index(d // 4) + by) % depth]
            pairs.append((d, target * 4 + d % 4))
        return lax.ppermute(x, "vir", pairs)

    def swap(x, bits):
        return lax.ppermute(x, "vir", [(d, d ^ bits) for d in range(devices)])

    residual, gathered, stats, *listing = prepare(
        me, ij_counts, ab_irrep, depth, shard_tiles, rows, width
    )
    listing = (me, ij_counts, *listing)
    state = (residual, gathered, stats)

    a, b, c, d = [amplitudes], [], [], []
    for k in range(depth):
        if 0 < k < depth - 1:
            a[k], state = lax.optimization_barrier((a[k], state))
        if k < depth - 1:
            b.append(swap(a[k], 2))
            a.append(shift_z(a[k], 1))
        else:
            part = shard_tiles // 2
            a[k], c[-1], back, state = lax.optimization_barrier(
                (a[k], c[-1], b[0][part:], state)
            )
            last = {part: shift_z(back, -1), 0: swap(a[k][:part], 2)}
        c.append(swap(a[k], 1))
        if k == 0:
            continue
        fresh = {(k, 0, 0, 0): a[k], (k - 1, 1, 0, 0): b[k - 1], (k - 1, 0, 1, 0): c[k - 1]}
        if k == 1:
            fresh[0, 0, 0, 0] = a[0]
        else:
            fresh[k - 2, 1, 1, 0] = d[k - 2]
        if k < depth - 1:
            d.append(swap(b[k - 1], 1))
        else:
            fresh[k, 0, 1, 0] = c[k]
        state = ladder(k - 1, depth, shard_tiles, integrals, listing, state, fresh)
    b[-1], last[0], state = lax.optimization_barrier((b[-1], last[0], state))
    first, second = {}, {(k, 1, 1, 0): swap(last[0], 1)}
    for tile in (0, part):
        first[k - 1, 1, 1, tile] = swap(b[-1][tile:tile + part], 1)
    last[part], state = lax.optimization_barrier((last[part], state))
    second[k, 1, 1, part] = swap(last[part], 1)
    for tile, piece in last.items():
        first[k, 1, 0, tile] = piece
    for number, fresh in ((k, first), (k + 1, second)):
        state = ladder(number, depth, shard_tiles, integrals, listing, state, fresh)

    residual, _, stats = state
    out = deliver(residual, 0)
    stats = sum([swap(stats, 4 * bits) for bits in range(depth - 1, 0, -1)], stats)
    stats, residual, out = lax.optimization_barrier((stats, residual, out))
    out = deliver(residual, 1, out)
    stats = sum([swap(stats, bits) for bits in (3, 2, 1)], stats)
    irrep_sums, ab_counts = jnp.sum(stats, axis=2)
    entries = ab_counts * ij_counts.astype(jnp.float32) * float(rows * rows)
    return out, jnp.sqrt(irrep_sums / entries + 1e-06)


def solution(mesh):
    in_specs = (
        P(("groups", "vir"), None, None),
        P("groups"),
        P(("groups", "vir"), None, None),
        P(("groups", "vir")),
    )
    out_specs = (P(("groups", "vir"), None, None), P("groups"))
    return jax.shard_map(
        per_device, mesh=mesh, in_specs=in_specs, out_specs=out_specs, check_vma=False
    )
```

```python
import functools

import jax
import jax.numpy as jnp
import numpy as np
from jax import lax
from jax.experimental import pallas as pl
from jax.experimental.pallas import tpu as pltpu
from jax.sharding import PartitionSpec as P

BATCH = 4
UNROLL = 4
MUTE = 1 << 28


def ring_of(depth):
    return [0, *range(1, depth, 2), *range(depth - 2 + depth % 2, 0, -2)]


def ring_place(z, depth):
    return jnp.where(z % 2 == 1, (z + 1) // 2, (depth - z // 2) % depth)


def ring_position(place, depth):
    return jnp.where(place <= depth // 2, jnp.maximum(2 * place - 1, 0), 2 * (depth - place))


def call_of(depth, lag, other_y, other_core):
    if other_y:
        return lag + other_core
    return min(lag, depth - 2) if other_core else max(lag - 1, 0)


def prepare_kernel(
    depth, shard_tiles,
    me_ref, counts_ref, irrep_ref,
    res_ref, gathered_ref, stats_ref, order_ref, offset_ref, stop_ref, end_ref, item_ref,
    next_ref, call_ref,
):
    own_tiles = irrep_ref.shape[0]
    irreps = counts_ref.shape[0]
    calls = end_ref.shape[0]
    most = item_ref.shape[0] // calls
    for s in range(irreps):
        stop_ref[s] = 0

    def count(l, carry):
        s = irrep_ref[l]
        stop_ref[s] = stop_ref[s] + 1
        return carry

    lax.fori_loop(0, own_tiles, count, 0)
    first, offset = jnp.int32(0), jnp.int32(0)
    for s in range(irreps):
        next_ref[s] = first
        first = first + stop_ref[s]
        stop_ref[s] = first
        offset_ref[s] = offset
        offset = offset + counts_ref[s]

    def place(l, carry):
        s = irrep_ref[l]
        slot = next_ref[s]
        next_ref[s] = slot + 1
        order_ref[slot] = l
        return carry

    lax.fori_loop(0, own_tiles, place, 0)

    me = me_ref[0]
    z, y, core = me // 4, me // 2 % 2, me % 2
    for lag in range(depth):
        at = ring_position(lax.rem(ring_place(z, depth) - lag + depth, depth), depth)
        for other_y, other_core in np.ndindex(2, 2):
            shard = (at * 2 + (1 - y if other_y else y)) * 2 + (1 - core if other_core else core)
            call_ref[shard] = call_of(depth, lag, other_y, other_core)

    for call in range(calls):
        end_ref[call] = call * most

    def symmetry(s, first):
        tiles, offset, stop = counts_ref[s], offset_ref[s], stop_ref[s]

        def block(j, carry):
            low = offset + j * BATCH
            high = offset + jnp.minimum(tiles, j * BATCH + BATCH) - 1
            call = jnp.maximum(call_ref[low // shard_tiles], call_ref[high // shard_tiles])
            word = (j * 256 + s) * 256 + first

            def batch(i, n):
                item_ref[n] = word + i * BATCH
                return n + 1

            end_ref[call] = lax.fori_loop(
                0, (stop - first + BATCH - 1) // BATCH, batch, end_ref[call]
            )
            return carry

        lax.fori_loop(0, (tiles + BATCH - 1) // BATCH, block, 0)
        return stop

    lax.fori_loop(0, irreps, symmetry, jnp.int32(0))
    for call in range(calls):
        end = end_ref[call]
        for spare in range(UNROLL - 1):
            item_ref[end + spare] = item_ref[jnp.maximum(end - 1, 0)] | MUTE

    def blank(l, carry):
        res_ref[l] = jnp.zeros(res_ref.shape[1:], res_ref.dtype)
        return carry

    lax.fori_loop(0, own_tiles, blank, 0)
    spare = jnp.zeros((BATCH, *gathered_ref.shape[1:]), gathered_ref.dtype)
    gathered_ref[pl.ds(gathered_ref.shape[0] - BATCH, BATCH)] = spare
    shape = stats_ref.shape[1:]
    at_row = lax.broadcasted_iota(jnp.int32, shape, 0)
    at_lane = lax.broadcasted_iota(jnp.int32, shape, 1)
    sizes = jnp.zeros(shape, jnp.int32)
    first = jnp.int32(0)
    for s in range(irreps):
        sizes = jnp.where((at_row == s) & (at_lane == 0), stop_ref[s] - first, sizes)
        first = stop_ref[s]
    stats_ref[0] = jnp.zeros(shape, jnp.float32)
    stats_ref[1] = sizes.astype(jnp.float32)


def prepare(me, counts, irrep, depth, shard_tiles, rows, width):
    own_tiles = irrep.shape[0]
    irreps = counts.shape[0]
    columns = shard_tiles * depth * rows
    all_tiles = 4 * shard_tiles * depth
    most = (all_tiles // BATCH + irreps) * (own_tiles // BATCH) + UNROLL
    smem = pl.BlockSpec(memory_space=pltpu.SMEM)
    vmem = pl.BlockSpec(memory_space=pltpu.VMEM)
    return pl.pallas_call(
        functools.partial(prepare_kernel, depth, shard_tiles),
        out_shape=(
            jax.ShapeDtypeStruct((own_tiles, rows, columns), jnp.bfloat16),
            jax.ShapeDtypeStruct((all_tiles + BATCH, rows, width), jnp.bfloat16),
            jax.ShapeDtypeStruct((2, irreps, 128), jnp.float32),
            jax.ShapeDtypeStruct((own_tiles,), jnp.int32),
            jax.ShapeDtypeStruct((irreps,), jnp.int32),
            jax.ShapeDtypeStruct((irreps,), jnp.int32),
            jax.ShapeDtypeStruct((depth + 1,), jnp.int32),
            jax.ShapeDtypeStruct(((depth + 1) * most,), jnp.int32),
        ),
        in_specs=[smem] * 3,
        out_specs=(vmem, vmem, vmem, smem, smem, smem, smem, smem),
        scratch_shapes=[
            pltpu.SMEM((irreps,), jnp.int32),
            pltpu.SMEM((4 * depth,), jnp.int32),
        ],
        compiler_params=pltpu.CompilerParams(
            vmem_limit_bytes=2 * all_tiles * rows * width + 2 * own_tiles * rows * columns
            + 4 * 1024 * 1024
        ),
        cost_estimate=pl.CostEstimate(
            flops=0, bytes_accessed=2 * own_tiles * rows * columns, transcendentals=0
        ),
        name="prepare",
    )(me, counts, irrep)


def ladder_kernel(
    call, depth, shard_tiles, layout,
    me_ref, counts_ref, order_ref, offset_ref, stop_ref, end_ref, item_ref,
    stats_in_ref, v_ref, res_in_ref, gathered_in_ref, *refs,
):
    del res_in_ref, gathered_in_ref
    fresh, refs = refs[:len(layout)], refs[len(layout):]
    res_ref, gathered_ref, stats_ref, acc_ref, a_sem = refs
    rows, width = v_ref.shape[1:]
    side = BATCH * rows
    most = item_ref.shape[0] // end_ref.shape[0]

    me = me_ref[0]
    z, y, core = me // 4, me // 2 % 2, me % 2
    arrivals = []
    for source, (lag, other_y, other_core, tile) in zip(fresh, layout):
        at = ring_position(lax.rem(ring_place(z, depth) - lag + depth, depth), depth)
        own_y = (1 - y) if other_y else y
        own_core = (1 - core) if other_core else core
        arrivals.append(pltpu.make_async_copy(
            source,
            gathered_ref.at[pl.ds(
                ((at * 2 + own_y) * 2 + own_core) * shard_tiles + tile, source.shape[0]
            )],
            a_sem.at[len(arrivals)],
        ))
    for arrival in arrivals:
        arrival.start()
    acc_ref[...] = jnp.zeros(acc_ref.shape, acc_ref.dtype)
    for arrival in arrivals:
        arrival.wait()

    col_at = lax.broadcasted_iota(jnp.int32, (1, side), 1)

    def item(n):
        word = item_ref[n]
        slot, group, block = word & 255, (word >> 8) & 255, (word >> 16) & 255
        members = stop_ref[group] - slot
        tiles = [order_ref[slot + jnp.minimum(t, members - 1)] for t in range(BATCH)]
        return group, block, tiles, jnp.where(word >= MUTE, 0, members)

    def multiply(n):
        group, block, tiles, _ = item(n)
        left = jnp.concatenate([v_ref[tile] for tile in tiles])
        right = gathered_ref[pl.ds(offset_ref[group] + block * BATCH, BATCH)].reshape(side, width)
        return lax.dot_general(
            left, right, (((1,), (1,)), ((), ())), preferred_element_type=jnp.float32
        )

    def keep(n, values):
        group, block, tiles, members = item(n)
        limit = (counts_ref[group] - block * BATCH) * rows
        values = jnp.where(col_at < limit, values, 0.0).reshape(BATCH, rows, side)
        columns = pl.ds(pl.multiple_of(block * side, side), side)
        total = jnp.zeros((8, side), jnp.float32)
        for t in range(BATCH):
            res_ref[tiles[t], :, columns] = values[t].astype(jnp.bfloat16)
            squares = jnp.sum((values[t] * values[t]).reshape(rows // 8, 8, side), axis=0)
            total = total + jnp.where(t < members, squares, 0.0)
        acc_ref[group] += total

    def several(u, carry):
        first = call * most + u * UNROLL
        values = multiply(first)
        for n in range(1, UNROLL):
            following = multiply(first + n)
            keep(first + n - 1, values)
            values = following
        keep(first + UNROLL - 1, values)
        return carry

    items = end_ref[call] - call * most
    lax.fori_loop(0, (items + UNROLL - 1) // UNROLL, several, 0)
    sums = jnp.sum(acc_ref[...], axis=1)
    sums = sum(sums[:, k:k + 128] for k in range(0, side, 128))
    stats_ref[0] = stats_in_ref[0] + sums
    stats_ref[1] = stats_in_ref[1]


def ladder(call, depth, shard_tiles, integrals, listing, state, arrived):
    residual, gathered, stats = state
    layout, fresh = tuple(arrived), tuple(arrived.values())
    rows, width = integrals.shape[1:]
    irreps = stats.shape[1]
    smem = pl.BlockSpec(memory_space=pltpu.SMEM)
    vmem = pl.BlockSpec(memory_space=pltpu.VMEM)
    anywhere = pl.BlockSpec(memory_space=pl.ANY)
    tiles = sum(source.shape[0] for source in fresh)
    return pl.pallas_call(
        functools.partial(ladder_kernel, call, depth, shard_tiles, layout),
        out_shape=(
            jax.ShapeDtypeStruct(residual.shape, residual.dtype),
            jax.ShapeDtypeStruct(gathered.shape, gathered.dtype),
            jax.ShapeDtypeStruct(stats.shape, stats.dtype),
        ),
        in_specs=[smem] * 7 + [vmem] * 4 + [anywhere] * len(fresh),
        out_specs=(vmem, vmem, vmem),
        scratch_shapes=[
            pltpu.VMEM((irreps, 8, BATCH * rows), jnp.float32),
            pltpu.SemaphoreType.DMA((len(fresh),)),
        ],
        input_output_aliases={9: 0, 10: 1},
        compiler_params=pltpu.CompilerParams(
            vmem_limit_bytes=2 * (residual.size + integrals.size + gathered.size) + 6 * 1024 * 1024
        ),
        cost_estimate=pl.CostEstimate(
            flops=residual.size * width * tiles // (4 * shard_tiles * depth),
            bytes_accessed=2 * residual.size * tiles // (4 * shard_tiles * depth),
            transcendentals=0,
        ),
        name=f"ladder_{call}",
    )(*listing, stats, integrals, residual, gathered, *fresh)


def deliver_kernel(part, held_ref, *refs):
    out_ref, sem = refs[-2:]
    tiles = held_ref.shape[0] // 2
    copy = pltpu.make_async_copy(
        held_ref.at[pl.ds(part * tiles, tiles)], out_ref.at[pl.ds(part * tiles, tiles)], sem
    )
    copy.start()
    copy.wait()


def deliver(held, part, *out):
    anywhere = pl.BlockSpec(memory_space=pl.ANY)
    return pl.pallas_call(
        functools.partial(deliver_kernel, part),
        out_shape=jax.ShapeDtypeStruct(held.shape, held.dtype),
        in_specs=[pl.BlockSpec(memory_space=pltpu.VMEM)] + [anywhere] * len(out),
        out_specs=anywhere,
        scratch_shapes=[pltpu.SemaphoreType.DMA],
        input_output_aliases={1: 0} if out else {},
        compiler_params=pltpu.CompilerParams(vmem_limit_bytes=2 * held.size + 1024 * 1024),
        name=f"deliver_{part}",
    )(held, *out)


def per_device(amplitudes, ij_counts, integrals, ab_irrep):
    shard_tiles, rows, width = amplitudes.shape
    devices = lax.axis_size("vir")
    depth = devices // 4
    me = lax.axis_index("vir").astype(jnp.int32).reshape(1)
    ring = ring_of(depth)

    def shift_z(x, by):
        pairs = []
        for d in range(devices):
            target = ring[(ring.index(d // 4) + by) % depth]
            pairs.append((d, target * 4 + d % 4))
        return lax.ppermute(x, "vir", pairs)

    def swap(x, bits):
        return lax.ppermute(x, "vir", [(d, d ^ bits) for d in range(devices)])

    residual, gathered, stats, *listing = prepare(
        me, ij_counts, ab_irrep, depth, shard_tiles, rows, width
    )
    listing = (me, ij_counts, *listing)
    state = (residual, gathered, stats)

    a, b, c, d = [amplitudes], [], [], []
    for k in range(depth):
        if 0 < k < depth - 1:
            if k == 1:
                a[k], state = lax.optimization_barrier((a[k], state))
            else:
                a[k], c[-1], state = lax.optimization_barrier((a[k], c[-1], state))
        if k < depth - 1:
            b.append(swap(a[k], 2))
            a.append(shift_z(a[k], 1))
        else:
            part = shard_tiles // 2
            a[k], c[-1], back, state = lax.optimization_barrier(
                (a[k], c[-1], b[0][part:], state)
            )
            last = {part: shift_z(back, -1), 0: swap(a[k][:part], 2)}
        c.append(swap(a[k], 1))
        if k == 0:
            continue
        fresh = {(k, 0, 0, 0): a[k], (k - 1, 1, 0, 0): b[k - 1], (k - 1, 0, 1, 0): c[k - 1]}
        if k == 1:
            fresh[0, 0, 0, 0] = a[0]
        else:
            fresh[k - 2, 1, 1, 0] = d[k - 2]
        if k < depth - 1:
            d.append(swap(b[k - 1], 1))
        else:
            fresh[k, 0, 1, 0] = c[k]
        state = ladder(k - 1, depth, shard_tiles, integrals, listing, state, fresh)
    b[-1], last[0], state = lax.optimization_barrier((b[-1], last[0], state))
    first, second = {}, {(k, 1, 1, 0): swap(last[0], 1)}
    for tile in (0, part):
        first[k - 1, 1, 1, tile] = swap(b[-1][tile:tile + part], 1)
    last[part], state = lax.optimization_barrier((last[part], state))
    second[k, 1, 1, part] = swap(last[part], 1)
    for tile, piece in last.items():
        first[k, 1, 0, tile] = piece
    for number, fresh in ((k, first), (k + 1, second)):
        state = ladder(number, depth, shard_tiles, integrals, listing, state, fresh)

    residual, _, stats = state
    out = deliver(residual, 0)
    stats = sum([swap(stats, 4 * bits) for bits in range(depth - 1, 0, -1)], stats)
    stats, residual, out = lax.optimization_barrier((stats, residual, out))
    out = deliver(residual, 1, out)
    stats = sum([swap(stats, bits) for bits in (3, 2, 1)], stats)
    irrep_sums, ab_counts = jnp.sum(stats, axis=2)
    entries = ab_counts * ij_counts.astype(jnp.float32) * float(rows * rows)
    return out, jnp.sqrt(irrep_sums / entries + 1e-06)


def solution(mesh):
    in_specs = (
        P(("groups", "vir"), None, None),
        P("groups"),
        P(("groups", "vir"), None, None),
        P(("groups", "vir")),
    )
    out_specs = (P(("groups", "vir"), None, None), P("groups"))
    return jax.shard_map(
        per_device, mesh=mesh, in_specs=in_specs, out_specs=out_specs, check_vma=False
    )
```
